32 devices in a mesh: dev: 8 (over z, x), ta: 4 (over y, core).
Axes of the slice: x: 2, y: 2, z: 4, core: 2. Of those that a mesh axis runs over, the one named last changes fastest.
Arguments:
- tokens: bfloat16 [4096, 2048], P(('dev', 'ta')), may hold values from -6 to 6
- cotangent: bfloat16 [4096, 2048], P(('dev', 'ta')), may hold values from -6 to 6
- lengths: int32 [6], replicated, may hold values from 1 to 3970, 4096 in all
- pad_mask: int32 [4096], P(('dev', 'ta')), may hold values 0 or 1
- attn_gain: float32 [2048], replicated, may hold values from 0.5 to 1.5
- projection_weight: bfloat16 [2048, 4, 2048], P(('dev', 'ta')), may hold values from -0.125 to 0.125
- w_beta: bfloat16 [2048, 16], P(('dev', 'ta')), may hold values from -0.125 to 0.125
- beta_bias: float32 [16], replicated, may hold values from -5 to 0
- conv_weight: float32 [3, 4, 2048], replicated, may hold values from -3 to 3
- head_gain: float32 [128], replicated, may hold values from 0.5 to 1.5
- mlp_gain: float32 [2048], replicated, may hold values from 0.5 to 1.5
- w_gate: bfloat16 [2048, 5632], P(None, 'ta'), may hold values from -0.125 to 0.125
- w_up: bfloat16 [2048, 5632], P(None, 'ta'), may hold values from -0.125 to 0.125
- w_down: bfloat16 [5632, 2048], P('ta'), may hold values from -0.078125 to 0.078125
Outputs:
- block_out: bfloat16 [4096, 2048], P(('dev', 'ta'))
- grad_tokens: float32 [4096, 2048], P(('dev', 'ta'))
- grad_attn_gain: float32 [2048], replicated
- gradient_projection_weight: float32 [2048, 4, 2048], P(('dev', 'ta'))
- grad_w_beta: float32 [2048, 16], P(('dev', 'ta'))
- grad_beta_bias: float32 [16], replicated
- grad_conv: float32 [3, 4, 2048], replicated
- grad_head_gain: float32 [128], replicated
- grad_mlp_gain: float32 [2048], replicated
- grad_w_gate: float32 [2048, 5632], P(None, 'ta')
- grad_w_up: float32 [2048, 5632], P(None, 'ta')
- grad_w_down: float32 [5632, 2048], P('ta')
The draws below stay inside these ranges and needn't reach their ends.
Inputs may be any that keep to these rules, and one draw needn't show every extreme that they name: 6 documents lie end to end in this order from position 0; their lengths sum to 4096.
All inputs are finite; a program needn't handle non-finite values. No bound on the sum of `pad_mask` on one device may be relied on, other than what follows from the above.
Results may differ from the reference program's by a relative error of at most 0.024.
Values may be sent and summed in bfloat16 or wider, within the bound.
No kernel may reach another device: no remote copies, remote signals or barrier semaphores. Data moves between devices by JAX's collectives and lax.ppermute only.
A program may use at most 640 MiB of HBM per device.

```python
import math
import jax
import jax.numpy as jnp
import numpy as np
from jax import lax

D = 2048
HEADS = 16
HEAD_DIM = 128
FF = 5632
KSIZE = 4
SPAN = 64
TOK_DEV = 128
DOCS = 6
TOKENS = 4096


def with_ends(drawn, stream_key, smallest, high):
    shape = drawn.shape
    place = [jax.random.randint(jax.random.fold_in(stream_key, axis), (), 0, shape[axis]) for axis in range(len(shape))]
    drawn = drawn.at[tuple(place)].set(smallest)
    longest = shape.index(max(shape))
    place[longest] = (place[longest] + 1) % shape[longest]
    return drawn.at[tuple(place)].set(high)


def levels(own_key, shape, pieces, least, top_value):
    def one(axis_at, blocks):
        heights = jax.random.uniform(jax.random.fold_in(jax.random.fold_in(own_key, 6), axis_at), (blocks,), jnp.float32, least / len(pieces), top_value / len(pieces))
        return jnp.repeat(jnp.exp(heights), shape[axis_at] // blocks).reshape((-1,) + (1,) * (len(shape) - axis_at - 1))

    factor_of = one(*pieces[0])
    for cut in pieces[1:]:
        factor_of = factor_of * one(*cut)
    return factor_of


def length_profile(amount, total, reach, skew):
    loads = [(1 << 20) // math.isqrt(grade ** skew) + 1 for grade in range(2, amount + 1)]
    spare, given = total - reach - (amount - 1), [1] * (amount - 1)
    while spare > 0:
        free = [i for i in range(amount - 1) if given[i] < reach]
        mass, left = sum([loads[i] for i in free]), spare
        for i in free:
            extra = min(reach - given[i], max(1, left * loads[i] // mass), spare)
            given[i] = given[i] + extra
            spare = spare - extra
    return np.array([reach] + given)


def uneven_parts(rng, count, total, most, skew):
    if count == 2:
        one = jax.random.randint(rng, (), max(1, total - most), min(most, total - 1) + 1)
        return jnp.stack([one, total - one])
    sizes = jnp.asarray(length_profile(count, total, most, skew), jnp.int32)
    couples = (count - 1) // 2
    donor, receiver = sizes[1:1 + 2 * couples:2], sizes[2:2 + 2 * couples:2]
    margin = jnp.minimum(donor - 1, most - receiver)
    passed = jax.random.randint(jax.random.fold_in(rng, 1), (couples,), 0, 1 << 20) % (margin + 1)
    sizes = sizes.at[1:1 + 2 * couples:2].set(donor - passed).at[2:2 + 2 * couples:2].set(receiver + passed)
    return sizes[jax.random.permutation(jax.random.fold_in(rng, 2), count)]


def bell_draw(rng, shape, spread, reach, shards=(), kind=jnp.bfloat16):
    drawn = spread * jax.random.normal(rng, shape, jnp.float32)
    if shards:
        drawn = drawn * levels(rng, shape, shards, -0.22, 0.18)
    return jnp.clip(drawn, -reach, reach).astype(kind)


def setup_inputs(seed: int = 0) -> dict:
    streams_of = jax.random.split(jax.random.key(seed), 15)
    tokens = bell_draw(streams_of[0], (TOKENS, D), 1.0, 6.0, ((0, 32),))
    cotangent = bell_draw(streams_of[1], (TOKENS, D), 1.0, 6.0, ((0, 32),))
    lengths = uneven_parts(streams_of[2], DOCS, TOKENS, TOKENS - TOK_DEV + 2, 2).astype(jnp.int32)
    pad_mask = with_ends((jax.random.randint(streams_of[3], (TOKENS,), 0, 8) < 7).astype(jnp.int32), jax.random.fold_in(streams_of[3], 1), 0, 1)
    attn_gain = jnp.clip(1.0 + 0.1 * jax.random.normal(streams_of[4], (D,), jnp.float32), 0.5, 1.5)
    projection_weight = bell_draw(streams_of[5], (D, 4, D), D ** -0.5, 0.125, ((0, 32),))
    w_beta = bell_draw(streams_of[6], (D, HEADS), D ** -0.5, 0.125, ((0, 32),))
    beta_bias = jnp.clip(jax.random.uniform(streams_of[7], (HEADS,), jnp.float32, -5.0, 0.0), -5.0, 0.0)
    conv_weight = bell_draw(streams_of[8], (3, KSIZE, D), KSIZE ** -0.5, 3.0, (), jnp.float32)
    head_gain = jnp.clip(1.0 + 0.1 * jax.random.normal(streams_of[9], (HEAD_DIM,), jnp.float32), 0.5, 1.5)
    mlp_gain = jnp.clip(1.0 + 0.1 * jax.random.normal(streams_of[10], (D,), jnp.float32), 0.5, 1.5)
    w_gate = bell_draw(streams_of[11], (D, FF), D ** -0.5, 0.125, ((1, 4),))
    w_up = bell_draw(streams_of[12], (D, FF), D ** -0.5, 0.125, ((1, 4),))
    w_down = bell_draw(streams_of[13], (FF, D), FF ** -0.5, 0.078125, ((0, 4),))
    return {"tokens": tokens, "cotangent": cotangent, "lengths": lengths, "pad_mask": pad_mask, "attn_gain": attn_gain, "projection_weight": projection_weight, "w_beta": w_beta, "beta_bias": beta_bias, "conv_weight": conv_weight, "head_gain": head_gain, "mlp_gain": mlp_gain, "w_gate": w_gate, "w_up": w_up, "w_down": w_down}


HIGHEST_ACCURACY = lax.Precision.HIGHEST
NORM_EPS = 1e-06
HEAD_EPS = 1e-05
UNIT_EPS = 1e-06

@jax.custom_vjp
def low(v):
    return lax.optimization_barrier(v.astype(jnp.bfloat16)).astype(jnp.float32)

@jax.custom_vjp
def low_back(v):
    return v

def low_keep(v):
    return (low(v), None)

def low_pass(kept, grad):
    return (grad,)

def back_keep(v):
    return (v, None)

def back_low(kept, grad):
    return (low(grad),)
low.defvjp(low_keep, low_pass)
low_back.defvjp(back_keep, back_low)

def rms_scale(values, gain):
    return values * lax.rsqrt(lax.optimization_barrier(jnp.mean(values * values, axis=-1, keepdims=True)) + NORM_EPS) * gain

def unit_rows(values):
    return values * lax.rsqrt(lax.optimization_barrier(jnp.sum(values * values, axis=-1, keepdims=True)) + UNIT_EPS)

def document_of(lengths, positions):
    starts = (jnp.cumsum(lengths) - lengths).astype(jnp.int32)
    above = (starts[None, :] <= positions[:, None]).astype(jnp.int32)
    return (lax.optimization_barrier(jnp.sum(above, axis=1)) - 1).astype(jnp.int32)

def short_conv(masked, conv_weight, documents):
    summed = masked * conv_weight[:, KSIZE - 1, :][None]
    for delay in range(1, KSIZE):
        moved = jnp.concatenate([jnp.zeros((delay,) + masked.shape[1:], masked.dtype), masked[:-delay]], axis=0)
        earlier = jnp.concatenate([jnp.full((delay,), -1, jnp.int32), documents[:-delay]])
        inside = (earlier == documents).astype(masked.dtype)
        summed = summed + moved * conv_weight[:, KSIZE - 1 - delay, :][None] * inside[:, None, None]
    return summed

def span_step(state, block):
    queries, keys, values, beta, documents, previous = block
    same = documents[:, None] == documents[None, :]
    order = jnp.arange(SPAN, dtype=jnp.int32)
    strict = (same & (order[:, None] > order[None, :])).astype(jnp.float32)
    weak = (same & (order[:, None] >= order[None, :])).astype(jnp.float32)
    continuing = (documents == previous).astype(jnp.float32)
    closing = (documents == documents[SPAN - 1]).astype(jnp.float32)
    rates = beta.T
    key_key = jnp.einsum('thd,shd->hts', keys, keys, precision=HIGHEST_ACCURACY)
    query_key = jnp.einsum('thd,shd->hts', queries, keys, precision=HIGHEST_ACCURACY)
    system = jnp.eye(SPAN, dtype=jnp.float32)[None] + key_key * rates[:, None, :] * strict[None]
    recalled = jnp.einsum('thd,hde->hte', keys, state, precision=HIGHEST_ACCURACY)
    target = jnp.transpose(values, (1, 0, 2)) - continuing[None, :, None] * recalled
    renewed = jax.scipy.linalg.solve_triangular(system, target, lower=True)
    mixing = query_key * rates[:, None, :] * weak[None]
    outputs = continuing[None, :, None] * jnp.einsum('thd,hde->hte', queries, state, precision=HIGHEST_ACCURACY)
    outputs = outputs + jnp.einsum('hts,hse->hte', mixing, renewed, precision=HIGHEST_ACCURACY)
    written = rates * closing[None, :]
    state_next = continuing[SPAN - 1] * state + jnp.einsum('thd,ht,hte->hde', keys, written, renewed, precision=HIGHEST_ACCURACY)
    return (state_next, jnp.transpose(outputs, (1, 0, 2)))

def block_forward(tokens_f, attn_gain, projection_weight, w_beta, beta_bias, conv_weight, head_gain, mlp_gain, w_gate, w_up, w_down, live, documents, previous):
    normalized_rows = low(rms_scale(tokens_f, attn_gain))
    projected_rows = low_back(jnp.einsum('sq,qbw->sbw', normalized_rows, projection_weight[:, 0:3], precision=HIGHEST_ACCURACY))
    beta_logit = low_back(jnp.dot(normalized_rows, w_beta, precision=HIGHEST_ACCURACY))
    masked = projected_rows * live[:, None, None]
    active = jax.nn.silu(short_conv(masked, conv_weight, documents)).reshape(TOKENS, 3, HEADS, HEAD_DIM)
    queries = unit_rows(active[:, 0]) * HEAD_DIM ** (-0.5)
    keys = unit_rows(active[:, 1])
    values = active[:, 2]
    beta = jax.nn.sigmoid(beta_logit + beta_bias) * live[:, None]
    count = TOKENS // SPAN
    blocks = (queries.reshape(count, SPAN, HEADS, HEAD_DIM), keys.reshape(count, SPAN, HEADS, HEAD_DIM), values.reshape(count, SPAN, HEADS, HEAD_DIM), beta.reshape(count, SPAN, HEADS), documents.reshape(count, SPAN), previous)
    start = jnp.zeros((HEADS, HEAD_DIM, HEAD_DIM), jnp.float32)
    _, outputs = lax.scan(jax.checkpoint(span_step), start, blocks)
    heads_out = outputs.reshape(TOKENS, HEADS, HEAD_DIM)
    scaled = heads_out * lax.rsqrt(lax.optimization_barrier(jnp.mean(heads_out * heads_out, axis=-1, keepdims=True)) + HEAD_EPS) * head_gain
    head_normed = low(scaled.reshape(TOKENS, D))
    residual = tokens_f + low_back(jnp.dot(head_normed, projection_weight[:, 3], precision=HIGHEST_ACCURACY))
    feed = low(rms_scale(residual, mlp_gain))
    gate = low_back(jnp.dot(feed, w_gate, precision=HIGHEST_ACCURACY))
    lifted = low_back(jnp.dot(feed, w_up, precision=HIGHEST_ACCURACY))
    hidden = low(jax.nn.silu(gate) * lifted)
    return residual + low_back(jnp.dot(hidden, w_down, precision=HIGHEST_ACCURACY))

def reference(tokens, cotangent, lengths, pad_mask, attn_gain, projection_weight, w_beta, beta_bias, conv_weight, head_gain, mlp_gain, w_gate, w_up, w_down):
    positions = jnp.arange(TOKENS, dtype=jnp.int32)
    documents = document_of(lengths, positions)
    previous = document_of(lengths, (positions[::SPAN] - 1).astype(jnp.int32))
    live = pad_mask.astype(jnp.float32)

    def forward(tokens_f, attn_gain, projection_weight, w_beta, beta_bias, conv_weight, head_gain, mlp_gain, w_gate, w_up, w_down):
        return block_forward(tokens_f, attn_gain, projection_weight, w_beta, beta_bias, conv_weight, head_gain, mlp_gain, w_gate, w_up, w_down, live, documents, previous)
    result, backward = jax.vjp(forward, tokens.astype(jnp.float32), attn_gain, projection_weight.astype(jnp.float32), w_beta.astype(jnp.float32), beta_bias, conv_weight, head_gain, mlp_gain, w_gate.astype(jnp.float32), w_up.astype(jnp.float32), w_down.astype(jnp.float32))
    grads = backward(cotangent.astype(jnp.float32))
    return (result.astype(jnp.bfloat16), grads[0], grads[1], grads[2], grads[3], grads[4], grads[5], grads[6], grads[7], grads[8], grads[9], grads[10])
```

```python
import jax
import jax.numpy as jnp
from jax import lax
from jax.sharding import PartitionSpec as P

HIGHEST = lax.Precision.HIGHEST
NORM_EPS = 1e-06
HEAD_EPS = 1e-05
UNIT_EPS = 1e-06
BOTH = ("dev", "ta")
BF = jnp.bfloat16
F32 = jnp.float32


def swap(x, axis, bit):
    return lax.ppermute(x, axis, [(i, i ^ bit) for i in range(lax.axis_size(axis))])


def gather_parts(x):
    parts = [x]
    for j in range(1, lax.axis_size("ta")):
        bit = j & -j
        parts.append(swap(parts[j ^ bit], "ta", bit))
    return parts


def in_order(parts, rank, axis):
    size = parts[0].shape[axis]
    shape = list(parts[0].shape)
    shape[axis] = size * len(parts)
    joined = jnp.zeros(shape, parts[0].dtype)
    for j, part in enumerate(parts):
        joined = lax.dynamic_update_slice_in_dim(joined, part, (rank ^ j) * size, axis)
    return joined


def exchange(blocks, rank):
    lanes = lax.axis_size("ta")
    parts = []
    for j in range(lanes):
        block = lax.dynamic_index_in_dim(blocks, rank ^ j, 0, False)
        parts.append(swap(block, "ta", j) if j else block)
    return parts


def scatter_sum(blocks, rank):
    lanes = lax.axis_size("ta")
    bit = 1
    while bit < lanes:
        pairs = blocks.reshape((blocks.shape[0] // 2, 2) + blocks.shape[1:])
        mine = (rank // bit) % 2
        kept = lax.dynamic_index_in_dim(pairs, mine, 1, False)
        sent = lax.dynamic_index_in_dim(pairs, 1 - mine, 1, False)
        arrived = swap(sent.astype(BF), "ta", bit)
        blocks = kept.astype(F32) + arrived.astype(F32)
        bit *= 2
    return blocks[0]


def ring_order(size):
    if size % 2:
        return list(range(size))
    return list(range(0, size, 2)) + list(range(size - 1, 0, -2))


class Ring:
    def __init__(self):
        self.size = lax.axis_size("dev")
        self.order = ring_order(self.size)
        self.spot = [self.order.index(i) for i in range(self.size)]
        self.place = lax.axis_index("dev")

    def move(self, x, step):
        n = self.size
        return lax.ppermute(x, "dev", [(self.order[p], self.order[(p + step) % n]) for p in range(n)])

    def at(self, distance):
        n = self.size
        table = jnp.array([self.order[(self.spot[i] + distance) % n] for i in range(n)], jnp.int32)
        return table[self.place]

    def gather(self, x):
        n = self.size
        half = x.shape[0] // 2
        joined = jnp.zeros((n,) + x.shape, x.dtype)
        joined = lax.dynamic_update_index_in_dim(joined, x, self.place, 0)
        onward, back = x, x
        for s in range(1, n // 2):
            onward, back = self.move(onward, 1), self.move(back, -1)
            joined = lax.dynamic_update_index_in_dim(joined, onward, self.at(-s), 0)
            joined = lax.dynamic_update_index_in_dim(joined, back, self.at(s), 0)
        far = jnp.concatenate([self.move(onward[:half], 1), self.move(back[half:], -1)], axis=0)
        return lax.dynamic_update_index_in_dim(joined, far, self.at(n // 2), 0)

    def scatter(self, blocks):
        n = self.size
        half = blocks.shape[1] // 2

        def block(distance):
            return lax.dynamic_index_in_dim(blocks, self.at(distance), 0, False)

        far = block(n // 2)
        ahead = self.move(far[:half], 1)
        behind = self.move(far[half:], -1)
        for s in range(n // 2 - 1, 0, -1):
            right, left = block(s).astype(F32), block(-s).astype(F32)
            if s == n // 2 - 1:
                right = jnp.concatenate([right[:half] + ahead.astype(F32), right[half:]], axis=0)
                left = jnp.concatenate([left[:half], left[half:] + behind.astype(F32)], axis=0)
            else:
                right, left = right + ahead.astype(F32), left + behind.astype(F32)
            ahead, behind = self.move(right.astype(BF), 1), self.move(left.astype(BF), -1)
        return block(0).astype(F32) + ahead.astype(F32) + behind.astype(F32)


def sum_over(x, axis):
    size = lax.axis_size(axis)
    bit = 1
    while bit < size:
        x = x + swap(x, axis, bit)
        bit *= 2
    return x


def shifted(x, distance):
    devices = range(lax.axis_size("dev"))
    return lax.ppermute(x, "dev", [(i - distance, i) for i in devices if i - distance in devices])


def rms_scale(values, gain):
    return values * lax.rsqrt(jnp.mean(values * values, axis=-1, keepdims=True) + NORM_EPS) * gain


def head_norm(heads_out, head_gain):
    scaled = (
        heads_out
        * lax.rsqrt(jnp.mean(heads_out * heads_out, axis=-1, keepdims=True) + HEAD_EPS)
        * head_gain
    )
    return scaled.reshape(heads_out.shape[0], -1)


def unit_rows(values):
    return values * lax.rsqrt(jnp.sum(values * values, axis=-1, keepdims=True) + UNIT_EPS)


def document_of(lengths, positions):
    starts = jnp.cumsum(lengths) - lengths
    above = (starts[None, :] <= positions[:, None]).astype(jnp.int32)
    return jnp.sum(above, axis=1) - 1


def contract_rows(left, right):
    return lax.dot_general(left, right, (((0,), (0,)), ((), ())), preferred_element_type=F32)


def contract_cols(left, right):
    return lax.dot_general(left, right, (((1,), (1,)), ((), ())), preferred_element_type=F32)


def dot(left, right):
    return jnp.dot(left, right, preferred_element_type=F32)


def mixer_inputs(extended, conv_weight, valid, beta_logit, beta_bias, live):
    width, heads = beta_logit.shape
    ksize = conv_weight.shape[1]
    summed = extended[0:width] * conv_weight[:, 0, :][None] * valid[:, 0, None, None]
    for offset in range(1, ksize):
        summed = (
            summed
            + extended[offset : offset + width]
            * conv_weight[:, offset, :][None]
            * valid[:, offset, None, None]
        )
    active = jax.nn.silu(summed).reshape(width, 3, heads, -1)
    depth = active.shape[3]
    queries = unit_rows(active[:, 0]) * depth ** (-0.5)
    keys = unit_rows(active[:, 1])
    values = active[:, 2]
    beta = jax.nn.sigmoid(beta_logit + beta_bias) * live[:, None]
    return (queries, keys, values, beta)


def mm(spec, a, b):
    return jnp.einsum(spec, a, b, precision=HIGHEST)


def inverse_of(lower):
    size = lower.shape[-1]
    row = jnp.arange(size)[:, None]
    col = jnp.arange(size)[None, :]
    found = jnp.eye(size, dtype=F32) - lower * ((row // 2 == col // 2)).astype(F32)
    block = 2
    while block < size:
        joint = (row // (2 * block) == col // (2 * block)) & (row // block != col // block)
        step = mm("...ts,...su->...tu", lower * joint.astype(F32), found)
        found = found - mm("...ts,...su->...tu", found, step)
        block *= 2
    return found


class Chunks:
    def __init__(self, queries, keys, values, beta, documents, previous):
        size = documents.shape[1]
        order = jnp.arange(size, dtype=jnp.int32)
        same = documents[:, :, None] == documents[:, None, :]
        self.q, self.k, self.v, self.beta = queries, keys, values, beta
        self.strict = (same & (order[:, None] > order[None, :])[None]).astype(F32)
        self.weak = (same & (order[:, None] >= order[None, :])[None]).astype(F32)
        self.cont = (documents == previous[:, None]).astype(F32)
        self.clos = (documents == documents[:, size - 1 :]).astype(F32)
        self.keep = self.cont[:, size - 1]
        k, q = keys, queries
        rate = beta[:, :, None, :]
        self.kk = mm("hctd,hcsd->hcts", k, k)
        self.qk = mm("hctd,hcsd->hcts", q, k)
        self.inv = inverse_of(self.kk * rate * self.strict)
        self.mix = self.qk * rate * self.weak
        self.wk = k * (beta * self.clos)[..., None]
        plain = mm("hcts,hcse->hcte", self.inv, values)
        reach = mm("hcts,hcsd->hctd", self.inv, k * self.cont[..., None])
        self.plain, self.reach = plain, reach
        self.read = q * self.cont[..., None] - mm("hcts,hcsd->hctd", self.mix, reach)
        self.direct = mm("hcts,hcse->hcte", self.mix, plain)
        eye = jnp.eye(k.shape[-1], dtype=F32)
        self.trans = self.keep[:, None, None] * eye - mm("hctd,hcte->hcde", self.wk, reach)
        self.fresh = mm("hctd,hcte->hcde", self.wk, plain)

    def whole(self):
        count = self.trans.shape[1]
        total, added = self.trans[:, 0], self.fresh[:, 0]
        for c in range(1, count):
            total = mm("hde,hef->hdf", self.trans[:, c], total)
            added = mm("hde,hef->hdf", self.trans[:, c], added) + self.fresh[:, c]
        return total, added

    def outputs(self, incoming):
        states = [incoming]
        for c in range(self.trans.shape[1] - 1):
            states.append(mm("hde,hef->hdf", self.trans[:, c], states[-1]) + self.fresh[:, c])
        self.states = jnp.stack(states, axis=1)
        return self.direct + mm("hctd,hcdf->hctf", self.read, self.states)

    def leak(self, grad_out):
        self.from_out = mm("hctd,hcte->hcde", self.read, grad_out)
        total = self.from_out[:, -1]
        for c in range(self.trans.shape[1] - 2, -1, -1):
            total = mm("hed,hef->hdf", self.trans[:, c], total) + self.from_out[:, c]
        return total

    def back(self, grad_out, leaving):
        grads = [leaving]
        for c in range(self.trans.shape[1] - 1, 0, -1):
            grads.append(mm("hed,hef->hdf", self.trans[:, c], grads[-1]) + self.from_out[:, c])
        ds = jnp.stack(grads[::-1], axis=1)
        q, k, beta, s = self.q, self.k, self.beta, self.states
        rate = beta[:, :, None, :]
        u = self.plain - mm("hctd,hcde->hcte", self.reach, s)
        kds = mm("hctd,hcde->hcte", k, ds)
        du = mm("hcts,hcte->hcse", self.mix, grad_out) + (beta * self.clos)[..., None] * kds
        dr = mm("hcts,hcte->hcse", self.inv, du)
        dp = mm("hcte,hcse->hcts", grad_out, u) * self.weak
        dl = -mm("hcte,hcse->hcts", dr, u) * self.strict
        dbeta = jnp.sum(dp * self.qk + dl * self.kk, axis=2) + self.clos * jnp.sum(kds * u, axis=-1)
        dqk = dp * rate
        da = dl * rate
        cont = self.cont[..., None]
        dq = cont * mm("hcte,hcde->hctd", grad_out, s) + mm("hcts,hcsd->hctd", dqk, k)
        dk = (
            mm("hcts,hctd->hcsd", dqk, q)
            + (beta * self.clos)[..., None] * mm("hcte,hcde->hctd", u, ds)
            - cont * mm("hcte,hcde->hctd", dr, s)
            + mm("hcts,hcsd->hctd", da, k)
            + mm("hcts,hctd->hcsd", da, k)
        )
        return dq, dk, dr, dbeta


def body(
    tokens,
    cotangent,
    lengths,
    pad_mask,
    attn_gain,
    projection_weight,
    w_beta,
    beta_bias,
    conv_weight,
    head_gain,
    mlp_gain,
    w_gate,
    w_up,
    w_down,
):
    width, model = tokens.shape
    heads = w_beta.shape[1]
    depth = head_gain.shape[0]
    ksize = conv_weight.shape[1]
    margin = ksize - 1
    lanes, blocks = lax.axis_size("ta"), lax.axis_size("dev")
    rank, place = lax.axis_index("ta"), lax.axis_index("dev")
    own_heads = heads // lanes
    cols = own_heads * depth
    rows = projection_weight.shape[0]
    group = lanes * width
    ring = Ring()

    positions = place * group + jnp.arange(group, dtype=jnp.int32)
    documents = document_of(lengths, positions)
    valid = jnp.stack(
        [
            (document_of(lengths, positions - margin + offset) == documents).astype(F32)
            for offset in range(ksize)
        ],
        axis=1,
    )
    previous = document_of(lengths, positions[::width] - 1)

    split = jnp.transpose(
        projection_weight[:, 0:3].reshape(rows, 3, lanes, cols), (2, 0, 1, 3)
    ).reshape(lanes, rows, 3 * cols)
    beta_split = jnp.transpose(w_beta.reshape(rows, lanes, own_heads), (1, 0, 2))
    own_rows = in_order(exchange(split, rank), rank, 0)
    own_beta = in_order(exchange(beta_split, rank), rank, 0)
    wqkv = ring.gather(own_rows).reshape(model, 3 * cols)
    wbeta = ring.gather(own_beta).reshape(model, own_heads)

    live_row = jnp.zeros((8, model), BF).at[0, 0:width].set(pad_mask.astype(BF))
    packed = in_order(gather_parts(jnp.concatenate([tokens, live_row], axis=0)[None]), rank, 0)
    halo = shifted(packed[lanes - 1, width - 8 :], 1)
    group_tokens = packed[:, :width].reshape(group, model).astype(F32)
    live = packed[:, width, 0:width].reshape(group).astype(F32)
    live_ext = jnp.concatenate([halo[8, width - 8 : width].astype(F32), live])
    normed = rms_scale(jnp.concatenate([halo[0:8].astype(F32), group_tokens], axis=0), attn_gain)
    normed = normed.astype(BF)
    normed_group = normed[8:]
    projected = dot(normed, wqkv) * live_ext[:, None]
    extended = projected[8 - margin :].reshape(group + margin, 3, cols)
    beta_logit = dot(normed_group, wbeta)

    own_conv = lax.dynamic_slice_in_dim(conv_weight, rank * cols, cols, 2)
    own_bias = lax.dynamic_slice_in_dim(beta_bias, rank * own_heads, own_heads, 0)

    def prepare(extended, conv_weight, beta_logit, beta_bias):
        return mixer_inputs(extended, conv_weight, valid, beta_logit, beta_bias, live)

    (queries, keys, values, beta), prepare_back = jax.vjp(
        prepare, extended, own_conv, beta_logit, own_bias
    )

    def by_chunk(x):
        return jnp.transpose(x.reshape(lanes, width, own_heads, depth), (2, 0, 1, 3))

    def by_token(x):
        return jnp.transpose(x, (1, 2, 0, 3)).reshape(group, own_heads, depth)

    chunks = Chunks(
        by_chunk(queries),
        by_chunk(keys),
        by_chunk(values),
        jnp.transpose(beta.reshape(lanes, width, own_heads), (2, 0, 1)),
        documents.reshape(lanes, width),
        previous,
    )
    whole_map, whole_add = chunks.whole()
    both = ring.gather(jnp.stack([whole_map, whole_add]).astype(BF))
    incoming = jnp.zeros((own_heads, depth, depth), F32)
    for i in range(blocks - 1):
        new = mm("hde,hef->hdf", both[i, 0].astype(F32), incoming) + both[i, 1].astype(F32)
        incoming = jnp.where(i < place, new, incoming)
    outputs = by_token(chunks.outputs(incoming))

    head_normed, head_back = jax.vjp(head_norm, outputs, head_gain)
    heads_low = in_order(gather_parts(head_normed.astype(BF)), rank, 1)
    w_out = lax.all_gather(projection_weight[:, 3], BOTH, axis=0, tiled=True)
    residual = group_tokens + dot(heads_low, w_out)
    feed_rows = rms_scale(residual, mlp_gain).astype(BF)
    own_residual = lax.dynamic_slice_in_dim(residual, rank * width, width, 0)
    own_feed = lax.dynamic_slice_in_dim(feed_rows, rank * width, width, 0)
    feed_all = lax.all_gather(own_feed, BOTH, axis=0, tiled=True)
    cot_all = lax.all_gather(cotangent, BOTH, axis=0, tiled=True)
    cot_group = lax.dynamic_slice_in_dim(cot_all, place * group, group, 0)

    def feed_forward(feed, grad_rows):
        gate = dot(feed, w_gate)
        lifted = dot(feed, w_up)
        sig = jax.nn.sigmoid(gate)
        swish = gate * sig
        hidden = (swish * lifted).astype(BF)
        grad_hidden = contract_cols(grad_rows, w_down)
        grad_gate = (grad_hidden * lifted * sig * (1.0 + gate * (1.0 - sig))).astype(BF)
        grad_lifted = (grad_hidden * swish).astype(BF)
        return hidden, grad_gate, grad_lifted

    hidden, grad_gate, grad_lifted = feed_forward(feed_rows, cot_group)
    partial_feed = contract_cols(grad_gate, w_gate) + contract_cols(grad_lifted, w_up)
    grad_feed = scatter_sum(partial_feed.astype(BF).reshape(lanes, width, model), rank)
    branch = scatter_sum(dot(hidden, w_down).astype(BF).reshape(lanes, width, model), rank)
    block_out = (own_residual + branch).astype(BF)

    hidden, grad_gate, grad_lifted = feed_forward(feed_all, cot_all)
    grad_w_down = contract_rows(hidden, cot_all)
    grad_w_gate = contract_rows(feed_all, grad_gate)
    grad_w_up = contract_rows(feed_all, grad_lifted)

    _, feed_back = jax.vjp(rms_scale, own_residual, mlp_gain)
    grad_from_feed, grad_mlp_gain = feed_back(grad_feed)
    grad_residual = cotangent.astype(F32) + grad_from_feed
    grad_mixed = grad_residual.astype(BF)
    grad_heads = contract_cols(grad_mixed, w_out).astype(BF)

    def to_heads(x):
        split = jnp.transpose(x.reshape(width, lanes, cols), (1, 0, 2))
        return in_order(exchange(split, rank), rank, 0)

    grad_heads = to_heads(grad_heads).astype(F32)
    mixed_cols = to_heads(grad_mixed)
    grad_outputs, grad_head_gain = head_back(grad_heads)
    grad_outputs = by_chunk(grad_outputs)
    leaks = ring.gather(chunks.leak(grad_outputs).astype(BF))
    leaving = jnp.zeros((own_heads, depth, depth), F32)
    for i in range(blocks - 1, 0, -1):
        new = mm("hed,hef->hdf", both[i, 0].astype(F32), leaving) + leaks[i].astype(F32)
        leaving = jnp.where(i > place, new, leaving)
    grad_q, grad_k, grad_v, grad_beta = chunks.back(grad_outputs, leaving)
    grad_extended, grad_conv, grad_logit, grad_bias = prepare_back(
        (
            by_token(grad_q),
            by_token(grad_k),
            by_token(grad_v),
            jnp.transpose(grad_beta, (1, 2, 0)).reshape(group, own_heads),
        )
    )
    spilled = shifted(grad_extended[:margin].astype(BF), -1).astype(F32)
    grad_masked = grad_extended[margin:] + jnp.concatenate(
        [jnp.zeros((group - margin, 3, cols), F32), spilled], axis=0
    )
    grad_projected = (grad_masked * live[:, None, None]).astype(BF).reshape(group, 3 * cols)
    grad_logit_low = grad_logit.astype(BF)
    partial_normed = contract_cols(grad_projected, wqkv) + contract_cols(grad_logit_low, wbeta)
    grad_normed = scatter_sum(partial_normed.astype(BF).reshape(lanes, width, model), rank)
    _, attention_back = jax.vjp(rms_scale, tokens.astype(F32), attn_gain)
    grad_from_norm, grad_attn_gain = attention_back(grad_normed)
    grad_tokens = grad_residual + grad_from_norm

    def weight_rows(partial):
        share = partial.shape[1]
        part = ring.scatter(partial.astype(BF).reshape(blocks, model // blocks, share))
        return exchange(part.astype(BF).reshape(lanes, rows, share), rank)

    qkv_parts = weight_rows(contract_rows(normed_group, grad_projected))
    out_parts = weight_rows(contract_rows(heads_low, mixed_cols))
    qkv_grad = in_order([p.astype(F32).reshape(rows, 3, cols) for p in qkv_parts], rank, 2)
    out_grad = in_order([p.astype(F32) for p in out_parts], rank, 1)
    grad_projection = jnp.concatenate([qkv_grad, out_grad[:, None]], axis=1)

    partial_wbeta = contract_rows(normed_group, grad_logit_low)
    sizes = [3 * ksize * cols, own_heads * model, own_heads]
    flat = jnp.concatenate([grad_conv.reshape(-1), partial_wbeta.T.reshape(-1), grad_bias])
    flat = jnp.pad(flat, (0, -flat.shape[0] % 1024)).reshape(-1, 128)
    flat = in_order(gather_parts(sum_over(flat, "dev")[None]), rank, 0).reshape(lanes, -1)
    conv_sum = flat[:, : sizes[0]].reshape(lanes, 3, ksize, cols)
    conv_sum = jnp.transpose(conv_sum, (1, 2, 0, 3)).reshape(3, ksize, lanes * cols)
    wbeta_sum = flat[:, sizes[0] : sizes[0] + sizes[1]].reshape(heads, model).T
    grad_w_beta = lax.dynamic_slice_in_dim(wbeta_sum, (place * lanes + rank) * rows, rows, 0)
    bias_sum = flat[:, sizes[0] + sizes[1] : sum(sizes)].reshape(heads)

    gains = jnp.concatenate([grad_mlp_gain, grad_head_gain, grad_attn_gain])
    gains = jnp.pad(gains, (0, -gains.shape[0] % 1024)).reshape(-1, 128)
    gains = sum_over(sum_over(gains, "dev"), "ta").reshape(-1)
    return (
        block_out,
        grad_tokens,
        gains[model + depth : 2 * model + depth],
        grad_projection,
        grad_w_beta,
        bias_sum,
        conv_sum,
        gains[model : model + depth],
        gains[:model],
        grad_w_gate,
        grad_w_up,
        grad_w_down,
    )


def solution(mesh):
    rows = P(BOTH, None)
    three = P(BOTH, None, None)
    return jax.shard_map(
        body,
        mesh=mesh,
        in_specs=(
            rows,
            rows,
            P(),
            P(BOTH),
            P(),
            three,
            rows,
            P(),
            P(),
            P(),
            P(),
            P(None, "ta"),
            P(None, "ta"),
            P("ta", None),
        ),
        out_specs=(
            rows,
            rows,
            P(),
            three,
            rows,
            P(),
            P(),
            P(),
            P(),
            P(None, "ta"),
            P(None, "ta"),
            P("ta", None),
        ),
        check_vma=False,
    )
```

```python
import functools

import jax
import jax.numpy as jnp
from jax import lax
from jax.experimental import pallas as pl
from jax.experimental.pallas import tpu as pltpu
from jax.sharding import PartitionSpec as P

NORM_EPS = 1e-06
HEAD_EPS = 1e-05
UNIT_EPS = 1e-06
BOTH = ("dev", "ta")
BF = jnp.bfloat16
F32 = jnp.float32


def swap(x, axis, bit):
    return lax.ppermute(x, axis, [(i, i ^ bit) for i in range(lax.axis_size(axis))])


def gather_parts(x):
    parts = [x]
    for j in range(1, lax.axis_size("ta")):
        bit = j & -j
        parts.append(swap(parts[j ^ bit], "ta", bit))
    return parts


def in_order(parts, rank, axis):
    size = parts[0].shape[axis]
    shape = list(parts[0].shape)
    shape[axis] = size * len(parts)
    joined = jnp.zeros(shape, parts[0].dtype)
    for j, part in enumerate(parts):
        joined = lax.dynamic_update_slice_in_dim(joined, part, (rank ^ j) * size, axis)
    return joined


def exchange(blocks, rank):
    lanes = lax.axis_size("ta")
    parts = []
    for j in range(lanes):
        block = lax.dynamic_index_in_dim(blocks, rank ^ j, 0, False)
        parts.append(swap(block, "ta", j) if j else block)
    return parts


def scatter_sum(blocks, rank, beside=None):
    lanes = lax.axis_size("ta")
    made = None
    bit = 1
    while bit < lanes:
        pairs = blocks.reshape((blocks.shape[0] // 2, 2) + blocks.shape[1:])
        mine = (rank // bit) % 2
        kept = lax.dynamic_index_in_dim(pairs, mine, 1, False)
        sent = lax.dynamic_index_in_dim(pairs, 1 - mine, 1, False).astype(BF)
        arrived = swap(sent, "ta", bit)
        bit *= 2
        if beside and bit == lanes:
            made = beside(sent)
            arrived = gate(arrived, made[0])
        blocks = kept.astype(F32) + arrived.astype(F32)
    return (blocks[0], made) if beside else blocks[0]


def ring_order(size):
    if size % 2:
        return list(range(size))
    return list(range(0, size, 2)) + list(range(size - 1, 0, -2))


class Ring:
    def __init__(self):
        self.size = lax.axis_size("dev")
        self.order = ring_order(self.size)
        self.spot = [self.order.index(i) for i in range(self.size)]
        self.place = lax.axis_index("dev")

    def move(self, x, step):
        n = self.size
        return lax.ppermute(x, "dev", [(self.order[p], self.order[(p + step) % n]) for p in range(n)])

    def at(self, distance):
        n = self.size
        table = jnp.array([self.order[(self.spot[i] + distance) % n] for i in range(n)], jnp.int32)
        return table[self.place]

    def gather(self, x):
        last = self.size // 2
        half = x.shape[0] // 2
        joined = jnp.zeros((self.size,) + x.shape, x.dtype)

        def put_at(joined, part, distance):
            return lax.dynamic_update_index_in_dim(joined, part, self.at(distance), 0)

        joined = put_at(joined, x, 0)
        onward, back = x, x
        for s in range(1, last):
            onward, back = self.move(onward, 1), self.move(back, -1)
            joined = put_at(put_at(joined, onward, -s), back, s)
        far = [self.move(onward[:half], 1), self.move(back[half:], -1)]
        return put_at(joined, jnp.concatenate(far, axis=0), last)

    def scatter(self, blocks, beside=()):
        last = self.size // 2
        half = blocks.shape[1] // 2
        beside = list(beside) + [None] * last

        def block(distance):
            return lax.dynamic_index_in_dim(blocks, self.at(distance), 0, False)

        far = block(last)
        right, left = far[:half], far[half:]
        for s in range(last - 1, -1, -1):
            ahead, behind = self.move(right, 1), self.move(left, -1)
            if beside[last - 1 - s]:
                token = beside[last - 1 - s](right)
                ahead, behind = gate(ahead, token), gate(behind, token)
            ahead, behind = ahead.astype(F32), behind.astype(F32)
            if s:
                right, left = block(s).astype(F32), block(-s).astype(F32)
                if s == last - 1:
                    right = jnp.concatenate([right[:half] + ahead, right[half:]], axis=0)
                    left = jnp.concatenate([left[:half], left[half:] + behind], axis=0)
                else:
                    right, left = right + ahead, left + behind
                right, left = right.astype(BF), left.astype(BF)
        return block(0).astype(F32) + ahead + behind


def gather_dev(x):
    place = lax.axis_index("dev")
    held = x[None]
    bit = 1
    while bit < lax.axis_size("dev"):
        other = swap(held, "dev", bit)
        upper = (place // bit) % 2 == 1
        held = jnp.concatenate([jnp.where(upper, other, held), jnp.where(upper, held, other)], axis=0)
        bit *= 2
    return held


def sum_over(x, axis):
    size = lax.axis_size(axis)
    bit = 1
    while bit < size:
        x = x + swap(x, axis, bit)
        bit *= 2
    return x


def gate(x, *deps):
    return pl.pallas_call(
        lambda *refs: None,
        name="gate",
        out_shape=jax.ShapeDtypeStruct(x.shape, x.dtype),
        in_specs=[pl.BlockSpec(memory_space=pl.ANY)] * (1 + len(deps)),
        out_specs=pl.BlockSpec(memory_space=pl.ANY),
        input_output_aliases={0: 0},
    )(x, *deps)


def shifted(x, distance):
    devices = range(lax.axis_size("dev"))
    return lax.ppermute(x, "dev", [(i - distance, i) for i in devices if i - distance in devices])


def rms_scale(values, gain):
    return values * lax.rsqrt(jnp.mean(values * values, axis=-1, keepdims=True) + NORM_EPS) * gain


def document_of(lengths, positions):
    starts = jnp.cumsum(lengths) - lengths
    above = (starts[None, :] <= positions[:, None]).astype(jnp.int32)
    return jnp.sum(above, axis=1) - 1


def contract_rows(left, right):
    return lax.dot_general(left, right, (((0,), (0,)), ((), ())), preferred_element_type=F32)


def contract_cols(left, right):
    return lax.dot_general(left, right, (((1,), (1,)), ((), ())), preferred_element_type=F32)


def dot(left, right):
    return jnp.dot(left, right, preferred_element_type=F32)


PAD = 8
VMEM_LIMIT = 48 * 1024 * 1024
FFN_VMEM = 56 * 1024 * 1024


def dims(a, b, ca, cb):
    return lax.dot_general(a, b, (((ca,), (cb,)), ((), ())), preferred_element_type=F32)


def d1(a, b, ca=1, cb=0):
    return dims(a.astype(BF), b.astype(BF), ca, cb)


def parts_of(a):
    high = a.astype(BF)
    return high, (a - high.astype(F32)).astype(BF)


def d3(a, b, ca=1, cb=0):
    ah, al = parts_of(a)
    bh, bl = parts_of(b)
    return dims(ah, bh, ca, cb) + (dims(ah, bl, ca, cb) + dims(al, bh, ca, cb))


def iotas(size):
    return (
        lax.broadcasted_iota(jnp.int32, (size, size), 0),
        lax.broadcasted_iota(jnp.int32, (size, size), 1),
    )


def inverses_of(lowers):
    size = lowers[0].shape[0]
    row, col = iotas(size)
    eye = (row == col).astype(F32)
    pair = (row // 2 == col // 2).astype(F32)
    found = [eye - low * pair for low in lowers]
    block = 2
    while block < size:
        joint = ((row // (2 * block) == col // (2 * block)) & (row // block != col // block)).astype(F32)
        steps = [d3(low * joint, x) for low, x in zip(lowers, found)]
        found = [x - d3(x, s) for x, s in zip(found, steps)]
        block *= 2
    return found


def unit_of(active):
    scale = lax.rsqrt(jnp.sum(active * active, axis=-1, keepdims=True) + UNIT_EPS)
    return active * scale, scale


def masks_of(aux, row, at, size):
    doc, doc_row = aux[at, 6:7], row[6:7, at]
    r, c = iotas(size)
    same = doc == doc_row
    weak = (same & (r >= c)).astype(F32)
    strict = (same & (r > c)).astype(F32)
    return weak, strict


def forward_kernel(size, xq, xk, xv, conv, aux_ref, row_ref, yq, yk, yv, inv, plain, reach, read, direct, trans, fresh, whole):
    count = inv.shape[1]
    depth = xq.shape[1]
    ksize = conv.shape[1]
    aux, row = aux_ref.at[0], row_ref.at[0]
    r, c = iotas(depth)
    eye = (r == c).astype(F32)
    spans = [slice(n * size, (n + 1) * size) for n in range(count)]
    saved = []
    lowers = []
    for n, at in enumerate(spans):
        active = []
        for i, (x, y) in enumerate(((xq, yq), (xk, yk), (xv, yv))):
            first = PAD - (ksize - 1) + n * size
            summed = x[first + ksize - 1 : first + ksize - 1 + size, :] * conv[i, ksize - 1 : ksize, :]
            for j in range(ksize - 1):
                summed = summed + x[first + j : first + j + size, :] * conv[i, j : j + 1, :] * aux[at, j : j + 1]
            y[at, :] = summed
            active.append(summed * jax.nn.sigmoid(summed))
        q = unit_of(active[0])[0] * depth ** (-0.5)
        k = unit_of(active[1])[0]
        weak, strict = masks_of(aux, row, at, size)
        rate = row[7:8, at]
        products = d3(jnp.concatenate([q, k], axis=0), k, 1, 1)
        lowers.append(products[size:] * rate * strict)
        saved.append((q, k, active[2], products[:size] * rate * weak))
    inverses = inverses_of(lowers)
    total = added = None
    for n, at in enumerate(spans):
        q, k, v, mix = saved[n]
        cont, clos, beta = aux[at, 3:4], aux[at, 4:5], aux[at, 7:8]
        both = d3(inverses[n], jnp.concatenate([v, k * cont], axis=1))
        spread = d3(mix, both)
        inv[0, n] = inverses[n]
        plain[0, at, :] = both[:, :depth]
        reach[0, at, :] = both[:, depth:]
        direct[0, at, :] = spread[:, :depth]
        read[0, at, :] = q * cont - spread[:, depth:]
        gained = d3(k * (beta * clos), both, 0, 0)
        map_n = aux[(n + 1) * size - 1 : (n + 1) * size, 3:4] * eye - gained[:, depth:]
        add_n = gained[:, :depth]
        trans[0, n] = map_n
        fresh[0, n] = add_n
        if n == 0:
            total, added = map_n, add_n
        else:
            new = d3(map_n, jnp.concatenate([added, total], axis=1))
            total, added = new[:, depth:], new[:, :depth] + add_n
    whole[0, 0] = total.astype(BF)
    whole[0, 1] = added.astype(BF)


def read_kernel(size, place, both, trans, fresh, read, direct, gain, states, outputs, normed):
    heads, count = trans.shape[0], trans.shape[1]
    depth = trans.shape[-1]

    def earlier(i, carry):
        return tuple(
            d3(both[i, h, 0].astype(F32), carry[h]) + both[i, h, 1].astype(F32) for h in range(heads)
        )

    carry = lax.fori_loop(0, place[0], earlier, tuple(jnp.zeros((depth, depth), F32) for _ in range(heads)))
    carry = list(carry)
    for n in range(count):
        at = slice(n * size, (n + 1) * size)
        for h in range(heads):
            state = carry[h]
            states[h, n] = state
            out = direct[h, at, :] + d3(read[h, at, :], state)
            cols = slice(h * depth, (h + 1) * depth)
            outputs[at, cols] = out
            scale = lax.rsqrt(jnp.mean(out * out, axis=-1, keepdims=True) + HEAD_EPS)
            normed[at, cols] = (out * scale * gain[...]).astype(BF)
            if n < count - 1:
                carry[h] = d3(trans[h, n], state) + fresh[h, n]


def leak_kernel(size, grads, outputs, gain, read, trans, grad_out, from_out, leak, grad_gain):
    heads, count = trans.shape[0], trans.shape[1]
    depth = trans.shape[-1]
    gained = jnp.zeros((1, depth), F32)
    totals = [None] * heads
    for n in range(count - 1, -1, -1):
        at = slice(n * size, (n + 1) * size)
        for h in range(heads):
            cols = slice(h * depth, (h + 1) * depth)
            out, grad = outputs[at, cols], grads[at, cols].astype(F32)
            scale = lax.rsqrt(jnp.mean(out * out, axis=-1, keepdims=True) + HEAD_EPS)
            unit = out * scale
            gained = gained + jnp.sum(grad * unit, axis=0, keepdims=True)
            grad = grad * gain[...]
            grad = scale * (grad - unit * jnp.mean(grad * unit, axis=-1, keepdims=True))
            grad_out[h, at, :] = grad
            term = d3(read[h, at, :], grad, 0, 0)
            from_out[h, n] = term
            totals[h] = term if n == count - 1 else d3(trans[h, n], totals[h], 0, 0) + term
    for h in range(heads):
        leak[h] = totals[h].astype(BF)
    grad_gain[...] = gained


def chain_kernel(place, both, leaks, trans, from_out, grads):
    heads, count = trans.shape[0], trans.shape[1]
    depth = trans.shape[-1]
    devices = both.shape[0]

    def later(i, carry):
        at = devices - 1 - i
        return tuple(
            d3(both[at, h, 0].astype(F32), carry[h], 0, 0) + leaks[at, h].astype(F32) for h in range(heads)
        )

    zero = tuple(jnp.zeros((depth, depth), F32) for _ in range(heads))
    carry = list(lax.fori_loop(0, devices - 1 - place[0], later, zero))
    for n in range(count - 1, -1, -1):
        for h in range(heads):
            grads[h, n] = carry[h]
            if n:
                carry[h] = d3(trans[h, n], carry[h], 0, 0) + from_out[h, n]


def backward_kernel(size, xq, xk, xv, yq, yk, yv, conv, aux_ref, row_ref, inv, plain, reach, states, grads, grad_out,
                    gq, gk, gv, tail, spill, grad_conv, grad_beta, zs):
    count = inv.shape[1]
    depth = xq.shape[1]
    ksize = conv.shape[1]
    aux, row = aux_ref.at[0], row_ref.at[0]
    length = count * size
    scale_q = depth ** (-0.5)
    for n in range(count):
        at = slice(n * size, (n + 1) * size)
        cont, clos, beta = aux[at, 3:4], aux[at, 4:5], aux[at, 7:8]
        weak, strict = masks_of(aux, row, at, size)
        rate = row[7:8, at]
        ys = [yq[at, :], yk[at, :], yv[at, :]]
        sigs = [jax.nn.sigmoid(y) for y in ys]
        uq, rq = unit_of(ys[0] * sigs[0])
        k, rk = unit_of(ys[1] * sigs[1])
        q = uq * scale_q
        products = d1(jnp.concatenate([q, k], axis=0), k, 1, 1)
        qk, kk = products[:size], products[size:]
        mix = qk * rate * weak
        state, grad_state, dout = states[0, n], grads[0, n], grad_out[0, at, :]
        u = plain[0, at, :] - d1(reach[0, at, :], state)
        kds = d1(k, grad_state)
        written = beta * clos
        du = d1(mix, dout, 0, 0) + written * kds
        dr = d1(inv[0, n], du, 0, 0)
        pair = jnp.concatenate([dout, dr], axis=0)
        outer = d1(pair, u, 1, 1)
        through = d1(pair, state, 1, 1)
        dp = outer[:size] * weak
        dl = -outer[size:] * strict
        per_key = jnp.sum(dp * qk + dl * kk, axis=0, keepdims=True)
        per_state = jnp.sum((kds * u).T, axis=0, keepdims=True)
        grad_beta[0, :, at] = per_key + row[4:5, at] * per_state
        dqk = dp * rate
        da = dl * rate
        dq = cont * through[:size] + d1(dqk, k)
        dk = d1(dqk, q, 0, 0) + written * d1(u, grad_state, 1, 1) - cont * through[size:] + d1(da + da.T, k)
        dq = dq * scale_q
        acts = [
            rq * (dq - uq * jnp.sum(uq * dq, axis=-1, keepdims=True)),
            rk * (dk - k * jnp.sum(k * dk, axis=-1, keepdims=True)),
            dr,
        ]
        for i, x in enumerate((xq, xk, xv)):
            dy = acts[i] * sigs[i] * (1.0 + ys[i] * (1.0 - sigs[i]))
            first = PAD - (ksize - 1) + n * size
            for j in range(ksize):
                dv = dy if j == ksize - 1 else dy * aux[at, j : j + 1]
                term = jnp.sum(dv * x[first + j : first + j + size, :], axis=0, keepdims=True)
                before = jnp.zeros_like(term) if n == 0 else grad_conv[i, j : j + 1, :]
                grad_conv[i, j : j + 1, :] = before + term
                zs[i, j, PAD + n * size : PAD + (n + 1) * size, :] = dv * conv[i, j : j + 1, :]
    for i, g in enumerate((gq, gk, gv)):
        for j in range(ksize):
            zs[i, j, 0:PAD, :] = jnp.zeros((PAD, depth), F32)
            zs[i, j, PAD + length : 2 * PAD + length, :] = jnp.zeros((PAD, depth), F32)

        def shifted_sum(first, rows):
            return sum(zs[i, j, first + ksize - 1 - j : first + ksize - 1 - j + rows, :] for j in range(ksize))

        for n in range(count):
            at = slice(n * size, (n + 1) * size)
            g[at, :] = (shifted_sum(PAD + n * size, size) * aux[at, 5:6]).astype(BF)
        tail[i] = shifted_sum(length, PAD)
        spill[i] = shifted_sum(0, PAD)


def vmem_call(name, kernel, out_shape, inputs, flops, deps=()):
    return pl.pallas_call(
        lambda *refs: kernel(*refs[: len(inputs)], *refs[len(inputs) + len(deps) :]),
        name=name,
        out_shape=out_shape,
        in_specs=[
            pl.BlockSpec(memory_space=pltpu.SMEM if x.dtype == jnp.int32 else pltpu.VMEM) for x in inputs
        ]
        + [pl.BlockSpec(memory_space=pl.ANY)] * len(deps),
        out_specs=[pl.BlockSpec(memory_space=pltpu.VMEM)] * len(out_shape),
        cost_estimate=cost(flops, inputs, out_shape),
        compiler_params=pltpu.CompilerParams(vmem_limit_bytes=VMEM_LIMIT),
    )(*inputs, *deps)


def cost(flops, inputs, outputs):
    moved = sum(x.size * x.dtype.itemsize for x in list(inputs) + list(outputs))
    return pl.CostEstimate(flops=int(flops), bytes_accessed=int(moved), transcendentals=0)


def shape(dims, dtype=F32):
    return jax.ShapeDtypeStruct(dims, dtype)


class Mixer:
    def __init__(self, projected, own_conv, aux, row, size):
        self.size = size
        self.heads, self.length = aux.shape[0], aux.shape[1]
        self.depth = own_conv.shape[2] // self.heads
        self.count = self.length // size
        self.projected, self.conv, self.aux, self.row = projected, own_conv, aux, row
        heads, length, depth, count = self.heads, self.length, self.depth, self.count
        ksize = own_conv.shape[1]
        self.token_specs = [
            pl.BlockSpec((length + PAD, depth), lambda h, i=i: (0, i * heads + h)) for i in range(3)
        ]
        self.head_cols = pl.BlockSpec((length, depth), lambda h: (0, h))
        self.conv_spec = pl.BlockSpec((3, ksize, depth), lambda h: (0, 0, h))
        self.aux_specs = [
            pl.BlockSpec((1, length, 8), lambda h: (h, 0, 0)),
            pl.BlockSpec((1, 8, length), lambda h: (h, 0, 0)),
        ]
        self.chunk_spec = pl.BlockSpec((1, count, depth, depth), lambda h: (h, 0, 0, 0))
        self.inv_spec = pl.BlockSpec((1, count, size, size), lambda h: (h, 0, 0, 0))
        self.rows_spec = pl.BlockSpec((1, length, depth), lambda h: (h, 0, 0))
        self.flops = 2 * heads * count * size * depth * depth
        inputs = [projected] * 3 + [own_conv, aux, row]
        square = shape((heads, count, depth, depth))
        tokens = shape((heads, length, depth))
        out_shape = (
            [shape((length, heads * depth))] * 3
            + [shape((heads, count, size, size))]
            + [tokens] * 4
            + [square] * 2
            + [shape((heads, 2, depth, depth), BF)]
        )
        (
            self.yq, self.yk, self.yv, self.inv, self.plain, self.reach, self.read, self.direct,
            self.trans, self.fresh, self.whole,
        ) = pl.pallas_call(
            functools.partial(forward_kernel, size),
            name="mixer_forward",
            out_shape=out_shape,
            grid=(heads,),
            in_specs=self.token_specs + [self.conv_spec] + self.aux_specs,
            out_specs=[self.head_cols] * 3
            + [self.inv_spec]
            + [self.rows_spec] * 4
            + [self.chunk_spec] * 2
            + [pl.BlockSpec((1, 2, depth, depth), lambda h: (h, 0, 0, 0))],
            cost_estimate=cost(60 * self.flops, inputs, out_shape),
            compiler_params=pltpu.CompilerParams(vmem_limit_bytes=VMEM_LIMIT),
        )(*inputs)

    def outputs(self, place, both, head_gain):
        heads, length, depth, count = self.heads, self.length, self.depth, self.count
        self.place, self.both, self.gain = place, both, head_gain
        self.states, self.out, normed = vmem_call(
            "mixer_read",
            functools.partial(read_kernel, self.size),
            [
                shape((heads, count, depth, depth)),
                shape((length, heads * depth)),
                shape((length, heads * depth), BF),
            ],
            [place, both, self.trans, self.fresh, self.read, self.direct, head_gain],
            12 * self.flops,
        )
        return normed

    def leak(self, grads, deps=()):
        heads, length, depth, count = self.heads, self.length, self.depth, self.count
        self.grad_out, self.from_out, leak, grad_gain = vmem_call(
            "mixer_leak",
            functools.partial(leak_kernel, self.size),
            [
                shape((heads, length, depth)),
                shape((heads, count, depth, depth)),
                shape((heads, depth, depth), BF),
                shape((1, depth)),
            ],
            [grads, self.out, self.gain, self.read, self.trans],
            6 * self.flops,
            deps,
        )
        return leak, grad_gain

    def back(self, leaks):
        heads, length, depth, count = self.heads, self.length, self.depth, self.count
        ksize = self.conv.shape[1]
        (grads,) = vmem_call(
            "mixer_chain",
            chain_kernel,
            [shape((heads, count, depth, depth))],
            [self.place, self.both, leaks, self.trans, self.from_out],
            6 * self.flops,
        )
        inputs = [self.projected] * 3 + [self.yq, self.yk, self.yv, self.conv, self.aux, self.row]
        inputs += [self.inv, self.plain, self.reach, self.states, grads, self.grad_out]
        edge = shape((3, PAD, heads * depth))
        out_shape = [shape((length, heads * depth), BF)] * 3 + [edge] * 2
        out_shape += [shape((3, ksize, heads * depth)), shape((heads, 1, length))]
        edge_spec = pl.BlockSpec((3, PAD, depth), lambda h: (0, 0, h))
        return pl.pallas_call(
            functools.partial(backward_kernel, self.size),
            name="mixer_backward",
            out_shape=out_shape,
            grid=(heads,),
            in_specs=self.token_specs
            + [self.head_cols] * 3
            + [self.conv_spec]
            + self.aux_specs
            + [self.inv_spec, self.rows_spec, self.rows_spec, self.chunk_spec, self.chunk_spec, self.rows_spec],
            out_specs=[self.head_cols] * 3
            + [edge_spec] * 2
            + [self.conv_spec, pl.BlockSpec((1, 1, length), lambda h: (h, 0, 0))],
            scratch_shapes=[pltpu.VMEM((3, ksize, length + 2 * PAD, depth), F32)],
            cost_estimate=cost(30 * self.flops, inputs, out_shape),
            compiler_params=pltpu.CompilerParams(vmem_limit_bytes=VMEM_LIMIT),
        )(*inputs)


ANY = pl.BlockSpec(memory_space=pl.ANY)
TOKEN = shape((8, 128))


def resident(x):
    return pl.BlockSpec(x.shape, lambda *_: (0,) * x.ndim, pipeline_mode=pl.Buffered(1))


def activations(gate, lifted, grad_hidden):
    sig = jax.nn.sigmoid(gate)
    swish = gate * sig
    return (
        (swish * lifted).astype(BF),
        (grad_hidden * lifted * sig * (1.0 + gate * (1.0 - sig))).astype(BF),
        (grad_hidden * swish).astype(BF),
    )


def chunks_of(size, chunk=256):
    return [slice(at, min(at + chunk, size)) for at in range(0, size, chunk)]


def params(flops, moved):
    return dict(
        cost_estimate=pl.CostEstimate(flops=int(flops), bytes_accessed=int(moved), transcendentals=0),
        compiler_params=pltpu.CompilerParams(vmem_limit_bytes=FFN_VMEM),
    )


TOKEN_SPEC = pl.BlockSpec((8, 128), lambda *_: (0, 0))


def own_kernel(groups, feed, cot, wg, wu, wd, hidden, grad_gate, grad_lifted, grad_feed, branch):
    units, model = wd.shape
    for cut in chunks_of(units):
        gated = jnp.dot(feed[...], wg[:, cut], preferred_element_type=F32)
        lifted = jnp.dot(feed[...], wu[:, cut], preferred_element_type=F32)
        grad_hidden = dims(cot[...], wd[cut, :], 1, 1)
        hidden[:, cut], grad_gate[:, cut], grad_lifted[:, cut] = activations(gated, lifted, grad_hidden)
    for cut in chunks_of(model):
        total = dims(grad_gate[...], wg[cut, :], 1, 1) + dims(grad_lifted[...], wu[cut, :], 1, 1)
        grad_feed[:, cut] = total.astype(BF)
        branch[:, cut] = jnp.dot(hidden[...], wd[:, cut], preferred_element_type=F32).astype(BF)


def hidden_kernel(groups, cot, wd, *refs):
    out, token = refs[-2:]
    out[...] = dims(cot[...], wd[...], 1, 1).astype(BF)
    token[...] = jnp.zeros_like(token)


def rows_kernel(groups, feed, grad_hidden, wg, wu, *refs):
    hidden, grad_gate, grad_lifted, token = refs[-4:]
    for cut in chunks_of(wg.shape[1]):
        gated = jnp.dot(feed[...], wg[:, cut], preferred_element_type=F32)
        lifted = jnp.dot(feed[...], wu[:, cut], preferred_element_type=F32)
        hidden[:, cut], grad_gate[:, cut], grad_lifted[:, cut] = activations(
            gated, lifted, grad_hidden[:, cut].astype(F32)
        )
    token[...] = jnp.zeros_like(token)


def by_group(name, kernel, groups, size, inputs, weights, outs, held, deps, products):
    tokens = inputs[0].shape[0]
    count = groups.shape[0]
    picked = lambda width: pl.BlockSpec((size, width), lambda i, g: (g[i], 0))
    first = 1 + len(inputs) + len(weights) + len(deps)
    return pl.pallas_call(
        kernel,
        name=name,
        out_shape=[shape((tokens, width), BF) for width in outs] + [TOKEN],
        grid_spec=pltpu.PrefetchScalarGridSpec(
            num_scalar_prefetch=1,
            grid=(count,),
            in_specs=[picked(x.shape[1]) for x in inputs]
            + [resident(w) for w in weights]
            + [ANY] * (len(deps) + len(held)),
            out_specs=[picked(width) for width in outs] + [TOKEN_SPEC],
        ),
        input_output_aliases={first + n: n for n in range(len(held))},
        **params(
            2 * count * size * weights[0].size * products,
            sum(w.size for w in weights) * 2 + count * size * 2 * (sum(outs) + sum(x.shape[1] for x in inputs)),
        ),
    )(groups, *inputs, *weights, *deps, *held)


def feed_own(place, feed, cot, weights, tokens):
    rows, model = feed.shape
    units = weights[0].shape[1]
    block = 256
    count = rows // block
    wide = pl.BlockSpec((block, units), lambda i, g: (g[0] * count + i, 0))
    here = pl.BlockSpec((block, model), lambda i, g: (i, 0))
    return pl.pallas_call(
        own_kernel,
        name="feed_own",
        out_shape=[shape((tokens, units), BF)] * 3 + [shape((rows, model), BF)] * 2,
        grid_spec=pltpu.PrefetchScalarGridSpec(
            num_scalar_prefetch=1,
            grid=(count,),
            in_specs=[here] * 2 + [resident(w) for w in weights],
            out_specs=[wide] * 3 + [here] * 2,
        ),
        **params(12 * rows * model * units, 6 * model * units + rows * (3 * units + 4 * model) * 2),
    )(place, feed, cot, *weights)


GRAD_COLS = 256


def grad_kernel(transposed, left, right, *refs):
    out, token = refs[-2:]
    term = dims(left[...], right[...], 0, 0)
    out[...] = term.T if transposed else term
    token[...] = jnp.zeros_like(token)


def weight_grad(part, parts, left, right, held, deps, transposed):
    rows, model = left.shape
    units = right.shape[1]
    count = model // GRAD_COLS // parts
    if transposed:
        out_spec = pl.BlockSpec((units, GRAD_COLS), lambda m: (0, part * count + m))
    else:
        out_spec = pl.BlockSpec((GRAD_COLS, units), lambda m: (part * count + m, 0))
    return pl.pallas_call(
        functools.partial(grad_kernel, transposed),
        name="weight_grad",
        out_shape=[shape((units, model) if transposed else (model, units)), TOKEN],
        grid=(count,),
        in_specs=[pl.BlockSpec((rows, GRAD_COLS), lambda m: (0, part * count + m)), resident(right)]
        + [ANY] * (len(deps) + len(held)),
        out_specs=[out_spec, pl.BlockSpec((8, 128), lambda m: (0, 0))],
        input_output_aliases={2 + len(deps) + n: n for n in range(len(held))},
        **params(
            2 * rows * count * GRAD_COLS * units,
            2 * rows * (units + count * GRAD_COLS) + 4 * count * GRAD_COLS * units,
        ),
    )(left, right, *deps, *held)


def body(
    tokens,
    cotangent,
    lengths,
    pad_mask,
    attn_gain,
    projection_weight,
    w_beta,
    beta_bias,
    conv_weight,
    head_gain,
    mlp_gain,
    w_gate,
    w_up,
    w_down,
):
    width, model = tokens.shape
    heads = w_beta.shape[1]
    depth = head_gain.shape[0]
    ksize = conv_weight.shape[1]
    margin = ksize - 1
    lanes, blocks = lax.axis_size("ta"), lax.axis_size("dev")
    rank, place = lax.axis_index("ta"), lax.axis_index("dev")
    own_heads = heads // lanes
    cols = own_heads * depth
    rows = projection_weight.shape[0]
    group = lanes * width
    ring = Ring()

    positions = place * group + jnp.arange(group, dtype=jnp.int32)
    documents = document_of(lengths, positions)
    valid = jnp.stack(
        [
            (document_of(lengths, positions - margin + offset) == documents).astype(F32)
            for offset in range(ksize)
        ],
        axis=1,
    )
    previous = document_of(lengths, positions[::width] - 1)

    extra = jnp.zeros((8, model), BF).at[0, 0:width].set(pad_mask.astype(BF))
    extra = extra.at[1, 0 : rows * heads].set(w_beta.reshape(-1))
    packed = in_order(gather_parts(jnp.concatenate([tokens, extra], axis=0)[None]), rank, 0)
    cot_group = in_order(gather_parts(cotangent), rank, 0)

    split = jnp.transpose(projection_weight.reshape(rows, 4, lanes, cols), (2, 0, 1, 3))
    own_rows = in_order(exchange(split.reshape(lanes, rows, 4 * cols), rank), rank, 0)
    w_all = ring.gather(own_rows).reshape(model, 4 * cols)
    w_out = in_order(gather_parts(w_all[:, 3 * cols :]), rank, 1)
    beta_rows = packed[:, width + 1, 0 : rows * heads].reshape(lanes * rows * heads // 128, 128)
    wbeta = gather_dev(beta_rows).reshape(model, lanes, own_heads)
    wbeta = lax.dynamic_index_in_dim(wbeta, rank, 1, False)
    cot_all = lax.all_gather(gate(cotangent, w_all), BOTH, axis=0, tiled=True)

    halo = shifted(packed[lanes - 1, width - 8 :], 1)
    group_tokens = packed[:, :width].reshape(group, model).astype(F32)
    live = packed[:, width, 0:width].reshape(group).astype(F32)
    live_ext = jnp.concatenate([halo[8, width - 8 : width].astype(F32), live])
    normed = rms_scale(jnp.concatenate([halo[0:8].astype(F32), group_tokens], axis=0), attn_gain)
    normed = normed.astype(BF)
    normed_group = normed[8:]
    projected = dot(normed, w_all) * live_ext[:, None]
    beta_logit = dot(normed_group, wbeta)

    own_conv = lax.dynamic_slice_in_dim(conv_weight, rank * cols, cols, 2)
    own_bias = lax.dynamic_slice_in_dim(beta_bias, rank * own_heads, own_heads, 0)
    sig_beta = jax.nn.sigmoid(beta_logit + own_bias)
    beta = sig_beta * live[:, None]
    chunk_docs = documents.reshape(lanes, width)
    continuing = (chunk_docs == previous[:, None]).reshape(group).astype(F32)
    closing = (chunk_docs == chunk_docs[:, width - 1 :]).reshape(group).astype(F32)
    shared = jnp.stack(
        [valid[:, j] for j in range(margin)] + [continuing, closing, live, documents.astype(F32)], axis=0
    )
    row = jnp.concatenate(
        [jnp.broadcast_to(shared, (own_heads,) + shared.shape), beta.T[:, None]], axis=1
    )
    mixer = Mixer(projected, own_conv, jnp.transpose(row, (0, 2, 1)), row, width)
    both = ring.gather(mixer.whole)
    at_place = place.astype(jnp.int32).reshape(1)
    head_normed = mixer.outputs(at_place, both, head_gain[None])
    heads_low = in_order(gather_parts(head_normed), rank, 1)
    residual = group_tokens + dot(heads_low, w_out)
    feed_rows = rms_scale(residual, mlp_gain).astype(BF)
    own_residual = lax.dynamic_slice_in_dim(residual, rank * width, width, 0)

    own_feed = lax.dynamic_slice_in_dim(feed_rows, rank * width, width, 0)
    feed_all = lax.all_gather(own_feed, BOTH, axis=0, tiled=True)

    weights = [w_gate, w_up, w_down]
    units = w_gate.shape[1]
    *arrays, partial_feed, partial_branch = feed_own(at_place, feed_rows, cot_group, weights, blocks * group)
    others = lax.rem(place + 1 + jnp.arange(blocks - 1, dtype=jnp.int32), blocks)
    grad_feed, (token, grad_hidden) = scatter_sum(
        partial_feed.reshape(lanes, width, model), rank,
        lambda sent: by_group(
            "feed_hidden", hidden_kernel, others, group, [cot_all], [w_down], [units], [], [sent], 1
        )[::-1],
    )
    row_parts = [others[: (blocks - 1) // 2], others[(blocks - 1) // 2 :]]

    def fill_rows(deps):
        *arrays[:], token = by_group(
            "feed_rows", rows_kernel, row_parts.pop(0), group, [feed_all, grad_hidden], weights[:2],
            [units] * 3, list(arrays), deps, 2,
        )
        return token

    grad_parts = [(which, part) for which in range(3) for part in range(2)]
    ffn_grads = [[], [], []]

    def fill_grads(*deps):
        which, part = grad_parts.pop(0)
        left = cot_all if which == 2 else feed_all
        hidden, grad_gate, grad_lifted = arrays
        right = (grad_gate, grad_lifted, hidden)[which]
        out, token = weight_grad(part, 2, left, right, ffn_grads[which], deps, which == 2)
        ffn_grads[which] = [out]
        return token

    _, feed_back = jax.vjp(rms_scale, own_residual, mlp_gain)
    grad_from_feed, grad_mlp_gain = feed_back(grad_feed)
    grad_residual = cotangent.astype(F32) + grad_from_feed
    grad_mixed = grad_residual.astype(BF)

    parts, sent = [], []
    for j in range(lanes):
        at = (rank ^ j) * cols
        heads_part = contract_cols(grad_mixed, lax.dynamic_slice_in_dim(w_out, at, cols, 0)).astype(BF)
        mixed_part = lax.dynamic_slice_in_dim(grad_mixed, at, cols, 1)
        sent.append(jnp.concatenate([heads_part, mixed_part], axis=1))
        parts.append(swap(sent[j], "ta", j) if j else sent[j])
    by_heads = in_order(parts, rank, 0)
    mixed_cols = by_heads[:, cols:]
    leak, grad_head_gain = mixer.leak(by_heads)
    grad_head_gain = grad_head_gain[0]
    leaks = ring.gather(leak)
    grad_q, grad_k, grad_v, tail, spill, grad_conv, grad_beta = mixer.back(leaks)
    arrived = shifted(spill.astype(BF), -1).astype(F32)
    last = ((tail + arrived) * live[None, group - PAD :, None]).astype(BF)
    grad_projected = jnp.concatenate([grad_q, grad_k, grad_v], axis=1)
    last = jnp.transpose(last, (1, 0, 2)).reshape(PAD, 3 * cols)
    grad_projected = lax.dynamic_update_slice(grad_projected, last, (group - PAD, 0))
    grad_logit = grad_beta[:, 0].T * beta * (1.0 - sig_beta)
    grad_bias = jnp.sum(grad_logit, axis=0)
    grad_logit_low = grad_logit.astype(BF)

    def weight_rows(partial, beside):
        share = partial.shape[1]
        part = ring.scatter(partial.reshape(blocks, model // blocks, share), beside)
        return exchange(part.astype(BF).reshape(lanes, rows, share), rank)

    w_partial = jnp.concatenate(
        [contract_rows(normed_group, grad_projected).astype(BF), contract_rows(heads_low, mixed_cols).astype(BF)],
        axis=1,
    )
    w_parts = weight_rows(
        w_partial, [lambda x: fill_rows([x]), lambda x: fill_rows([x]), fill_grads, fill_grads]
    )
    grad_projection = in_order([p.astype(F32).reshape(rows, 4, cols) for p in w_parts], rank, 2)

    partial_normed = contract_cols(grad_projected, w_all[:, : 3 * cols]) + contract_cols(grad_logit_low, wbeta)
    scale = lax.rsqrt(jnp.mean(group_tokens * group_tokens, axis=-1, keepdims=True) + NORM_EPS)
    grad_attn_gain = jnp.sum(partial_normed * (group_tokens * scale), axis=0)
    both_sums = jnp.stack([partial_normed.astype(BF), partial_branch]).reshape(2, lanes, width, model)
    both_sums = scatter_sum(jnp.transpose(both_sums, (1, 0, 2, 3)), rank)
    grad_normed, branch = both_sums[0], both_sums[1]
    block_out = (own_residual + branch).astype(BF)
    _, attention_back = jax.vjp(lambda x: rms_scale(x, attn_gain), tokens.astype(F32))
    grad_tokens = grad_residual + attention_back(grad_normed)[0]

    partial_wbeta = contract_rows(normed_group, grad_logit_low)
    gains = jnp.concatenate([grad_mlp_gain, grad_head_gain, grad_attn_gain])
    pieces = [grad_conv.reshape(-1), partial_wbeta.T.reshape(-1), grad_bias, gains]
    ends = [0]
    for piece in pieces:
        ends.append(ends[-1] + piece.shape[0])
    flat = jnp.concatenate(pieces)
    flat = jnp.pad(flat, (0, -flat.shape[0] % 1024)).reshape(-1, 128)
    flat = in_order(gather_parts(sum_over(flat, "dev")[None]), rank, 0).reshape(lanes, -1)
    conv_sum, wbeta_sum, bias_sum, gains = (flat[:, a:b] for a, b in zip(ends, ends[1:]))
    conv_sum = jnp.transpose(conv_sum.reshape(lanes, 3, ksize, cols), (1, 2, 0, 3))
    conv_sum = conv_sum.reshape(3, ksize, lanes * cols)
    wbeta_sum = lax.dynamic_slice_in_dim(
        wbeta_sum.reshape(heads, model), (place * lanes + rank) * rows, rows, 1
    )
    grad_w_beta = wbeta_sum.T
    bias_sum = bias_sum.reshape(heads)
    gains = jnp.sum(gains, axis=0)

    while grad_parts:
        fill_grads(w_partial)
    (grad_w_gate,), (grad_w_up,), (grad_w_down,) = ffn_grads
    return (
        block_out,
        grad_tokens,
        gains[model + depth : 2 * model + depth],
        grad_projection,
        grad_w_beta,
        bias_sum,
        conv_sum,
        gains[model : model + depth],
        gains[:model],
        grad_w_gate,
        grad_w_up,
        grad_w_down,
    )


def solution(mesh):
    rows = P(BOTH, None)
    three = P(BOTH, None, None)
    return jax.shard_map(
        body,
        mesh=mesh,
        in_specs=(
            rows,
            rows,
            P(),
            P(BOTH),
            P(),
            three,
            rows,
            P(),
            P(),
            P(),
            P(),
            P(None, "ta"),
            P(None, "ta"),
            P("ta", None),
        ),
        out_specs=(
            rows,
            rows,
            P(),
            three,
            rows,
            P(),
            P(),
            P(),
            P(),
            P(None, "ta"),
            P(None, "ta"),
            P("ta", None),
        ),
        check_vma=False,
    )
```

```python
import functools

import jax
import jax.numpy as jnp
from jax import lax
from jax.experimental import pallas as pl
from jax.experimental.pallas import tpu as pltpu
from jax.sharding import PartitionSpec as P

NORM_EPS = 1e-06
HEAD_EPS = 1e-05
UNIT_EPS = 1e-06
BOTH = ("dev", "ta")
BF = jnp.bfloat16
F32 = jnp.float32


def swap(x, axis, bit):
    return lax.ppermute(x, axis, [(i, i ^ bit) for i in range(lax.axis_size(axis))])


def gather_parts(x, *waits):
    parts = [x]
    for j in range(1, lax.axis_size("ta")):
        bit = j & -j
        if waits and j == 2 * bit + bit:
            parts[j ^ bit] = gate(parts[j ^ bit], *waits)
        parts.append(swap(parts[j ^ bit], "ta", bit))
    return parts


def gate(x, *deps):
    return pl.pallas_call(
        lambda *refs: None,
        name="gate",
        out_shape=jax.ShapeDtypeStruct(x.shape, x.dtype),
        in_specs=[pl.BlockSpec(memory_space=pl.ANY)] * (1 + len(deps)),
        out_specs=pl.BlockSpec(memory_space=pl.ANY),
        input_output_aliases={0: 0},
    )(x, *deps)


class Ring:
    def __init__(self):
        n = self.size = lax.axis_size("dev")
        self.last = n // 2
        self.order = list(range(0, n, 2)) + list(range(n - 1, 0, -2))
        self.place = lax.axis_index("dev")
        self.spot = self.spot_of(self.place)
        distances = [0] + [d for s in range(1, self.last) for d in (-s, s)] + [self.last]
        spots = lax.rem(self.spot + n + jnp.array(distances, jnp.int32), n)
        self.slots = jnp.where(2 * spots < n, 2 * spots, 2 * (n - 1 - spots) + 1)
        away = lax.rem(self.spot_of(jnp.arange(n, dtype=jnp.int32)) + n - self.spot, n)
        slot = jnp.where(away < self.last, 2 * away, 2 * (n - away) - 1)
        self.slot_of = jnp.where(away == self.last, n - 1, slot)

    def spot_of(self, index):
        return jnp.where(index % 2 == 0, index // 2, self.size - 1 - index // 2)

    def move(self, x, step):
        n = self.size
        return lax.ppermute(x, "dev", [(self.order[p], self.order[(p + step) % n]) for p in range(n)])

    def collect(self, x, waits=()):
        half = x.shape[0] // 2
        found = [x]
        onward, back = x, x
        for s in range(1, self.last):
            onward, back = self.move(onward, 1), self.move(back, -1)
            if len(waits) >= s and waits[s - 1]:
                onward, back = gate(onward, *waits[s - 1]), gate(back, *waits[s - 1])
            found += [onward, back]
        far = [self.move(onward[:half], 1), self.move(back[half:], -1)]
        return found + [jnp.concatenate(far, axis=0)]

    def scatter(self, blocks, beside=()):
        last = self.last
        beside = list(beside) + [None] * last
        block = lambda d: blocks[0 if d == 0 else 2 * d if 0 < d < last else -2 * d - 1 if d < 0 else -1]
        half = blocks[0].shape[0] // 2
        right, left = block(last)[:half], block(last)[half:]
        for s in range(last - 1, -1, -1):
            ahead, behind = self.move(right, 1), self.move(left, -1)
            deps = [beside[last - 1 - s](right)] if beside[last - 1 - s] else []
            if s:
                like = [shape(block(s).shape, BF)] * 2
                right, left = vmem_call(
                    "ring_add", ring_add_kernel, like, [block(s), block(-s), ahead, behind], 0, deps
                )
        return [block(0), ahead, behind], deps


def ring_add_kernel(first, second, ahead, behind, right, left):
    rows, part = first.shape[0], ahead.shape[0]
    for block, arrived, out, at in (
        (first, ahead, right, slice(0, part)),
        (second, behind, left, slice(rows - part, rows)),
    ):
        if part < rows:
            out[...] = block[...]
        out[at, :] = (block[at, :].astype(F32) + arrived[...].astype(F32)).astype(BF)


def sum_kernel(x, y, z, out):
    out[...] = (x[...].astype(F32) + (y[...].astype(F32) + z[...].astype(F32))).astype(BF)


def assemble_kernel(rank, *refs):
    out, parts = refs[-1], refs[:-1]
    count = out.shape[1]
    cols = parts[0].shape[1] // count
    for j, part in enumerate(parts):
        at = pl.ds(pl.multiple_of((rank[0] ^ j) * cols, cols), cols)
        for i in range(count):
            out[:, i, at] = part[:, i * cols : (i + 1) * cols].astype(F32)


def add_kernel(x, y, out):
    out[...] = x[...] + y[...]


def exchange(blocks, rank):
    parts = []
    for j in range(lax.axis_size("ta")):
        block = lax.dynamic_index_in_dim(blocks, rank ^ j, 0, False)
        parts.append(swap(block, "ta", j) if j else block)
    return parts


def sum_over(x, axis, waits):
    size = lax.axis_size(axis)
    bit, n = 1, 0
    while bit < size:
        (x,) = vmem_call("add", add_kernel, [shape(x.shape)], [x, swap(x, axis, bit)], 0, waits[n : n + 1])
        bit, n = 2 * bit, n + 1
    return x


def scatter_sum(kept, sent, rank, beside=None):
    lanes = lax.axis_size("ta")
    made = None
    bit = 1
    while True:
        arrived = swap(sent, "ta", bit)
        bit *= 2
        if bit == lanes:
            if beside:
                made = beside(sent)
                arrived = gate(arrived, made[0])
            return kept[0], arrived[0], made
        blocks = kept.astype(F32) + arrived.astype(F32)
        pairs = blocks.reshape((blocks.shape[0] // 2, 2) + blocks.shape[1:])
        mine = (rank // bit) % 2
        kept = lax.dynamic_index_in_dim(pairs, mine, 1, False)
        sent = lax.dynamic_index_in_dim(pairs, 1 - mine, 1, False).astype(BF)


def rms_scale(values, gain):
    return values * lax.rsqrt(jnp.mean(values * values, axis=-1, keepdims=True) + NORM_EPS) * gain


def document_of(lengths, positions):
    starts = jnp.cumsum(lengths) - lengths
    above = (starts[None, :] <= positions[:, None]).astype(jnp.int32)
    return jnp.sum(above, axis=1) - 1


def contract_rows(left, right):
    return lax.dot_general(left, right, (((0,), (0,)), ((), ())), preferred_element_type=F32)


def contract_cols(left, right):
    return lax.dot_general(left, right, (((1,), (1,)), ((), ())), preferred_element_type=F32)


def dot(left, right):
    return jnp.dot(left, right, preferred_element_type=F32)


PAD = 8
VMEM_LIMIT = 48 * 1024 * 1024
FFN_VMEM = 56 * 1024 * 1024


def dims(a, b, ca, cb):
    return lax.dot_general(a, b, (((ca,), (cb,)), ((), ())), preferred_element_type=F32)


def d1(a, b, ca=1, cb=0):
    return dims(a.astype(BF), b.astype(BF), ca, cb)


def parts_of(a):
    high = a.astype(BF)
    return high, (a - high.astype(F32)).astype(BF)


def d3(a, b, ca=1, cb=0):
    ah, al = parts_of(a)
    bh, bl = parts_of(b)
    return dims(ah, bh, ca, cb) + (dims(ah, bl, ca, cb) + dims(al, bh, ca, cb))


def iotas(size):
    return (
        lax.broadcasted_iota(jnp.int32, (size, size), 0),
        lax.broadcasted_iota(jnp.int32, (size, size), 1),
    )


def inverses_of(lowers):
    size = lowers[0].shape[0]
    row, col = iotas(size)
    eye = (row == col).astype(F32)
    pair = (row // 2 == col // 2).astype(F32)
    found = [eye - low * pair for low in lowers]
    block = 2
    while block < size:
        joint = ((row // (2 * block) == col // (2 * block)) & (row // block != col // block)).astype(F32)
        steps = [d1(low * joint, x) for low, x in zip(lowers, found)]
        found = [x - d1(x, s) for x, s in zip(found, steps)]
        block *= 2
    errors = [d3(low, x) + (x - eye) for low, x in zip(lowers, found)]
    return [x - d1(x, e) for x, e in zip(found, errors)]


def unit_of(active):
    scale = lax.rsqrt(jnp.sum(active * active, axis=-1, keepdims=True) + UNIT_EPS)
    return active * scale, scale


def masks_of(aux, row, at, size):
    doc, doc_row = aux[at, 6:7], row[6:7, at]
    r, c = iotas(size)
    same = doc == doc_row
    weak = (same & (r >= c)).astype(F32)
    strict = (same & (r > c)).astype(F32)
    return weak, strict


def forward_kernel(size, xq, xk, xv, conv, aux_ref, row_ref, yq, yk, yv, inv, plain, reach, read, direct, trans, fresh, whole):
    count = inv.shape[1]
    depth = xq.shape[1]
    ksize = conv.shape[1]
    aux, row = aux_ref.at[0], row_ref.at[0]
    r, c = iotas(depth)
    eye = (r == c).astype(F32)
    spans = [slice(n * size, (n + 1) * size) for n in range(count)]
    saved = []
    lowers = []
    for n, at in enumerate(spans):
        active = []
        for i, (x, y) in enumerate(((xq, yq), (xk, yk), (xv, yv))):
            first = PAD - (ksize - 1) + n * size
            summed = x[first + ksize - 1 : first + ksize - 1 + size, :] * conv[i, ksize - 1 : ksize, :]
            for j in range(ksize - 1):
                summed = summed + x[first + j : first + j + size, :] * conv[i, j : j + 1, :] * aux[at, j : j + 1]
            y[at, :] = summed
            active.append(summed * jax.nn.sigmoid(summed))
        q = unit_of(active[0])[0] * depth ** (-0.5)
        k = unit_of(active[1])[0]
        weak, strict = masks_of(aux, row, at, size)
        rate = row[7:8, at]
        products = d3(jnp.concatenate([q, k], axis=0), k, 1, 1)
        lowers.append(products[size:] * rate * strict)
        saved.append((q, k, active[2], products[:size] * rate * weak))
    inverses = inverses_of(lowers)
    total = added = None
    for n, at in enumerate(spans):
        q, k, v, mix = saved[n]
        cont, clos, beta = aux[at, 3:4], aux[at, 4:5], aux[at, 7:8]
        both = d3(inverses[n], jnp.concatenate([v, k * cont], axis=1))
        spread = d1(mix, both)
        inv[0, n] = inverses[n]
        plain[0, at, :] = both[:, :depth]
        reach[0, at, :] = both[:, depth:]
        direct[0, at, :] = spread[:, :depth]
        read[0, at, :] = q * cont - spread[:, depth:]
        gained = d3(k * (beta * clos), both, 0, 0)
        map_n = aux[(n + 1) * size - 1 : (n + 1) * size, 3:4] * eye - gained[:, depth:]
        add_n = gained[:, :depth]
        trans[0, n] = map_n
        fresh[0, n] = add_n
        if n == 0:
            total, added = map_n, add_n
        else:
            new = d3(map_n, jnp.concatenate([added, total], axis=1))
            total, added = new[:, depth:], new[:, :depth] + add_n
    whole[0, 0] = total.astype(BF)
    whole[0, 1] = added.astype(BF)


def read_kernel(size, count_of, index, *refs):
    parts, refs = refs[:count_of], refs[count_of:]
    trans, fresh, read, direct, gain, both, states, outputs, normed = refs
    heads, count = trans.shape[0], trans.shape[1]
    depth = trans.shape[-1]
    for n, part in enumerate(parts):
        both[index[1 + n]] = part[...]

    def earlier(i, carry):
        return tuple(
            d3(both[i, h, 0].astype(F32), carry[h]) + both[i, h, 1].astype(F32) for h in range(heads)
        )

    carry = lax.fori_loop(0, index[0], earlier, tuple(jnp.zeros((depth, depth), F32) for _ in range(heads)))
    carry = list(carry)
    for n in range(count):
        at = slice(n * size, (n + 1) * size)
        for h in range(heads):
            state = carry[h]
            states[h, n] = state
            out = direct[h, at, :] + d3(read[h, at, :], state)
            cols = slice(h * depth, (h + 1) * depth)
            outputs[at, cols] = out
            scale = lax.rsqrt(jnp.mean(out * out, axis=-1, keepdims=True) + HEAD_EPS)
            normed[at, cols] = (out * scale * gain[...]).astype(BF)
            if n < count - 1:
                carry[h] = d3(trans[h, n], state) + fresh[h, n]


def leak_kernel(size, lanes, rank, *refs):
    parts, refs = refs[:lanes], refs[lanes:]
    outputs, gain, read, trans, grad_out, from_out, leak, grad_gain, mixed, grads = refs
    heads, count = trans.shape[0], trans.shape[1]
    depth = trans.shape[-1]
    for j, part in enumerate(parts):
        at = pl.ds(pl.multiple_of((rank[0] ^ j) * size, size), size)
        grads[at, :] = part[:, : heads * depth]
        mixed[at, :] = part[:, heads * depth :]
    gained = jnp.zeros((1, depth), F32)
    totals = [None] * heads
    for n in range(count - 1, -1, -1):
        at = slice(n * size, (n + 1) * size)
        for h in range(heads):
            cols = slice(h * depth, (h + 1) * depth)
            out, grad = outputs[at, cols], grads[at, cols].astype(F32)
            scale = lax.rsqrt(jnp.mean(out * out, axis=-1, keepdims=True) + HEAD_EPS)
            unit = out * scale
            gained = gained + jnp.sum(grad * unit, axis=0, keepdims=True)
            grad = grad * gain[...]
            grad = scale * (grad - unit * jnp.mean(grad * unit, axis=-1, keepdims=True))
            grad_out[h, at, :] = grad
            term = d3(read[h, at, :], grad, 0, 0)
            from_out[h, n] = term
            totals[h] = term if n == count - 1 else d3(trans[h, n], totals[h], 0, 0) + term
    for h in range(heads):
        leak[h] = totals[h].astype(BF)
    grad_gain[...] = gained


def chain_kernel(index, *refs):
    both, trans, from_out, grads = refs[-4:]
    leaks = refs[:-4]
    heads, count = trans.shape[0], trans.shape[1]
    depth = trans.shape[-1]
    devices = both.shape[0]
    carry = [jnp.zeros((depth, depth), F32) for _ in range(heads)]
    for k in range(devices - 1, 0, -1):
        at = jnp.minimum(index[0] + k, devices - 1)
        carry = [
            d3(both[at, h, 0].astype(F32), carry[h], 0, 0) + leaks[k - 1][h].astype(F32) for h in range(heads)
        ]
    for n in range(count - 1, -1, -1):
        for h in range(heads):
            grads[h, n] = carry[h]
            if n:
                carry[h] = d3(trans[h, n], carry[h], 0, 0) + from_out[h, n]


def backward_kernel(size, xq, xk, xv, yq, yk, yv, conv, aux_ref, row_ref, inv, plain, reach, states, grads, grad_out,
                    gq, gk, gv, tail, spill, grad_conv, grad_beta, zs):
    count = inv.shape[1]
    depth = xq.shape[1]
    ksize = conv.shape[1]
    aux, row = aux_ref.at[0], row_ref.at[0]
    length = count * size
    scale_q = depth ** (-0.5)
    for n in range(count):
        at = slice(n * size, (n + 1) * size)
        cont, clos, beta = aux[at, 3:4], aux[at, 4:5], aux[at, 7:8]
        weak, strict = masks_of(aux, row, at, size)
        rate = row[7:8, at]
        ys = [yq[at, :], yk[at, :], yv[at, :]]
        sigs = [jax.nn.sigmoid(y) for y in ys]
        uq, rq = unit_of(ys[0] * sigs[0])
        k, rk = unit_of(ys[1] * sigs[1])
        q = uq * scale_q
        products = d1(jnp.concatenate([q, k], axis=0), k, 1, 1)
        qk, kk = products[:size], products[size:]
        mix = qk * rate * weak
        state, grad_state, dout = states[0, n], grads[0, n], grad_out[0, at, :]
        u = plain[0, at, :] - d1(reach[0, at, :], state)
        kds = d1(k, grad_state)
        written = beta * clos
        du = d1(mix, dout, 0, 0) + written * kds
        dr = d1(inv[0, n], du, 0, 0)
        pair = jnp.concatenate([dout, dr], axis=0)
        outer = d1(pair, u, 1, 1)
        through = d1(pair, state, 1, 1)
        dp = outer[:size] * weak
        dl = -outer[size:] * strict
        per_key = jnp.sum(dp * qk + dl * kk, axis=0, keepdims=True)
        per_state = jnp.sum((kds * u).T, axis=0, keepdims=True)
        grad_beta[0, :, at] = per_key + row[4:5, at] * per_state
        dqk = dp * rate
        da = dl * rate
        dq = cont * through[:size] + d1(dqk, k)
        dk = d1(dqk, q, 0, 0) + written * d1(u, grad_state, 1, 1) - cont * through[size:] + d1(da + da.T, k)
        dq = dq * scale_q
        acts = [
            rq * (dq - uq * jnp.sum(uq * dq, axis=-1, keepdims=True)),
            rk * (dk - k * jnp.sum(k * dk, axis=-1, keepdims=True)),
            dr,
        ]
        for i, x in enumerate((xq, xk, xv)):
            dy = acts[i] * sigs[i] * (1.0 + ys[i] * (1.0 - sigs[i]))
            first = PAD - (ksize - 1) + n * size
            for j in range(ksize):
                dv = dy if j == ksize - 1 else dy * aux[at, j : j + 1]
                term = jnp.sum(dv * x[first + j : first + j + size, :], axis=0, keepdims=True)
                before = jnp.zeros_like(term) if n == 0 else grad_conv[i, j : j + 1, :]
                grad_conv[i, j : j + 1, :] = before + term
                zs[i, j, PAD + n * size : PAD + (n + 1) * size, :] = dv * conv[i, j : j + 1, :]
    for i, g in enumerate((gq, gk, gv)):
        for j in range(ksize):
            zs[i, j, 0:PAD, :] = jnp.zeros((PAD, depth), F32)
            zs[i, j, PAD + length : 2 * PAD + length, :] = jnp.zeros((PAD, depth), F32)

        def shifted_sum(first, rows):
            return sum(zs[i, j, first + ksize - 1 - j : first + ksize - 1 - j + rows, :] for j in range(ksize))

        for n in range(count):
            at = slice(n * size, (n + 1) * size)
            g[at, :] = (shifted_sum(PAD + n * size, size) * aux[at, 5:6]).astype(BF)
        tail[i] = shifted_sum(length, PAD)
        spill[i] = shifted_sum(0, PAD)


def vmem_call(name, kernel, out_shape, inputs, flops, deps=(), scratch=()):
    smem, vmem = (pl.BlockSpec(memory_space=m) for m in (pltpu.SMEM, pltpu.VMEM))

    def run(*refs):
        kernel(*refs[: len(inputs)], *refs[len(inputs) + len(deps) :])

    return pl.pallas_call(
        run,
        name=name,
        out_shape=out_shape,
        in_specs=[smem if x.dtype == jnp.int32 else vmem for x in inputs]
        + [pl.BlockSpec(memory_space=pl.ANY)] * len(deps),
        out_specs=[vmem] * len(out_shape),
        scratch_shapes=list(scratch),
        cost_estimate=cost(flops, inputs, out_shape),
        compiler_params=pltpu.CompilerParams(vmem_limit_bytes=FFN_VMEM),
    )(*inputs, *deps)


def cost(flops, inputs, outputs):
    moved = sum(x.size * x.dtype.itemsize for x in list(inputs) + list(outputs))
    return pl.CostEstimate(flops=int(flops), bytes_accessed=int(moved), transcendentals=0)


def shape(dims, dtype=F32):
    return jax.ShapeDtypeStruct(dims, dtype)


class Mixer:
    def __init__(self, projected, own_conv, aux, row, size):
        self.size = size
        self.heads, self.length = aux.shape[0], aux.shape[1]
        self.depth = own_conv.shape[2] // self.heads
        self.count = self.length // size
        self.projected, self.conv, self.aux, self.row = projected, own_conv, aux, row
        heads, length, depth, count = self.heads, self.length, self.depth, self.count
        ksize = own_conv.shape[1]
        self.token_specs = [
            pl.BlockSpec((length + PAD, depth), lambda h, i=i: (0, i * heads + h)) for i in range(3)
        ]
        self.head_cols = pl.BlockSpec((length, depth), lambda h: (0, h))
        self.conv_spec = pl.BlockSpec((3, ksize, depth), lambda h: (0, 0, h))
        self.aux_specs = [
            pl.BlockSpec((1, length, 8), lambda h: (h, 0, 0)),
            pl.BlockSpec((1, 8, length), lambda h: (h, 0, 0)),
        ]
        self.chunk_spec = pl.BlockSpec((1, count, depth, depth), lambda h: (h, 0, 0, 0))
        self.inv_spec = pl.BlockSpec((1, count, size, size), lambda h: (h, 0, 0, 0))
        self.rows_spec = pl.BlockSpec((1, length, depth), lambda h: (h, 0, 0))
        self.flops = 2 * heads * count * size * depth * depth
        inputs = [projected] * 3 + [own_conv, aux, row]
        square = shape((heads, count, depth, depth))
        tokens = shape((heads, length, depth))
        out_shape = (
            [shape((length, heads * depth))] * 3
            + [shape((heads, count, size, size))]
            + [tokens] * 4
            + [square] * 2
            + [shape((heads, 2, depth, depth), BF)]
        )
        (
            self.yq, self.yk, self.yv, self.inv, self.plain, self.reach, self.read, self.direct,
            self.trans, self.fresh, self.whole,
        ) = pl.pallas_call(
            functools.partial(forward_kernel, size),
            name="mixer_forward",
            out_shape=out_shape,
            grid=(heads,),
            in_specs=self.token_specs + [self.conv_spec] + self.aux_specs,
            out_specs=[self.head_cols] * 3
            + [self.inv_spec]
            + [self.rows_spec] * 4
            + [self.chunk_spec] * 2
            + [pl.BlockSpec((1, 2, depth, depth), lambda h: (h, 0, 0, 0))],
            cost_estimate=cost(60 * self.flops, inputs, out_shape),
            compiler_params=pltpu.CompilerParams(vmem_limit_bytes=VMEM_LIMIT),
        )(*inputs)

    def outputs(self, index, parts, head_gain):
        heads, length, depth, count = self.heads, self.length, self.depth, self.count
        self.index, self.gain = index, head_gain
        self.both, self.states, self.out, normed = vmem_call(
            "mixer_read",
            functools.partial(read_kernel, self.size, len(parts)),
            [
                shape((len(parts),) + parts[0].shape, BF),
                shape((heads, count, depth, depth)),
                shape((length, heads * depth)),
                shape((length, heads * depth), BF),
            ],
            [index, *parts, self.trans, self.fresh, self.read, self.direct, head_gain],
            12 * self.flops,
        )
        return normed

    def leak(self, rank, parts, deps=()):
        heads, length, depth, count = self.heads, self.length, self.depth, self.count
        self.grad_out, self.from_out, leak, grad_gain, mixed = vmem_call(
            "mixer_leak",
            functools.partial(leak_kernel, self.size, len(parts)),
            [
                shape((heads, length, depth)),
                shape((heads, count, depth, depth)),
                shape((heads, depth, depth), BF),
                shape((1, depth)),
                shape((length, heads * depth), BF),
            ],
            [rank, *parts, self.out, self.gain, self.read, self.trans],
            6 * self.flops,
            deps,
            scratch=[pltpu.VMEM((length, heads * depth), BF)],
        )
        return leak, grad_gain, mixed

    def back(self, leaks, deps=()):
        heads, length, depth, count = self.heads, self.length, self.depth, self.count
        ksize = self.conv.shape[1]
        (grads,) = vmem_call(
            "mixer_chain",
            chain_kernel,
            [shape((heads, count, depth, depth))],
            [self.index, *leaks, self.both, self.trans, self.from_out],
            6 * self.flops,
            deps,
        )
        inputs = [self.projected] * 3 + [self.yq, self.yk, self.yv, self.conv, self.aux, self.row]
        inputs += [self.inv, self.plain, self.reach, self.states, grads, self.grad_out]
        edge = shape((3, PAD, heads * depth))
        out_shape = [shape((length, heads * depth), BF)] * 3 + [edge] * 2
        out_shape += [shape((3, ksize, heads * depth)), shape((heads, 1, length))]
        edge_spec = pl.BlockSpec((3, PAD, depth), lambda h: (0, 0, h))
        return pl.pallas_call(
            functools.partial(backward_kernel, self.size),
            name="mixer_backward",
            out_shape=out_shape,
            grid=(heads,),
            in_specs=self.token_specs
            + [self.head_cols] * 3
            + [self.conv_spec]
            + self.aux_specs
            + [self.inv_spec, self.rows_spec, self.rows_spec, self.chunk_spec, self.chunk_spec, self.rows_spec],
            out_specs=[self.head_cols] * 3
            + [edge_spec] * 2
            + [self.conv_spec, pl.BlockSpec((1, 1, length), lambda h: (h, 0, 0))],
            scratch_shapes=[pltpu.VMEM((3, ksize, length + 2 * PAD, depth), F32)],
            cost_estimate=cost(30 * self.flops, inputs, out_shape),
            compiler_params=pltpu.CompilerParams(vmem_limit_bytes=VMEM_LIMIT),
        )(*inputs)


ANY = pl.BlockSpec(memory_space=pl.ANY)
TOKEN = shape((8, 128))


def resident(x):
    return pl.BlockSpec(x.shape, lambda *_: (0,) * x.ndim, pipeline_mode=pl.Buffered(1))


def activations(gate, lifted, grad_hidden):
    sig = jax.nn.sigmoid(gate)
    swish = gate * sig
    return (
        (swish * lifted).astype(BF),
        (grad_hidden * lifted * sig * (1.0 + gate * (1.0 - sig))).astype(BF),
        (grad_hidden * swish).astype(BF),
    )


def chunks_of(size, chunk=256):
    return [slice(at, min(at + chunk, size)) for at in range(0, size, chunk)]


def params(flops, moved):
    return dict(
        cost_estimate=pl.CostEstimate(flops=int(flops), bytes_accessed=int(moved), transcendentals=0),
        compiler_params=pltpu.CompilerParams(vmem_limit_bytes=FFN_VMEM),
    )


TOKEN_SPEC = pl.BlockSpec((8, 128), lambda *_: (0, 0))


def split_by_core(source, core, width, kept, sent):
    for p in range(kept.shape[0]):
        for ref, which in ((kept, core), (sent, 1 - core)):
            ref[p] = source[pl.ds(pl.multiple_of((2 * p + which) * width, width), width), :]


def own_kernel(index, feed, cot, wg, wu, wd, hidden, grad_gate, grad_lifted, kept, sent, branch, total):
    units, model = wd.shape
    for cut in chunks_of(units):
        gated = jnp.dot(feed[...], wg[:, cut], preferred_element_type=F32)
        lifted = jnp.dot(feed[...], wu[:, cut], preferred_element_type=F32)
        grad_hidden = dims(cot[...], wd[cut, :], 1, 1)
        hidden[:, cut], grad_gate[:, cut], grad_lifted[:, cut] = activations(gated, lifted, grad_hidden)
    for cut in chunks_of(model):
        grad_feed = dims(grad_gate[...], wg[cut, :], 1, 1) + dims(grad_lifted[...], wu[cut, :], 1, 1)
        total[:, cut] = grad_feed.astype(BF)
        branch[:, cut] = jnp.dot(hidden[...], wd[:, cut], preferred_element_type=F32).astype(BF)
    split_by_core(total, index[1], kept.shape[1], kept, sent)


def hidden_kernel(groups, cot, wd, *refs):
    out, token = refs[-2:]
    out[...] = dims(cot[...], wd[...], 1, 1).astype(BF)
    token[...] = jnp.zeros_like(token)


def rows_kernel(groups, feed, grad_hidden, wg, wu, *refs):
    *outs, token = refs[-4:]
    before = grad_hidden[...].reshape(feed.shape[0], -1)
    for cut in chunks_of(wg.shape[1]):
        gated = jnp.dot(feed[...], wg[:, cut], preferred_element_type=F32)
        lifted = jnp.dot(feed[...], wu[:, cut], preferred_element_type=F32)
        for out, value in zip(outs, activations(gated, lifted, before[:, cut].astype(F32))):
            out[:, :, :, cut] = value.reshape(out.shape[:-1] + (value.shape[-1],))
    token[...] = jnp.zeros_like(token)


def by_group(name, kernel, groups, size, inputs, weights, outs, held, deps, products, half=0):
    like = inputs[-1].shape
    count = groups.shape[0]

    def picked(x, width):
        if x.ndim == 2:
            return pl.BlockSpec((size, width), lambda i, g: (g[i], 0))
        return pl.BlockSpec((size // like[2], 1, like[2], width), lambda i, g: (g[i], half, 0, 0))

    first = 1 + len(inputs) + len(weights) + len(deps)
    return pl.pallas_call(
        kernel,
        name=name,
        out_shape=[shape(like[:-1] + (width,), BF) for width in outs] + [TOKEN],
        grid_spec=pltpu.PrefetchScalarGridSpec(
            num_scalar_prefetch=1,
            grid=(count,),
            in_specs=[picked(x, x.shape[-1]) for x in inputs]
            + [resident(w) for w in weights]
            + [ANY] * (len(deps) + len(held)),
            out_specs=[picked(inputs[-1], width) for width in outs] + [TOKEN_SPEC],
        ),
        input_output_aliases={first + n: n for n in range(len(held))},
        **params(
            2 * count * size * weights[0].size * products,
            sum(w.size for w in weights) * 2 + count * size * 2 * (sum(outs) + sum(x.shape[-1] for x in inputs)),
        ),
    )(groups, *inputs, *weights, *deps, *held)


def feed_own(index, feed, cot, weights, tokens, width):
    rows, model = feed.shape
    units = weights[0].shape[1]
    block = 2 * width
    count = rows // block
    wide = pl.BlockSpec((block, units), lambda i, g: (g[0] * count + i, 0))
    here = pl.BlockSpec((block, model), lambda i, g: (i, 0))
    half = pl.BlockSpec((1, width, model), lambda i, g: (i, 0, 0))
    return pl.pallas_call(
        own_kernel,
        name="feed_own",
        out_shape=[shape((tokens, units), BF)] * 3
        + [shape((count, width, model), BF)] * 2
        + [shape((rows, model), BF)],
        grid_spec=pltpu.PrefetchScalarGridSpec(
            num_scalar_prefetch=1,
            grid=(count,),
            in_specs=[here] * 2 + [resident(w) for w in weights],
            out_specs=[wide] * 3 + [half] * 2 + [here],
            scratch_shapes=[pltpu.VMEM((block, model), BF)],
        ),
        **params(12 * rows * model * units, 6 * model * units + rows * (3 * units + 4 * model) * 2),
    )(index, feed, cot, *weights)


GRAD_COLS = 256


def grad_kernel(transposed, count, *refs):
    lefts, right = refs[:count], refs[count]
    out, token = refs[-2:]
    units = right.shape[-1]
    if count == 1:
        term = dims(lefts[0][...], right[...].reshape(-1, units), 0, 0)
    else:
        term = sum(dims(left[...], right[:, n].reshape(-1, units), 0, 0) for n, left in enumerate(lefts))
    out[...] = term.T if transposed else term
    token[...] = jnp.zeros_like(token)


def weight_grad(part, parts, lefts, right, held, deps, transposed):
    rows, model = lefts[0].shape
    units = right.shape[-1]
    count = model // GRAD_COLS // parts
    if transposed:
        out_spec = pl.BlockSpec((units, GRAD_COLS), lambda m: (0, part * count + m))
    else:
        out_spec = pl.BlockSpec((GRAD_COLS, units), lambda m: (part * count + m, 0))
    first = len(lefts) + 1 + len(deps)
    tokens = rows * len(lefts)
    return pl.pallas_call(
        functools.partial(grad_kernel, transposed, len(lefts)),
        name="weight_grad",
        out_shape=[shape((units, model) if transposed else (model, units)), TOKEN],
        grid=(count,),
        in_specs=[pl.BlockSpec((rows, GRAD_COLS), lambda m: (0, part * count + m))] * len(lefts)
        + [resident(right)]
        + [ANY] * (len(deps) + len(held)),
        out_specs=[out_spec, TOKEN_SPEC],
        input_output_aliases={first + n: n for n in range(len(held))},
        **params(
            2 * tokens * count * GRAD_COLS * units,
            2 * tokens * (units + count * GRAD_COLS) + 4 * count * GRAD_COLS * units,
        ),
    )(*lefts, right, *deps, *held)


def order_kernel(rank, *refs):
    out = refs[-1]
    size = refs[0].shape[0]
    for j, part in enumerate(refs[:-1]):
        out[pl.ds(pl.multiple_of((rank[0] ^ j) * size, size), size), :] = part[...]


def in_order(parts, rank):
    rows, width = parts[0].shape
    return vmem_call(
        "in_order", order_kernel, [shape((rows * len(parts), width), parts[0].dtype)], [rank, *parts], 0
    )[0]


def norm_kernel(width, rank, *refs):
    gain, group, normed, extended, live = refs[-5:]
    parts = refs[:-5]

    def scaled(values):
        values = values.astype(F32)
        scale = lax.rsqrt(jnp.mean(values * values, axis=-1, keepdims=True) + NORM_EPS)
        return (values * scale * gain[...]).astype(BF)

    for j, part in enumerate(parts):
        at = rank[0] ^ j
        rows = part[0:width, :]
        group[pl.ds(pl.multiple_of(at * width, width), width), :] = rows
        rows = scaled(rows)
        normed[pl.ds(pl.multiple_of(at * width, width), width), :] = rows
        extended[pl.ds(pl.multiple_of(PAD + at * width, PAD), width), :] = rows
        live[at] = part[width : width + 8, 0 : 2 * width]

        @pl.when(at == 0)
        def _():
            extended[0:PAD, :] = scaled(part[width + 8 : width + 8 + PAD, :])


def weights_kernel(lanes, rank, *refs):
    out, parts = refs[-1], refs[:-1]
    rows = out.shape[0] - parts[0].shape[0]
    rows = rows // (lanes - 1)
    heads = parts[0].shape[0] - rows
    mine = lax.broadcasted_iota(jnp.int32, (heads, 128), 0) // (heads // lanes)
    tile = jnp.zeros((heads, 128), F32)
    for j, part in enumerate(parts):
        at = rank[0] ^ j
        out[pl.ds(pl.multiple_of(at * rows, rows), rows), :] = part[0:rows, :]
        tile = jnp.where(mine == at, part[rows:, 0:128].astype(F32), tile)
    out[lanes * rows :, :] = jnp.zeros((heads, out.shape[1]), BF)
    out[lanes * rows :, 0:128] = tile.astype(BF)


def project_kernel(lanes, slots, x, live, *refs):
    out, out_w, logit, wbeta = refs[-4:]
    parts, last = refs[: len(refs) // 2 - 2], refs[len(refs) // 2 - 2 : -4]
    size = out_w.shape[0] // len(parts)
    heads = parts[0].shape[0] - size
    own = heads // lanes
    total = None
    for n, part in enumerate(parts):
        at = pl.ds(pl.multiple_of(slots[n] * size, size), size)
        term = jnp.dot(x[:, at], part[0:size, :], preferred_element_type=F32)
        total = term if total is None else total + term
    out[...] = total * live[...]

    @pl.when(pl.program_id(0) == 0)
    def _():
        each = size // lanes
        row = lax.broadcasted_iota(jnp.int32, (heads, size), 0)
        col = lax.broadcasted_iota(jnp.int32, (heads, size), 1)
        own_row = lax.broadcasted_iota(jnp.int32, (8, heads), 0)
        own_col = lax.broadcasted_iota(jnp.int32, (8, heads), 1)
        picked = ((own_col % own == own_row) & (own_row < own)).astype(BF)
        for n, (part, columns) in enumerate(zip(parts, last)):
            out_w[n * size : (n + 1) * size, :] = columns[0:size, :]
            tile = jnp.concatenate([part[size:, 0:each]] * lanes, axis=1)
            tile = jnp.where(col // each == row // own, tile.astype(F32), 0.0).astype(BF)
            at = pl.ds(pl.multiple_of(slots[n] * size, size), size)
            wbeta[:, at] = jnp.dot(picked, tile, preferred_element_type=F32).astype(BF)
        logit[...] = dims(x[...], wbeta[...], 1, 1)


def project(slots, x, live, parts, lanes):
    rows, model = x.shape
    size, width = parts[0].shape
    cols = width // 4
    whole = lambda a: pl.BlockSpec(a.shape, lambda i, s: (0,) * len(a.shape))
    outs = [shape((rows, 3 * cols)), shape((model, cols), BF), shape((rows, 8)), shape((8, model), BF)]
    return pl.pallas_call(
        functools.partial(project_kernel, lanes),
        name="project",
        out_shape=outs,
        grid_spec=pltpu.PrefetchScalarGridSpec(
            num_scalar_prefetch=1,
            grid=(3,),
            in_specs=[whole(x), whole(live)]
            + [pl.BlockSpec((size, cols), lambda i, s: (0, i))] * len(parts)
            + [pl.BlockSpec((size, cols), lambda i, s: (0, 3))] * len(parts),
            out_specs=[pl.BlockSpec((rows, cols), lambda i, s: (0, i))] + [whole(a) for a in outs[1:]],
        ),
        **params(6 * rows * model * cols, 2 * x.size + 8 * model * cols),
    )(slots, x, live, *parts, *parts)


def out_kernel(lanes, index, *refs):
    heads, w, refs = refs[:lanes], refs[lanes : 2 * lanes], refs[2 * lanes :]
    tokens, gain, feed, *own_feed, own_residual, total = refs
    rank = index[0]
    width = own_residual.shape[0]
    cols = heads[0].shape[1]
    blocks = w[0].shape[0]
    size = w[0].shape[0] // (index.shape[0] - 1)
    per = cols // size
    for j in range(lanes):
        acc = None
        for i in range(lanes):
            for p in range(per):
                slot = index[1 + (rank ^ i) * per + p]
                rows = w[j][pl.ds(pl.multiple_of(slot * size, size), size), :]
                term = jnp.dot(heads[i][:, p * size : (p + 1) * size], rows, preferred_element_type=F32)
                acc = term if acc is None else acc + term
        at = pl.ds(pl.multiple_of((rank ^ j) * cols, cols), cols)
        total[:, at] = tokens[:, at].astype(F32) + acc
    for n in range(lanes):
        at = slice(n * width, (n + 1) * width)
        values = total[at, :]
        scale = lax.rsqrt(jnp.mean(values * values, axis=-1, keepdims=True) + NORM_EPS)
        feed[at, :] = (values * scale * gain[...]).astype(BF)
    own = pl.ds(pl.multiple_of(rank * width, width), width)
    own_residual[...] = total[own, :]
    for n, out in enumerate(own_feed):
        out[...] = feed[pl.ds(pl.multiple_of(rank * width + n * (width // 2), width // 2), width // 2), :]


def residual_kernel(lanes, index, *refs):
    w, refs = refs[:lanes], refs[lanes:]
    kept, arrived, residual, cot, gain, grad_residual, grad_gain = refs[:7]
    sent, mixed = refs[7 : 7 + lanes], refs[7 + lanes]
    rank = index[0]
    cols = w[0].shape[1]
    size = w[0].shape[0] // (index.shape[0] - 1)
    per = cols // size
    grad = kept[...].astype(F32) + arrived[...].astype(F32)
    values = residual[...]
    scale = lax.rsqrt(jnp.mean(values * values, axis=-1, keepdims=True) + NORM_EPS)
    unit = values * scale
    grad_gain[...] = jnp.sum(grad * unit, axis=0, keepdims=True)
    grad = grad * gain[...]
    grad = cot[...].astype(F32) + scale * (grad - unit * jnp.mean(grad * unit, axis=-1, keepdims=True))
    grad_residual[...] = grad
    mixed[...] = grad.astype(BF)
    columns = [pl.ds(pl.multiple_of((rank ^ j) * cols, cols), cols) for j in range(lanes)]
    for j in range(lanes):
        for p in range(per):
            slot = index[1 + (rank ^ j) * per + p]
            acc = None
            for i in range(lanes):
                rows = w[i][pl.ds(pl.multiple_of(slot * size, size), size), :]
                term = dims(mixed[:, columns[i]], rows, 1, 1)
                acc = term if acc is None else acc + term
            sent[j][:, p * size : (p + 1) * size] = acc.astype(BF)
        sent[j][:, cols:] = mixed[:, columns[j]]


def normed_back_kernel(blocks, index, *refs):
    w, refs = refs[:blocks], refs[blocks:]
    gq, gk, gv, tail, arrived, live, logit, wbeta, tokens, grads, kept, sent, gain, total = refs
    size = total.shape[1] // blocks
    cols = gq.shape[1]
    length = gq.shape[0]
    for i, g in enumerate((gq, gk, gv)):
        at = slice(i * cols, (i + 1) * cols)
        grads[:, at] = g[...]
        last = ((tail[i] + arrived[i].astype(F32)) * live[...]).astype(BF)
        grads[length - 16 :, at] = jnp.concatenate([g[length - 16 : length - PAD, :], last], axis=0)
    values = tokens[...].astype(F32)
    scale = lax.rsqrt(jnp.mean(values * values, axis=-1, keepdims=True) + NORM_EPS)
    for n in range(blocks):
        at = pl.ds(pl.multiple_of(index[1 + n] * size, size), size)
        part = dims(grads[...], w[n][0:size, : 3 * cols], 1, 1) + jnp.dot(
            logit[...], wbeta[:, at], preferred_element_type=F32
        )
        gain[:, at] = jnp.sum(part * (tokens[:, at].astype(F32) * scale), axis=0, keepdims=True)
        total[:, at] = part.astype(BF)
    split_by_core(total, index[0], kept.shape[1], kept, sent)


def weight_rows_kernel(lanes, index, *refs):
    heads, refs = refs[:lanes], refs[lanes:]
    normed, grads, mixed, logit = refs[:4]
    *outs, wbeta, joined = refs[4:]
    cols = mixed.shape[1]
    wide = grads.shape[1]
    size = outs[0].shape[0]
    rank = index[0]
    for j, part in enumerate(heads):
        joined[:, pl.ds(pl.multiple_of((rank ^ j) * cols, cols), cols)] = part[...]
    for n, out in enumerate(outs):
        at = pl.ds(pl.multiple_of(index[1 + n] * size, size), size)
        out[:, :wide] = dims(normed[:, at], grads[...], 0, 0).astype(BF)
        out[:, wide:] = dims(joined[:, at], mixed[...], 0, 0).astype(BF)
    wbeta[...] = dims(logit[...], normed[...], 0, 0)


def body(
    tokens,
    cotangent,
    lengths,
    pad_mask,
    attn_gain,
    projection_weight,
    w_beta,
    beta_bias,
    conv_weight,
    head_gain,
    mlp_gain,
    w_gate,
    w_up,
    w_down,
):
    width, model = tokens.shape
    heads = w_beta.shape[1]
    depth = head_gain.shape[0]
    ksize = conv_weight.shape[1]
    margin = ksize - 1
    lanes, blocks = lax.axis_size("ta"), lax.axis_size("dev")
    rank, place = lax.axis_index("ta"), lax.axis_index("dev")
    own_heads = heads // lanes
    cols = own_heads * depth
    rows = projection_weight.shape[0]
    group = lanes * width
    ring = Ring()

    positions = place * group + jnp.arange(group, dtype=jnp.int32)
    documents = document_of(lengths, positions)
    valid = jnp.stack(
        [
            (document_of(lengths, positions - margin + offset) == documents).astype(F32)
            for offset in range(ksize)
        ],
        axis=1,
    )
    previous = document_of(lengths, positions[::width] - 1)

    at_rank = rank.astype(jnp.int32).reshape(1)
    at_place = place.astype(jnp.int32).reshape(1)
    by_rank = jnp.concatenate([at_rank, ring.slot_of])

    flags = jnp.zeros((8, model), BF).at[0, 0:width].set(pad_mask.astype(BF))
    edge = jnp.concatenate([tokens[width - PAD :], flags], axis=0)
    route = [(i, i + 1) for i in range(lanes - 1, blocks * lanes - 1, lanes)]
    before = lax.ppermute(edge, BOTH, route)
    flags = flags.at[0, width : width + PAD].set(before[PAD, width - PAD : width])
    packed = gather_parts(jnp.concatenate([tokens, flags, before[0:PAD]], axis=0))
    cot_parts = gather_parts(cotangent)
    group_tokens, normed_group, normed, flags = vmem_call(
        "norm",
        functools.partial(norm_kernel, width),
        [
            shape((group, model), BF),
            shape((group, model), BF),
            shape((group + PAD, model), BF),
            shape((lanes, 8, 2 * width), BF),
        ],
        [at_rank, *packed, attn_gain[None]],
        0,
    )
    cot_group = in_order(cot_parts, at_rank)
    live = flags[:, 0, 0:width].reshape(group).astype(F32)
    live_ext = jnp.concatenate([flags[0, 0, width : width + PAD].astype(F32), live])[:, None]

    own_conv = lax.dynamic_slice_in_dim(conv_weight, rank * cols, cols, 2)
    own_bias = lax.dynamic_slice_in_dim(beta_bias, rank * own_heads, own_heads, 0)
    chunk_docs = documents.reshape(lanes, width)
    continuing = (chunk_docs == previous[:, None]).reshape(group).astype(F32)
    closing = (chunk_docs == chunk_docs[:, width - 1 :]).reshape(group).astype(F32)
    shared = jnp.stack(
        [valid[:, j] for j in range(margin)] + [continuing, closing, live, documents.astype(F32)], axis=0
    )
    shared = jnp.broadcast_to(shared, (own_heads,) + shared.shape)
    columns = jnp.transpose(shared, (0, 2, 1))

    split = jnp.transpose(projection_weight.reshape(rows, 4, lanes, cols), (2, 0, 1, 3)).reshape(lanes, rows, 4 * cols)
    turned = jnp.tile(w_beta.T.reshape(lanes, own_heads, rows), (1, lanes, 1))
    turned = jnp.pad(turned, ((0, 0), (0, 0), (0, 4 * cols - rows)))
    parts = exchange(jnp.concatenate([split, turned], axis=1), rank)
    (own_rows,) = vmem_call(
        "weights",
        functools.partial(weights_kernel, lanes),
        [shape((lanes * rows + heads, 4 * cols), BF)],
        [at_rank, *parts],
        0,
    )
    w = ring.collect(own_rows, [[packed[-1]], [normed, cot_group, live_ext], [columns, own_conv]])
    cot_all = lax.all_gather(gate(cotangent, w[-1]), BOTH, axis=0, tiled=True)
    projected, w_out, beta_logit, wbeta = project(ring.slots, normed, live_ext, w, lanes)
    beta_logit = beta_logit[PAD:, :own_heads]
    sig_beta = jax.nn.sigmoid(beta_logit + own_bias)
    beta = sig_beta * live[:, None]
    row = jnp.concatenate([shared, beta.T[:, None]], axis=1)
    columns = jnp.concatenate([columns, beta.T[:, :, None]], axis=2)
    mixer = Mixer(projected, own_conv, columns, row, width)
    head_normed = mixer.outputs(
        jnp.concatenate([at_place, ring.slots]), ring.collect(mixer.whole), head_gain[None]
    )
    w_out = gather_parts(w_out, head_normed)
    heads_low = gather_parts(head_normed)
    feed_rows, *own_feed, own_residual = vmem_call(
        "out",
        functools.partial(out_kernel, lanes),
        [shape((group, model), BF)] + [shape((width // 2, model), BF)] * 2 + [shape((width, model))],
        [by_rank, *heads_low, *w_out, group_tokens, mlp_gain[None]],
        2 * group * model * model,
        scratch=[pltpu.VMEM((group, model), F32)],
    )
    half_rows = width // 2
    feed_halves = [lax.all_gather(x, BOTH, axis=0, tiled=True) for x in own_feed]

    weights = [w_gate, w_up, w_down]
    units = w_gate.shape[1]
    core = (rank % 2).astype(jnp.int32).reshape(1)
    *arrays, kept, sent, partial_branch = feed_own(
        jnp.concatenate([at_place, core]), feed_rows, cot_group, weights, blocks * group, width
    )
    others = lax.rem(place + 1 + jnp.arange(blocks - 1, dtype=jnp.int32), blocks)
    row_parts = [others[: (blocks + 1) // 2], others[(blocks + 1) // 2 :]]

    def hidden_of(part, held, dep):
        return by_group(
            "feed_hidden", hidden_kernel, part, group, [cot_all], [w_down], [units], held, [dep], 1
        )[::-1]

    kept, arrived, (_, grad_hidden) = scatter_sum(
        kept, sent, rank, lambda sent: hidden_of(row_parts[0], [], sent)
    )

    halves_left = [0, 1]

    def by_halves(x):
        return x.reshape(blocks * lanes, 2, half_rows, x.shape[-1])

    def fill_rows(deps):
        half = halves_left.pop(0)
        *found, token = by_group(
            "feed_rows", rows_kernel, others, lanes * half_rows, [feed_halves[half], by_halves(grad_hidden)],
            weights[:2], [units] * 3, [by_halves(x) for x in arrays], deps, 2, half,
        )
        arrays[:] = [x.reshape(blocks * group, units) for x in found]
        return token

    order = [0, 1, 2]
    ffn_grads = [[], [], []]
    done = [0, 0, 0]

    def fill_grads(parts, dep):
        which = order[0]
        lefts = [cot_all] if which == 2 else feed_halves
        hidden, grad_gate, grad_lifted = arrays
        right = (grad_gate, grad_lifted, hidden)[which]
        right = by_halves(right)
        out, token = weight_grad(done[which], parts, lefts, right, ffn_grads[which], [dep], which == 2)
        ffn_grads[which] = [out]
        done[which] += 1
        if done[which] == parts:
            order.pop(0)
        return token

    grad_residual, grad_mlp_gain, *sent = vmem_call(
        "residual",
        functools.partial(residual_kernel, lanes),
        [shape((width, model)), shape((1, model))] + [shape((width, 2 * cols), BF)] * lanes,
        [by_rank, *w_out, kept, arrived, own_residual, cotangent, mlp_gain[None]],
        2 * width * model * model,
        scratch=[pltpu.VMEM((width, model), BF)],
    )
    by_heads = [swap(x, "ta", j) if j else x for j, x in enumerate(sent)]
    token, grad_hidden = hidden_of(row_parts[1], [grad_hidden], sent[0])
    leak, grad_head_gain, mixed_cols = mixer.leak(at_rank, by_heads, [token])
    leaks = [
        lax.ppermute(leak, "dev", [(i, i - k) for i in range(k, blocks)]) for k in range(1, blocks)
    ]
    token = fill_rows([leak])
    grad_q, grad_k, grad_v, tail, spill, grad_conv, grad_beta = mixer.back(leaks, [token])
    arrived = lax.ppermute(spill.astype(BF), "dev", [(i, i - 1) for i in range(1, blocks)])
    grad_logit = grad_beta[:, 0].T * beta * (1.0 - sig_beta)
    grad_bias = jnp.sum(grad_logit, axis=0)
    grad_logit_low = grad_logit.astype(BF)

    grad_logit_low = jnp.pad(grad_logit_low, ((0, 0), (0, 8 - own_heads)))

    half = (lanes // 2, width, model)
    grad_projected, kept, sent, grad_attn_gain = vmem_call(
        "normed_back",
        functools.partial(normed_back_kernel, blocks),
        [shape((group, 3 * cols), BF), shape(half, BF), shape(half, BF), shape((1, model))],
        [jnp.concatenate([core, ring.slots]), *w, grad_q, grad_k, grad_v, tail, arrived]
        + [live[group - PAD :, None], grad_logit_low, wbeta, group_tokens],
        2 * group * model * 3 * cols,
        scratch=[pltpu.VMEM((group, model), BF)],
    )

    *partial_rows, partial_wbeta = vmem_call(
        "weight_rows",
        functools.partial(weight_rows_kernel, lanes),
        [shape((model // blocks, 4 * cols), BF)] * blocks + [shape((8, model))],
        [jnp.concatenate([at_rank, ring.slots]), *heads_low, normed_group, grad_projected, mixed_cols]
        + [grad_logit_low],
        2 * group * model * 4 * cols,
        scratch=[pltpu.VMEM((group, model), BF)],
    )
    made = []

    def fill(function, *deps):
        made.append(function(*deps))
        return made[-1]

    terms, deps = ring.scatter(
        partial_rows,
        [
            lambda x: fill(fill_rows, [x]),
            lambda x: fill(fill_grads, 1, x),
            lambda x: fill(fill_grads, 1, x),
            lambda x: fill(fill_grads, 2, x),
        ],
    )
    (w_part,) = vmem_call("sum", sum_kernel, [shape(terms[0].shape, BF)], terms, 0, deps)
    w_parts = exchange(w_part.reshape(lanes, rows, 4 * cols), rank)
    token = fill_grads(2, w_part)
    (grad_projection,) = vmem_call(
        "assemble",
        assemble_kernel,
        [shape((rows, 4, model))],
        [at_rank, *w_parts],
        0,
        [token],
    )

    kept_b, sent_b = (
        lax.dynamic_index_in_dim(partial_branch.reshape(lanes // 2, 2, width, model), which, 1, False)
        for which in (rank % 2, 1 - rank % 2)
    )
    kept, arrived, _ = scatter_sum(
        jnp.concatenate([kept, kept_b], axis=1), jnp.concatenate([sent, sent_b], axis=1), rank,
        lambda sent: (made[0],),
    )
    both_sums = kept.astype(F32) + arrived.astype(F32)
    block_out = (own_residual + both_sums[width:]).astype(BF)
    _, attention_back = jax.vjp(lambda x: rms_scale(x, attn_gain), tokens.astype(F32))
    grad_tokens = grad_residual + attention_back(both_sums[:width])[0]

    gains = jnp.concatenate([grad_mlp_gain[0], grad_head_gain[0], grad_attn_gain[0]])
    pieces = [grad_conv.reshape(-1), partial_wbeta[:own_heads].reshape(-1), grad_bias, gains]
    ends = [0]
    for piece in pieces:
        ends.append(ends[-1] + piece.shape[0])
    flat = jnp.concatenate(pieces)
    flat = jnp.pad(flat, (0, -flat.shape[0] % 1024)).reshape(-1, 128)
    flat = sum_over(flat, "dev", made)
    flat = in_order(gather_parts(flat), at_rank).reshape(lanes, -1)
    conv_sum, wbeta_sum, bias_sum, gains = (flat[:, a:b] for a, b in zip(ends, ends[1:]))
    conv_sum = jnp.transpose(conv_sum.reshape(lanes, 3, ksize, cols), (1, 2, 0, 3))
    conv_sum = conv_sum.reshape(3, ksize, lanes * cols)
    wbeta_sum = lax.dynamic_slice_in_dim(
        wbeta_sum.reshape(heads, model), (place * lanes + rank) * rows, rows, 1
    )
    grad_w_beta = wbeta_sum.T
    bias_sum = bias_sum.reshape(heads)
    gains = jnp.sum(gains, axis=0)

    (grad_w_gate,), (grad_w_up,), (grad_w_down,) = ffn_grads
    return (
        block_out,
        grad_tokens,
        gains[model + depth : 2 * model + depth],
        grad_projection,
        grad_w_beta,
        bias_sum,
        conv_sum,
        gains[model : model + depth],
        gains[:model],
        grad_w_gate,
        grad_w_up,
        grad_w_down,
    )


def solution(mesh):
    rows = P(BOTH, None)
    three = P(BOTH, None, None)
    return jax.shard_map(
        body,
        mesh=mesh,
        in_specs=(
            rows,
            rows,
            P(),
            P(BOTH),
            P(),
            three,
            rows,
            P(),
            P(),
            P(),
            P(),
            P(None, "ta"),
            P(None, "ta"),
            P("ta", None),
        ),
        out_specs=(
            rows,
            rows,
            P(),
            three,
            rows,
            P(),
            P(),
            P(),
            P(),
            P(None, "ta"),
            P(None, "ta"),
            P("ta", None),
        ),
        check_vma=False,
    )
```

```python
import functools

import jax
import jax.numpy as jnp
from jax import lax
from jax.experimental import pallas as pl
from jax.experimental.pallas import tpu as pltpu
from jax.sharding import PartitionSpec as P

NORM_EPS = 1e-06
HEAD_EPS = 1e-05
UNIT_EPS = 1e-06
BOTH = ("dev", "ta")
BF = jnp.bfloat16
F32 = jnp.float32


def swap(x, axis, bit):
    return lax.ppermute(x, axis, [(i, i ^ bit) for i in range(lax.axis_size(axis))])


def gather_parts(x, *waits):
    parts = [x]
    for j in range(1, lax.axis_size("ta")):
        bit = j & -j
        if waits and j == 2 * bit + bit:
            parts[j ^ bit] = gate(parts[j ^ bit], *waits)
        parts.append(swap(parts[j ^ bit], "ta", bit))
    return parts


def gate(x, *deps):
    return pl.pallas_call(
        lambda *refs: None,
        name="gate",
        out_shape=jax.ShapeDtypeStruct(x.shape, x.dtype),
        in_specs=[pl.BlockSpec(memory_space=pl.ANY)] * (1 + len(deps)),
        out_specs=pl.BlockSpec(memory_space=pl.ANY),
        input_output_aliases={0: 0},
    )(x, *deps)


class Ring:
    def __init__(self):
        n = self.size = lax.axis_size("dev")
        self.last = n // 2
        self.order = list(range(0, n, 2)) + list(range(n - 1, 0, -2))
        self.place = lax.axis_index("dev")
        self.spot = self.spot_of(self.place)
        distances = [0] + [d for s in range(1, self.last) for d in (-s, s)] + [self.last]
        spots = lax.rem(self.spot + n + jnp.array(distances, jnp.int32), n)
        self.slots = jnp.where(2 * spots < n, 2 * spots, 2 * (n - 1 - spots) + 1)
        away = lax.rem(self.spot_of(jnp.arange(n, dtype=jnp.int32)) + n - self.spot, n)
        slot = jnp.where(away < self.last, 2 * away, 2 * (n - away) - 1)
        self.slot_of = jnp.where(away == self.last, n - 1, slot)

    def spot_of(self, index):
        return jnp.where(index % 2 == 0, index // 2, self.size - 1 - index // 2)

    def move(self, x, step):
        n = self.size
        return lax.ppermute(x, "dev", [(self.order[p], self.order[(p + step) % n]) for p in range(n)])

    def collect(self, x, waits=()):
        half = x.shape[0] // 2
        found = [x]
        onward, back = x, x
        for s in range(1, self.last):
            onward, back = self.move(onward, 1), self.move(back, -1)
            if len(waits) >= s and waits[s - 1]:
                onward, back = gate(onward, *waits[s - 1]), gate(back, *waits[s - 1])
            found += [onward, back]
        far = [self.move(onward[:half], 1), self.move(back[half:], -1)]
        return found + [jnp.concatenate(far, axis=0)]

    def scatter(self, blocks, beside=()):
        last = self.last
        beside = list(beside) + [None] * last
        block = lambda d: blocks[0 if d == 0 else 2 * d if d > 0 else -2 * d - 1]
        right, left = blocks[-2:]
        for s in range(last - 1, -1, -1):
            ahead, behind = self.move(right, 1), self.move(left, -1)
            deps = [beside[last - 1 - s](right)] if beside[last - 1 - s] else []
            if s:
                like = [shape(block(s).shape, BF)] * 2
                right, left = vmem_call(
                    "ring_add", ring_add_kernel, like, [block(s), block(-s), ahead, behind], 0, deps
                )
        return [block(0), ahead, behind], deps


def ring_add_kernel(first, second, ahead, behind, right, left):
    rows, part = first.shape[0], ahead.shape[0]
    for block, arrived, out, at in (
        (first, ahead, right, slice(0, part)),
        (second, behind, left, slice(rows - part, rows)),
    ):
        if part < rows:
            out[...] = block[...]
        out[at, :] = (block[at, :].astype(F32) + arrived[...].astype(F32)).astype(BF)


def sum_kernel(rank, x, y, z, *outs):
    rows = outs[0].shape[0]
    for j, out in enumerate(outs):
        at = pl.ds(pl.multiple_of((rank[0] ^ j) * rows, rows), rows)
        out[...] = (x[at, :].astype(F32) + (y[at, :].astype(F32) + z[at, :].astype(F32))).astype(BF)


def assemble_kernel(rank, *refs):
    out, parts = refs[-1], refs[:-1]
    count = out.shape[1]
    cols = parts[0].shape[1] // count
    for j, part in enumerate(parts):
        at = pl.ds(pl.multiple_of((rank[0] ^ j) * cols, cols), cols)
        for i in range(count):
            out[:, i, at] = part[:, i * cols : (i + 1) * cols].astype(F32)


def exchange(blocks, rank):
    parts = []
    for j in range(lax.axis_size("ta")):
        block = lax.dynamic_index_in_dim(blocks, rank ^ j, 0, False)
        parts.append(swap(block, "ta", j) if j else block)
    return parts


def scatter_sum(kept, sent, rank, beside=None):
    lanes = lax.axis_size("ta")
    made = None
    bit = 1
    while True:
        arrived = swap(sent, "ta", bit)
        bit *= 2
        if bit == lanes:
            if beside:
                made = beside(sent)
                arrived = gate(arrived, made[0])
            return kept[0], arrived[0], made
        half = (kept.shape[0] // 2,) + kept.shape[1:]
        mine = ((rank // bit) % 2).astype(jnp.int32).reshape(1)
        kept, sent = vmem_call("stage", stage_kernel, [shape(half), shape(half, BF)], [mine, kept, arrived], 0)


def stage_kernel(mine, first, second, kept, sent):
    for n in range(kept.shape[0]):
        for out, which in ((kept, mine[0]), (sent, 1 - mine[0])):
            at = 2 * n + which
            out[n] = (first[at].astype(F32) + second[at].astype(F32)).astype(out.dtype)


def rms_scale(values, gain):
    return values * lax.rsqrt(jnp.mean(values * values, axis=-1, keepdims=True) + NORM_EPS) * gain


def document_of(lengths, positions):
    starts = jnp.cumsum(lengths) - lengths
    above = (starts[None, :] <= positions[:, None]).astype(jnp.int32)
    return jnp.sum(above, axis=1) - 1


def contract_rows(left, right):
    return lax.dot_general(left, right, (((0,), (0,)), ((), ())), preferred_element_type=F32)


def contract_cols(left, right):
    return lax.dot_general(left, right, (((1,), (1,)), ((), ())), preferred_element_type=F32)


def dot(left, right):
    return jnp.dot(left, right, preferred_element_type=F32)


PAD = 8
HEADS_A_STEP = 2
VMEM_LIMIT = 48 * 1024 * 1024
FFN_VMEM = 56 * 1024 * 1024


def dims(a, b, ca, cb):
    return lax.dot_general(a, b, (((ca,), (cb,)), ((), ())), preferred_element_type=F32)


def d1(a, b, ca=1, cb=0):
    return dims(a.astype(BF), b.astype(BF), ca, cb)


def parts_of(a):
    high = a.astype(BF)
    return high, (a - high.astype(F32)).astype(BF)


def d3(a, b, ca=1, cb=0):
    ah, al = parts_of(a)
    bh, bl = parts_of(b)
    return dims(ah, bh, ca, cb) + (dims(ah, bl, ca, cb) + dims(al, bh, ca, cb))


def iotas(size):
    return (
        lax.broadcasted_iota(jnp.int32, (size, size), 0),
        lax.broadcasted_iota(jnp.int32, (size, size), 1),
    )


def inverses_of(lowers):
    size = lowers[0].shape[0]
    row, col = iotas(size)
    eye = (row == col).astype(F32)
    pair = (row // 2 == col // 2).astype(F32)
    found = [eye - low * pair for low in lowers]
    block = 2
    while block < size:
        joint = ((row // (2 * block) == col // (2 * block)) & (row // block != col // block)).astype(F32)
        steps = [d1(low * joint, x) for low, x in zip(lowers, found)]
        found = [x - d1(x, s) for x, s in zip(found, steps)]
        block *= 2
    errors = [d3(low, x) + (x - eye) for low, x in zip(lowers, found)]
    return [x - d1(x, e) for x, e in zip(found, errors)]


def unit_of(active):
    scale = lax.rsqrt(jnp.sum(active * active, axis=-1, keepdims=True) + UNIT_EPS)
    return active * scale, scale


def masks_of(aux, row, at, size):
    doc, doc_row = aux[at, 6:7], row[6:7, at]
    r, c = iotas(size)
    same = doc == doc_row
    weak = (same & (r >= c)).astype(F32)
    strict = (same & (r > c)).astype(F32)
    return weak, strict


def forward_kernel(size, xq, xk, xv, conv, aux_ref, row_ref, yq, yk, yv, inv, plain, reach, read, direct, trans, fresh, whole):
    heads, count = inv.shape[0], inv.shape[1]
    depth = xq.shape[1] // heads
    ksize = conv.shape[1]
    r, c = iotas(depth)
    eye = (r == c).astype(F32)
    spans = [slice(n * size, (n + 1) * size) for n in range(count)]
    saved = []
    lowers = []
    for h in range(heads):
        aux, row = aux_ref.at[h], row_ref.at[h]
        col = slice(h * depth, (h + 1) * depth)
        for n, at in enumerate(spans):
            active = []
            for i, (x, y) in enumerate(((xq, yq), (xk, yk), (xv, yv))):
                first = PAD - (ksize - 1) + n * size
                summed = x[first + ksize - 1 : first + ksize - 1 + size, col] * conv[i, ksize - 1 : ksize, col]
                for j in range(ksize - 1):
                    moved = x[first + j : first + j + size, col]
                    summed = summed + moved * conv[i, j : j + 1, col] * aux[at, j : j + 1]
                y[at, col] = summed
                active.append(summed * jax.nn.sigmoid(summed))
            q = unit_of(active[0])[0] * depth ** (-0.5)
            k = unit_of(active[1])[0]
            weak, strict = masks_of(aux, row, at, size)
            rate = row[7:8, at]
            products = d3(jnp.concatenate([q, k], axis=0), k, 1, 1)
            lowers.append(products[size:] * rate * strict)
            saved.append((h, n, q, k, active[2], products[:size] * rate * weak))
    inverses = inverses_of(lowers)
    total, added = [None] * heads, [None] * heads
    for inverse, (h, n, q, k, v, mix) in zip(inverses, saved):
        at = spans[n]
        aux = aux_ref.at[h]
        cont, clos, beta = aux[at, 3:4], aux[at, 4:5], aux[at, 7:8]
        both = d3(inverse, jnp.concatenate([v, k * cont], axis=1))
        spread = d1(mix, both)
        inv[h, n] = inverse
        plain[h, at, :] = both[:, :depth]
        reach[h, at, :] = both[:, depth:]
        direct[h, at, :] = spread[:, :depth]
        read[h, at, :] = q * cont - spread[:, depth:]
        gained = d3(k * (beta * clos), both, 0, 0)
        map_n = aux[(n + 1) * size - 1 : (n + 1) * size, 3:4] * eye - gained[:, depth:]
        add_n = gained[:, :depth]
        trans[h, n] = map_n
        fresh[h, n] = add_n
        if n == 0:
            total[h], added[h] = map_n, add_n
        else:
            new = d3(map_n, jnp.concatenate([added[h], total[h]], axis=1))
            total[h], added[h] = new[:, depth:], new[:, :depth] + add_n
    for h in range(heads):
        whole[h, 0] = total[h].astype(BF)
        whole[h, 1] = added[h].astype(BF)


def read_kernel(size, count_of, index, *refs):
    parts, refs = refs[:count_of], refs[count_of:]
    trans, fresh, read, direct, gain, both, states, outputs, normed = refs
    heads, count = trans.shape[0], trans.shape[1]
    depth = trans.shape[-1]
    for n, part in enumerate(parts):
        both[index[1 + n]] = part[...]

    def earlier(i, carry):
        return tuple(
            d3(both[i, h, 0].astype(F32), carry[h]) + both[i, h, 1].astype(F32) for h in range(heads)
        )

    carry = lax.fori_loop(0, index[0], earlier, tuple(jnp.zeros((depth, depth), F32) for _ in range(heads)))
    carry = list(carry)
    for n in range(count):
        at = slice(n * size, (n + 1) * size)
        for h in range(heads):
            state = carry[h]
            states[h, n] = state
            out = direct[h, at, :] + d3(read[h, at, :], state)
            cols = slice(h * depth, (h + 1) * depth)
            outputs[at, cols] = out
            scale = lax.rsqrt(jnp.mean(out * out, axis=-1, keepdims=True) + HEAD_EPS)
            normed[at, cols] = (out * scale * gain[...]).astype(BF)
            if n < count - 1:
                carry[h] = d3(trans[h, n], state) + fresh[h, n]


def leak_kernel(size, lanes, rank, *refs):
    parts, refs = refs[:lanes], refs[lanes:]
    outputs, gain, read, trans, grad_out, from_out, leak, grad_gain, mixed, grads = refs
    heads, count = trans.shape[0], trans.shape[1]
    depth = trans.shape[-1]
    for j, part in enumerate(parts):
        at = pl.ds(pl.multiple_of((rank[0] ^ j) * size, size), size)
        grads[at, :] = part[:, : heads * depth]
        mixed[at, :] = part[:, heads * depth :]
    gained = jnp.zeros((1, depth), F32)
    totals = [None] * heads
    for n in range(count - 1, -1, -1):
        at = slice(n * size, (n + 1) * size)
        for h in range(heads):
            cols = slice(h * depth, (h + 1) * depth)
            out, grad = outputs[at, cols], grads[at, cols].astype(F32)
            scale = lax.rsqrt(jnp.mean(out * out, axis=-1, keepdims=True) + HEAD_EPS)
            unit = out * scale
            gained = gained + jnp.sum(grad * unit, axis=0, keepdims=True)
            grad = grad * gain[...]
            grad = scale * (grad - unit * jnp.mean(grad * unit, axis=-1, keepdims=True))
            grad_out[h, at, :] = grad
            term = d3(read[h, at, :], grad, 0, 0)
            from_out[h, n] = term
            totals[h] = term if n == count - 1 else d3(trans[h, n], totals[h], 0, 0) + term
    for h in range(heads):
        leak[h] = totals[h].astype(BF)
    grad_gain[...] = gained


def chain_kernel(index, beside, *refs):
    both, trans, from_out, grads = refs[-4:]
    pairs = refs[:-4]
    heads, count = trans.shape[0], trans.shape[1]
    depth = trans.shape[-1]
    devices = both.shape[0]
    odd = index[0] % 2
    carry = [jnp.zeros((depth, depth), F32) for _ in range(heads)]

    def follow(at, leak):
        at = jnp.minimum(at, devices - 1)
        return [d3(both[at, h, 0].astype(F32), carry[h], 0, 0) + leak(h).astype(F32) for h in range(heads)]

    for k in range(len(pairs), 0, -1):
        pair = pairs[k - 1]
        first = index[0] - odd + 2 * k
        carry = follow(first + 1, lambda h: pair[1 - odd, h])
        carry = follow(first, lambda h: pair[odd, h])
    later = follow(index[0] + 1, lambda h: beside[h])
    carry = [jnp.where(odd == 0, x, y) for x, y in zip(later, carry)]
    for n in range(count - 1, -1, -1):
        for h in range(heads):
            grads[h, n] = carry[h]
            if n:
                carry[h] = d3(trans[h, n], carry[h], 0, 0) + from_out[h, n]


def backward_kernel(size, xq, xk, xv, yq, yk, yv, conv, aux_ref, row_ref, inv, plain, reach, states, grads, grad_out,
                    gq, gk, gv, tail, spill, grad_conv, grad_beta, zs):
    count = inv.shape[1]
    depth = xq.shape[1]
    ksize = conv.shape[1]
    aux, row = aux_ref.at[0], row_ref.at[0]
    length = count * size
    scale_q = depth ** (-0.5)
    for n in range(count):
        at = slice(n * size, (n + 1) * size)
        cont, clos, beta = aux[at, 3:4], aux[at, 4:5], aux[at, 7:8]
        weak, strict = masks_of(aux, row, at, size)
        rate = row[7:8, at]
        ys = [yq[at, :], yk[at, :], yv[at, :]]
        sigs = [jax.nn.sigmoid(y) for y in ys]
        uq, rq = unit_of(ys[0] * sigs[0])
        k, rk = unit_of(ys[1] * sigs[1])
        q = uq * scale_q
        products = d1(jnp.concatenate([q, k], axis=0), k, 1, 1)
        qk, kk = products[:size], products[size:]
        mix = qk * rate * weak
        state, grad_state, dout = states[0, n], grads[0, n], grad_out[0, at, :]
        u = plain[0, at, :] - d1(reach[0, at, :], state)
        kds = d1(k, grad_state)
        written = beta * clos
        du = d1(mix, dout, 0, 0) + written * kds
        dr = d1(inv[0, n], du, 0, 0)
        pair = jnp.concatenate([dout, dr], axis=0)
        outer = d1(pair, u, 1, 1)
        through = d1(pair, state, 1, 1)
        dp = outer[:size] * weak
        dl = -outer[size:] * strict
        per_key = jnp.sum(dp * qk + dl * kk, axis=0, keepdims=True)
        per_state = jnp.sum((kds * u).T, axis=0, keepdims=True)
        grad_beta[0, :, at] = per_key + row[4:5, at] * per_state
        dqk = dp * rate
        da = dl * rate
        dq = cont * through[:size] + d1(dqk, k)
        dk = d1(dqk, q, 0, 0) + written * d1(u, grad_state, 1, 1) - cont * through[size:] + d1(da + da.T, k)
        dq = dq * scale_q
        acts = [
            rq * (dq - uq * jnp.sum(uq * dq, axis=-1, keepdims=True)),
            rk * (dk - k * jnp.sum(k * dk, axis=-1, keepdims=True)),
            dr,
        ]
        for i, x in enumerate((xq, xk, xv)):
            dy = acts[i] * sigs[i] * (1.0 + ys[i] * (1.0 - sigs[i]))
            first = PAD - (ksize - 1) + n * size
            for j in range(ksize):
                dv = dy if j == ksize - 1 else dy * aux[at, j : j + 1]
                term = jnp.sum(dv * x[first + j : first + j + size, :], axis=0, keepdims=True)
                before = jnp.zeros_like(term) if n == 0 else grad_conv[i, j : j + 1, :]
                grad_conv[i, j : j + 1, :] = before + term
                zs[i, j, PAD + n * size : PAD + (n + 1) * size, :] = dv * conv[i, j : j + 1, :]
    for i, g in enumerate((gq, gk, gv)):
        for j in range(ksize):
            zs[i, j, 0:PAD, :] = jnp.zeros((PAD, depth), F32)
            zs[i, j, PAD + length : 2 * PAD + length, :] = jnp.zeros((PAD, depth), F32)

        def shifted_sum(first, rows):
            return sum(zs[i, j, first + ksize - 1 - j : first + ksize - 1 - j + rows, :] for j in range(ksize))

        for n in range(count):
            at = slice(n * size, (n + 1) * size)
            g[at, :] = (shifted_sum(PAD + n * size, size) * aux[at, 5:6]).astype(BF)
        tail[i] = shifted_sum(length, PAD)
        spill[i] = shifted_sum(0, PAD)


def vmem_call(name, kernel, out_shape, inputs, flops, deps=(), scratch=()):
    smem, vmem = (pl.BlockSpec(memory_space=m) for m in (pltpu.SMEM, pltpu.VMEM))

    def run(*refs):
        kernel(*refs[: len(inputs)], *refs[len(inputs) + len(deps) :])

    return pl.pallas_call(
        run,
        name=name,
        out_shape=out_shape,
        in_specs=[smem if x.dtype == jnp.int32 else vmem for x in inputs]
        + [pl.BlockSpec(memory_space=pl.ANY)] * len(deps),
        out_specs=[vmem] * len(out_shape),
        scratch_shapes=list(scratch),
        cost_estimate=cost(flops, inputs, out_shape),
        compiler_params=pltpu.CompilerParams(vmem_limit_bytes=FFN_VMEM),
    )(*inputs, *deps)


def cost(flops, inputs, outputs):
    moved = sum(x.size * x.dtype.itemsize for x in list(inputs) + list(outputs))
    return pl.CostEstimate(flops=int(flops), bytes_accessed=int(moved), transcendentals=0)


def shape(dims, dtype=F32):
    return jax.ShapeDtypeStruct(dims, dtype)


class Mixer:
    def __init__(self, projected, own_conv, aux, row, size):
        self.size = size
        self.heads, self.length = aux.shape[0], aux.shape[1]
        self.depth = own_conv.shape[2] // self.heads
        self.count = self.length // size
        self.projected, self.conv, self.aux, self.row = projected, own_conv, aux, row
        heads, length, depth, count = self.heads, self.length, self.depth, self.count
        ksize = own_conv.shape[1]
        self.token_specs = [
            pl.BlockSpec((length + PAD, depth), lambda h, i=i: (0, i * heads + h)) for i in range(3)
        ]
        self.head_cols = pl.BlockSpec((length, depth), lambda h: (0, h))
        self.conv_spec = pl.BlockSpec((3, ksize, depth), lambda h: (0, 0, h))
        self.aux_specs = [
            pl.BlockSpec((1, length, 8), lambda h: (h, 0, 0)),
            pl.BlockSpec((1, 8, length), lambda h: (h, 0, 0)),
        ]
        self.chunk_spec = pl.BlockSpec((1, count, depth, depth), lambda h: (h, 0, 0, 0))
        self.inv_spec = pl.BlockSpec((1, count, size, size), lambda h: (h, 0, 0, 0))
        self.rows_spec = pl.BlockSpec((1, length, depth), lambda h: (h, 0, 0))
        self.flops = 2 * heads * count * size * depth * depth
        inputs = [projected] * 3 + [own_conv, aux, row]
        square = shape((heads, count, depth, depth))
        tokens = shape((heads, length, depth))
        out_shape = (
            [shape((length, heads * depth))] * 3
            + [shape((heads, count, size, size))]
            + [tokens] * 4
            + [square] * 2
            + [shape((heads, 2, depth, depth), BF)]
        )
        step = HEADS_A_STEP if heads % HEADS_A_STEP == 0 else 1
        each = lambda x: pl.BlockSpec((step,) + x.shape[1:], lambda h: (h,) + (0,) * (len(x.shape) - 1))
        column = pl.BlockSpec((length, step * depth), lambda h: (0, h))
        (
            self.yq, self.yk, self.yv, self.inv, self.plain, self.reach, self.read, self.direct,
            self.trans, self.fresh, self.whole,
        ) = pl.pallas_call(
            functools.partial(forward_kernel, size),
            name="mixer_forward",
            out_shape=out_shape,
            grid=(heads // step,),
            in_specs=[
                pl.BlockSpec((length + PAD, step * depth), lambda h, i=i: (0, i * (heads // step) + h))
                for i in range(3)
            ]
            + [pl.BlockSpec((3, ksize, step * depth), lambda h: (0, 0, h)), each(aux), each(row)],
            out_specs=[column] * 3 + [each(x) for x in out_shape[3:]],
            cost_estimate=cost(60 * self.flops, inputs, out_shape),
            compiler_params=pltpu.CompilerParams(vmem_limit_bytes=VMEM_LIMIT),
        )(*inputs)

    def outputs(self, index, parts, head_gain):
        heads, length, depth, count = self.heads, self.length, self.depth, self.count
        self.index, self.gain = index, head_gain
        self.both, self.states, self.out, normed = vmem_call(
            "mixer_read",
            functools.partial(read_kernel, self.size, len(parts)),
            [
                shape((len(parts),) + parts[0].shape, BF),
                shape((heads, count, depth, depth)),
                shape((length, heads * depth)),
                shape((length, heads * depth), BF),
            ],
            [index, *parts, self.trans, self.fresh, self.read, self.direct, head_gain],
            12 * self.flops,
        )
        return normed

    def leak(self, rank, parts, deps=()):
        heads, length, depth, count = self.heads, self.length, self.depth, self.count
        self.grad_out, self.from_out, leak, grad_gain, mixed = vmem_call(
            "mixer_leak",
            functools.partial(leak_kernel, self.size, len(parts)),
            [
                shape((heads, length, depth)),
                shape((heads, count, depth, depth)),
                shape((heads, depth, depth), BF),
                shape((1, depth)),
                shape((length, heads * depth), BF),
            ],
            [rank, *parts, self.out, self.gain, self.read, self.trans],
            6 * self.flops,
            deps,
            scratch=[pltpu.VMEM((length, heads * depth), BF)],
        )
        return leak, grad_gain, mixed

    def back(self, leaks, deps=()):
        heads, length, depth, count = self.heads, self.length, self.depth, self.count
        ksize = self.conv.shape[1]
        (grads,) = vmem_call(
            "mixer_chain",
            chain_kernel,
            [shape((heads, count, depth, depth))],
            [self.index, *leaks, self.both, self.trans, self.from_out],
            6 * self.flops,
            deps,
        )
        inputs = [self.projected] * 3 + [self.yq, self.yk, self.yv, self.conv, self.aux, self.row]
        inputs += [self.inv, self.plain, self.reach, self.states, grads, self.grad_out]
        edge = shape((3, PAD, heads * depth))
        out_shape = [shape((length, heads * depth), BF)] * 3 + [edge] * 2
        out_shape += [shape((3, ksize, heads * depth)), shape((heads, 1, length))]
        edge_spec = pl.BlockSpec((3, PAD, depth), lambda h: (0, 0, h))
        return pl.pallas_call(
            functools.partial(backward_kernel, self.size),
            name="mixer_backward",
            out_shape=out_shape,
            grid=(heads,),
            in_specs=self.token_specs
            + [self.head_cols] * 3
            + [self.conv_spec]
            + self.aux_specs
            + [self.inv_spec, self.rows_spec, self.rows_spec, self.chunk_spec, self.chunk_spec, self.rows_spec],
            out_specs=[self.head_cols] * 3
            + [edge_spec] * 2
            + [self.conv_spec, pl.BlockSpec((1, 1, length), lambda h: (h, 0, 0))],
            scratch_shapes=[pltpu.VMEM((3, ksize, length + 2 * PAD, depth), F32)],
            cost_estimate=cost(30 * self.flops, inputs, out_shape),
            compiler_params=pltpu.CompilerParams(vmem_limit_bytes=VMEM_LIMIT),
        )(*inputs)


ANY = pl.BlockSpec(memory_space=pl.ANY)
TOKEN = shape((8, 128))


def resident(x):
    return pl.BlockSpec(x.shape, lambda *_: (0,) * x.ndim, pipeline_mode=pl.Buffered(1))


def activations(gate, lifted, grad_hidden):
    sig = jax.nn.sigmoid(gate)
    swish = gate * sig
    return (
        (swish * lifted).astype(BF),
        (grad_hidden * lifted * sig * (1.0 + gate * (1.0 - sig))).astype(BF),
        (grad_hidden * swish).astype(BF),
    )


def chunks_of(size, chunk=256):
    return [slice(at, min(at + chunk, size)) for at in range(0, size, chunk)]


def params(flops, moved):
    return dict(
        cost_estimate=pl.CostEstimate(flops=int(flops), bytes_accessed=int(moved), transcendentals=0),
        compiler_params=pltpu.CompilerParams(vmem_limit_bytes=FFN_VMEM),
    )


TOKEN_SPEC = pl.BlockSpec((8, 128), lambda *_: (0, 0))


def split_by_core(source, core, width, kept, sent):
    for p in range(kept.shape[0]):
        for ref, which in ((kept, core), (sent, 1 - core)):
            ref[p, 0:width, :] = source[pl.ds(pl.multiple_of((2 * p + which) * width, width), width), :]


def own_kernel(index, feed, cot, wg, wu, wd, hidden, grad_gate, grad_lifted, *refs):
    (kept, sent, kept_result, sent_result), (total, result) = refs[:4], refs[4:]
    units, model = wd.shape
    for cut in chunks_of(units):
        gated = jnp.dot(feed[...], wg[:, cut], preferred_element_type=F32)
        lifted = jnp.dot(feed[...], wu[:, cut], preferred_element_type=F32)
        grad_hidden = dims(cot[...], wd[cut, :], 1, 1)
        hidden[:, cut], grad_gate[:, cut], grad_lifted[:, cut] = activations(gated, lifted, grad_hidden)
    for cut in chunks_of(model):
        grad_feed = dims(grad_gate[...], wg[cut, :], 1, 1) + dims(grad_lifted[...], wu[cut, :], 1, 1)
        total[:, cut] = grad_feed.astype(BF)
        result[:, cut] = jnp.dot(hidden[...], wd[:, cut], preferred_element_type=F32).astype(BF)
    split_by_core(total, index[1], kept.shape[1], kept, sent)
    split_by_core(result, index[1], kept.shape[1], kept_result, sent_result)


def hidden_kernel(groups, cot, wd, *refs):
    out, token = refs[-2:]
    out[...] = dims(cot[...], wd[...], 1, 1).astype(BF)
    token[...] = jnp.zeros_like(token)


def rows_kernel(groups, feed, grad_hidden, wg, wu, *refs):
    *outs, token = refs[-4:]
    before = grad_hidden[...].reshape(feed.shape[0], -1)
    for cut in chunks_of(wg.shape[1]):
        gated = jnp.dot(feed[...], wg[:, cut], preferred_element_type=F32)
        lifted = jnp.dot(feed[...], wu[:, cut], preferred_element_type=F32)
        for out, value in zip(outs, activations(gated, lifted, before[:, cut].astype(F32))):
            out[:, :, :, cut] = value.reshape(out.shape[:-1] + (value.shape[-1],))
    token[...] = jnp.zeros_like(token)


def by_group(name, kernel, groups, size, inputs, weights, outs, held, deps, products, half=0):
    like = inputs[-1].shape
    count = groups.shape[0]

    def picked(x, width):
        if x.ndim == 2:
            return pl.BlockSpec((size, width), lambda i, g: (g[i], 0))
        return pl.BlockSpec((size // like[2], 1, like[2], width), lambda i, g: (g[i], half, 0, 0))

    first = 1 + len(inputs) + len(weights) + len(deps)
    return pl.pallas_call(
        kernel,
        name=name,
        out_shape=[shape(like[:-1] + (width,), BF) for width in outs] + [TOKEN],
        grid_spec=pltpu.PrefetchScalarGridSpec(
            num_scalar_prefetch=1,
            grid=(count,),
            in_specs=[picked(x, x.shape[-1]) for x in inputs]
            + [resident(w) for w in weights]
            + [ANY] * (len(deps) + len(held)),
            out_specs=[picked(inputs[-1], width) for width in outs] + [TOKEN_SPEC],
        ),
        input_output_aliases={first + n: n for n in range(len(held))},
        **params(
            2 * count * size * weights[0].size * products,
            sum(w.size for w in weights) * 2 + count * size * 2 * (sum(outs) + sum(x.shape[-1] for x in inputs)),
        ),
    )(groups, *inputs, *weights, *deps, *held)


def feed_own(index, feed, cot, weights, tokens, width):
    rows, model = feed.shape
    units = weights[0].shape[1]
    block = 2 * width
    count = rows // block
    wide = pl.BlockSpec((block, units), lambda i, g: (g[0] * count + i, 0))
    here = pl.BlockSpec((block, model), lambda i, g: (i, 0))
    half = pl.BlockSpec((1, width, model), lambda i, g: (i, 0, 0))
    return pl.pallas_call(
        own_kernel,
        name="feed_own",
        out_shape=[shape((tokens, units), BF)] * 3
        + [shape((count, width, model), BF)] * 4,
        grid_spec=pltpu.PrefetchScalarGridSpec(
            num_scalar_prefetch=1,
            grid=(count,),
            in_specs=[here] * 2 + [resident(w) for w in weights],
            out_specs=[wide] * 3 + [half] * 4,
            scratch_shapes=[pltpu.VMEM((block, model), BF)] * 2,
        ),
        **params(12 * rows * model * units, 6 * model * units + rows * (3 * units + 4 * model) * 2),
    )(index, feed, cot, *weights)


GRAD_COLS = 256


def grad_kernel(transposed, count, *refs):
    lefts, right = refs[:count], refs[count]
    out, token = refs[-2:]
    units = right.shape[-1]
    if count == 1:
        term = dims(lefts[0][...], right[...].reshape(-1, units), 0, 0)
    else:
        term = sum(dims(left[...], right[:, n].reshape(-1, units), 0, 0) for n, left in enumerate(lefts))
    out[...] = term.T if transposed else term
    token[...] = jnp.zeros_like(token)


def weight_grad(part, parts, lefts, right, held, deps, transposed):
    rows, model = lefts[0].shape
    units = right.shape[-1]
    count = model // GRAD_COLS // parts
    if transposed:
        out_spec = pl.BlockSpec((units, GRAD_COLS), lambda m: (0, part * count + m))
    else:
        out_spec = pl.BlockSpec((GRAD_COLS, units), lambda m: (part * count + m, 0))
    first = len(lefts) + 1 + len(deps)
    tokens = rows * len(lefts)
    return pl.pallas_call(
        functools.partial(grad_kernel, transposed, len(lefts)),
        name="weight_grad",
        out_shape=[shape((units, model) if transposed else (model, units)), TOKEN],
        grid=(count,),
        in_specs=[pl.BlockSpec((rows, GRAD_COLS), lambda m: (0, part * count + m))] * len(lefts)
        + [resident(right)]
        + [ANY] * (len(deps) + len(held)),
        out_specs=[out_spec, TOKEN_SPEC],
        input_output_aliases={first + n: n for n in range(len(held))},
        **params(
            2 * tokens * count * GRAD_COLS * units,
            2 * tokens * (units + count * GRAD_COLS) + 4 * count * GRAD_COLS * units,
        ),
    )(*lefts, right, *deps, *held)


def order_kernel(rank, *refs):
    out = refs[-1]
    size = refs[0].shape[0]
    for j, part in enumerate(refs[:-1]):
        out[pl.ds(pl.multiple_of((rank[0] ^ j) * size, size), size), :] = part[...]


def in_order(parts, rank):
    rows, width = parts[0].shape
    return vmem_call(
        "in_order", order_kernel, [shape((rows * len(parts), width), parts[0].dtype)], [rank, *parts], 0
    )[0]


def norm_kernel(width, rank, *refs):
    gain, group, normed, extended, live = refs[-5:]
    parts = refs[:-5]

    def scaled(values):
        values = values.astype(F32)
        scale = lax.rsqrt(jnp.mean(values * values, axis=-1, keepdims=True) + NORM_EPS)
        return (values * scale * gain[...]).astype(BF)

    for j, part in enumerate(parts):
        at = rank[0] ^ j
        rows = part[0:width, :]
        group[pl.ds(pl.multiple_of(at * width, width), width), :] = rows
        rows = scaled(rows)
        normed[pl.ds(pl.multiple_of(at * width, width), width), :] = rows
        extended[pl.ds(pl.multiple_of(PAD + at * width, PAD), width), :] = rows
        live[at] = part[width : width + 8, 0 : 2 * width]

        @pl.when(at == 0)
        def _():
            extended[0:PAD, :] = scaled(part[width + 8 : width + 8 + PAD, :])


def weights_kernel(lanes, rank, *refs):
    out, parts = refs[-1], refs[:-1]
    rows = out.shape[0] - parts[0].shape[0]
    rows = rows // (lanes - 1)
    heads = parts[0].shape[0] - rows
    mine = lax.broadcasted_iota(jnp.int32, (heads, 128), 0) // (heads // lanes)
    tile = jnp.zeros((heads, 128), F32)
    for j, part in enumerate(parts):
        at = rank[0] ^ j
        out[pl.ds(pl.multiple_of(at * rows, rows), rows), :] = part[0:rows, :]
        tile = jnp.where(mine == at, part[rows:, 0:128].astype(F32), tile)
    out[lanes * rows :, :] = jnp.zeros((heads, out.shape[1]), BF)
    out[lanes * rows :, 0:128] = tile.astype(BF)


def project_kernel(lanes, slots, x, live, *refs):
    out, out_w, logit, wbeta = refs[-4:]
    parts, last = refs[: len(refs) // 2 - 2], refs[len(refs) // 2 - 2 : -4]
    size = out_w.shape[0] // len(parts)
    heads = parts[0].shape[0] - size
    own = heads // lanes
    total = None
    for n, part in enumerate(parts):
        at = pl.ds(pl.multiple_of(slots[n] * size, size), size)
        term = jnp.dot(x[:, at], part[0:size, :], preferred_element_type=F32)
        total = term if total is None else total + term
    out[...] = total * live[...]

    @pl.when(pl.program_id(0) == 0)
    def _():
        each = size // lanes
        row = lax.broadcasted_iota(jnp.int32, (heads, size), 0)
        col = lax.broadcasted_iota(jnp.int32, (heads, size), 1)
        own_row = lax.broadcasted_iota(jnp.int32, (8, heads), 0)
        own_col = lax.broadcasted_iota(jnp.int32, (8, heads), 1)
        picked = ((own_col % own == own_row) & (own_row < own)).astype(BF)
        for n, (part, columns) in enumerate(zip(parts, last)):
            out_w[n * size : (n + 1) * size, :] = columns[0:size, :]
            tile = jnp.concatenate([part[size:, 0:each]] * lanes, axis=1)
            tile = jnp.where(col // each == row // own, tile.astype(F32), 0.0).astype(BF)
            at = pl.ds(pl.multiple_of(slots[n] * size, size), size)
            wbeta[:, at] = jnp.dot(picked, tile, preferred_element_type=F32).astype(BF)
        logit[...] = dims(x[...], wbeta[...], 1, 1)


def project(slots, x, live, parts, lanes):
    rows, model = x.shape
    size, width = parts[0].shape
    cols = width // 4
    whole = lambda a: pl.BlockSpec(a.shape, lambda i, s: (0,) * len(a.shape))
    outs = [shape((rows, 3 * cols)), shape((model, cols), BF), shape((rows, 8)), shape((8, model), BF)]
    return pl.pallas_call(
        functools.partial(project_kernel, lanes),
        name="project",
        out_shape=outs,
        grid_spec=pltpu.PrefetchScalarGridSpec(
            num_scalar_prefetch=1,
            grid=(3,),
            in_specs=[whole(x), whole(live)]
            + [pl.BlockSpec((size, cols), lambda i, s: (0, i))] * len(parts)
            + [pl.BlockSpec((size, cols), lambda i, s: (0, 3))] * len(parts),
            out_specs=[pl.BlockSpec((rows, cols), lambda i, s: (0, i))] + [whole(a) for a in outs[1:]],
        ),
        **params(6 * rows * model * cols, 2 * x.size + 8 * model * cols),
    )(slots, x, live, *parts, *parts)


def finish_kernel(kept, arrived, residual, grad_residual, tokens, gain, block_out, grad_tokens):
    width = tokens.shape[0]
    both = kept[...].astype(F32) + arrived[...].astype(F32)
    block_out[...] = (residual[...] + both[width:]).astype(BF)
    values = tokens[...].astype(F32)
    scale = lax.rsqrt(jnp.mean(values * values, axis=-1, keepdims=True) + NORM_EPS)
    unit = values * scale
    grad = both[:width] * gain[...]
    grad_tokens[...] = grad_residual[...] + scale * (
        grad - unit * jnp.mean(grad * unit, axis=-1, keepdims=True)
    )


def out_kernel(lanes, index, *refs):
    heads, w, refs = refs[:lanes], refs[lanes : 2 * lanes], refs[2 * lanes :]
    tokens, gain, feed, *own_feed, own_residual, total = refs
    rank = index[0]
    width = own_residual.shape[0]
    cols = heads[0].shape[1]
    blocks = w[0].shape[0]
    size = w[0].shape[0] // (index.shape[0] - 1)
    per = cols // size
    for j in range(lanes):
        acc = None
        for i in range(lanes):
            for p in range(per):
                slot = index[1 + (rank ^ i) * per + p]
                rows = w[j][pl.ds(pl.multiple_of(slot * size, size), size), :]
                term = jnp.dot(heads[i][:, p * size : (p + 1) * size], rows, preferred_element_type=F32)
                acc = term if acc is None else acc + term
        at = pl.ds(pl.multiple_of((rank ^ j) * cols, cols), cols)
        total[:, at] = tokens[:, at].astype(F32) + acc
    for n in range(lanes):
        at = slice(n * width, (n + 1) * width)
        values = total[at, :]
        scale = lax.rsqrt(jnp.mean(values * values, axis=-1, keepdims=True) + NORM_EPS)
        feed[at, :] = (values * scale * gain[...]).astype(BF)
    own = pl.ds(pl.multiple_of(rank * width, width), width)
    own_residual[...] = total[own, :]
    for n, out in enumerate(own_feed):
        out[...] = feed[pl.ds(pl.multiple_of(rank * width + n * (width // 2), width // 2), width // 2), :]


def residual_kernel(lanes, index, *refs):
    w, refs = refs[:lanes], refs[lanes:]
    kept, arrived, residual, cot, gain, grad_residual, grad_gain = refs[:7]
    sent, mixed = refs[7 : 7 + lanes], refs[7 + lanes]
    rank = index[0]
    cols = w[0].shape[1]
    size = w[0].shape[0] // (index.shape[0] - 1)
    per = cols // size
    grad = kept[...].astype(F32) + arrived[...].astype(F32)
    values = residual[...]
    scale = lax.rsqrt(jnp.mean(values * values, axis=-1, keepdims=True) + NORM_EPS)
    unit = values * scale
    grad_gain[...] = jnp.sum(grad * unit, axis=0, keepdims=True)
    grad = grad * gain[...]
    grad = cot[...].astype(F32) + scale * (grad - unit * jnp.mean(grad * unit, axis=-1, keepdims=True))
    grad_residual[...] = grad
    mixed[...] = grad.astype(BF)
    columns = [pl.ds(pl.multiple_of((rank ^ j) * cols, cols), cols) for j in range(lanes)]
    for j in range(lanes):
        for p in range(per):
            slot = index[1 + (rank ^ j) * per + p]
            acc = None
            for i in range(lanes):
                rows = w[i][pl.ds(pl.multiple_of(slot * size, size), size), :]
                term = dims(mixed[:, columns[i]], rows, 1, 1)
                acc = term if acc is None else acc + term
            sent[j][:, p * size : (p + 1) * size] = acc.astype(BF)
        sent[j][:, cols:] = mixed[:, columns[j]]


def normed_back_kernel(blocks, index, *refs):
    w, refs = refs[:blocks], refs[blocks:]
    gq, gk, gv, tail, arrived, live, logit, wbeta, tokens, kept_result, sent_result = refs[:11]
    grads, kept, sent, gain, total = refs[11:]
    size = total.shape[1] // blocks
    cols = gq.shape[1]
    length = gq.shape[0]
    for i, g in enumerate((gq, gk, gv)):
        at = slice(i * cols, (i + 1) * cols)
        grads[:, at] = g[...]
        last = ((tail[i] + arrived[i].astype(F32)) * live[...]).astype(BF)
        grads[length - 16 :, at] = jnp.concatenate([g[length - 16 : length - PAD, :], last], axis=0)
    values = tokens[...].astype(F32)
    scale = lax.rsqrt(jnp.mean(values * values, axis=-1, keepdims=True) + NORM_EPS)
    for n in range(blocks):
        at = pl.ds(pl.multiple_of(index[1 + n] * size, size), size)
        part = dims(grads[...], w[n][0:size, : 3 * cols], 1, 1) + dims(logit[...], wbeta[:, at], 0, 0)
        gain[:, at] = jnp.sum(part * (tokens[:, at].astype(F32) * scale), axis=0, keepdims=True)
        total[:, at] = part.astype(BF)
    width = kept_result.shape[1]
    split_by_core(total, index[0], width, kept, sent)
    for out, result in ((kept, kept_result), (sent, sent_result)):
        for n in range(out.shape[0]):
            out[n, width:, :] = result[n]


def weight_rows_kernel(lanes, index, *refs):
    heads, refs = refs[:lanes], refs[lanes:]
    normed, grads, mixed, logit = refs[:4]
    *outs, wbeta, joined = refs[4:]
    cols = mixed.shape[1]
    wide = grads.shape[1]
    size = outs[0].shape[0]
    rank = index[0]
    outs[-2:] = [outs[-2:]]
    for j, part in enumerate(heads):
        joined[:, pl.ds(pl.multiple_of((rank ^ j) * cols, cols), cols)] = part[...]
    for n, out in enumerate(outs):
        at = pl.ds(pl.multiple_of(index[1 + n] * size, size), size)
        first = dims(normed[:, at], grads[...], 0, 0).astype(BF)
        second = dims(joined[:, at], mixed[...], 0, 0).astype(BF)
        pieces = out if isinstance(out, list) else [out]
        for n, piece in enumerate(pieces):
            rows = slice(n * piece.shape[0], (n + 1) * piece.shape[0])
            piece[:, :wide] = first[rows]
            piece[:, wide:] = second[rows]
    wbeta[...] = dims(logit[...], normed[...], 1, 0)


def body(
    tokens,
    cotangent,
    lengths,
    pad_mask,
    attn_gain,
    projection_weight,
    w_beta,
    beta_bias,
    conv_weight,
    head_gain,
    mlp_gain,
    w_gate,
    w_up,
    w_down,
):
    width, model = tokens.shape
    heads = w_beta.shape[1]
    depth = head_gain.shape[0]
    ksize = conv_weight.shape[1]
    margin = ksize - 1
    lanes, blocks = lax.axis_size("ta"), lax.axis_size("dev")
    rank, place = lax.axis_index("ta"), lax.axis_index("dev")
    own_heads = heads // lanes
    cols = own_heads * depth
    rows = projection_weight.shape[0]
    group = lanes * width
    ring = Ring()

    positions = place * group + jnp.arange(group, dtype=jnp.int32)
    documents = document_of(lengths, positions)
    valid = jnp.stack(
        [
            (document_of(lengths, positions - margin + offset) == documents).astype(F32)
            for offset in range(ksize)
        ],
        axis=1,
    )
    previous = document_of(lengths, positions[::width] - 1)

    at_rank = rank.astype(jnp.int32).reshape(1)
    at_place = place.astype(jnp.int32).reshape(1)
    by_rank = jnp.concatenate([at_rank, ring.slot_of])

    flags = jnp.zeros((8, model), BF).at[0, 0:width].set(pad_mask.astype(BF))
    edge = jnp.concatenate([tokens[width - PAD :], flags], axis=0)
    route = [(i, i + 1) for i in range(lanes - 1, blocks * lanes - 1, lanes)]
    before = lax.ppermute(edge, BOTH, route)
    flags = flags.at[0, width : width + PAD].set(before[PAD, width - PAD : width])
    packed = gather_parts(jnp.concatenate([tokens, flags, before[0:PAD]], axis=0))
    cot_parts = gather_parts(cotangent)
    group_tokens, normed_group, normed, flags = vmem_call(
        "norm",
        functools.partial(norm_kernel, width),
        [
            shape((group, model), BF),
            shape((group, model), BF),
            shape((group + PAD, model), BF),
            shape((lanes, 8, 2 * width), BF),
        ],
        [at_rank, *packed, attn_gain[None]],
        0,
    )
    cot_group = in_order(cot_parts, at_rank)
    live = flags[:, 0, 0:width].reshape(group).astype(F32)
    live_ext = jnp.concatenate([flags[0, 0, width : width + PAD].astype(F32), live])[:, None]

    own_conv = lax.dynamic_slice_in_dim(conv_weight, rank * cols, cols, 2)
    own_bias = lax.dynamic_slice_in_dim(beta_bias, rank * own_heads, own_heads, 0)
    chunk_docs = documents.reshape(lanes, width)
    continuing = (chunk_docs == previous[:, None]).reshape(group).astype(F32)
    closing = (chunk_docs == chunk_docs[:, width - 1 :]).reshape(group).astype(F32)
    shared = jnp.stack(
        [valid[:, j] for j in range(margin)] + [continuing, closing, live, documents.astype(F32)], axis=0
    )
    shared = jnp.broadcast_to(shared, (own_heads,) + shared.shape)
    columns = jnp.transpose(shared, (0, 2, 1))

    split = jnp.transpose(projection_weight.reshape(rows, 4, lanes, cols), (2, 0, 1, 3)).reshape(lanes, rows, 4 * cols)
    turned = jnp.tile(w_beta.T.reshape(lanes, own_heads, rows), (1, lanes, 1))
    turned = jnp.pad(turned, ((0, 0), (0, 0), (0, 4 * cols - rows)))
    parts = exchange(jnp.concatenate([split, turned], axis=1), rank)
    (own_rows,) = vmem_call(
        "weights",
        functools.partial(weights_kernel, lanes),
        [shape((lanes * rows + heads, 4 * cols), BF)],
        [at_rank, *parts],
        0,
    )
    w = ring.collect(own_rows, [[packed[-1]], [normed, cot_group, live_ext], [columns, own_conv]])
    cot_all = lax.all_gather(gate(cotangent, w[-1]), BOTH, axis=0, tiled=True)
    projected, w_out, beta_logit, wbeta = project(ring.slots, normed, live_ext, w, lanes)
    sig_beta = jax.nn.sigmoid(beta_logit[PAD:, :own_heads].T + own_bias[:, None])
    beta = sig_beta * live[None]
    row = jnp.concatenate([shared, beta[:, None]], axis=1)
    columns = jnp.concatenate([columns, beta[:, :, None]], axis=2)
    mixer = Mixer(projected, own_conv, columns, row, width)
    head_normed = mixer.outputs(
        jnp.concatenate([at_place, ring.slots]), ring.collect(mixer.whole), head_gain[None]
    )
    w_out = gather_parts(w_out, head_normed)
    heads_low = gather_parts(head_normed)
    feed_rows, *own_feed, own_residual = vmem_call(
        "out",
        functools.partial(out_kernel, lanes),
        [shape((group, model), BF)] + [shape((width // 2, model), BF)] * 2 + [shape((width, model))],
        [by_rank, *heads_low, *w_out, group_tokens, mlp_gain[None]],
        2 * group * model * model,
        scratch=[pltpu.VMEM((group, model), F32)],
    )
    half_rows = width // 2
    feed_halves = [lax.all_gather(x, BOTH, axis=0, tiled=True) for x in own_feed]

    weights = [w_gate, w_up, w_down]
    units = w_gate.shape[1]
    core = (rank % 2).astype(jnp.int32).reshape(1)
    *arrays, kept, sent, kept_result, sent_result = feed_own(
        jnp.concatenate([at_place, core]), feed_rows, cot_group, weights, blocks * group, width
    )
    others = lax.rem(place + 1 + jnp.arange(blocks - 1, dtype=jnp.int32), blocks)
    row_parts = [others[: (blocks + 1) // 2], others[(blocks + 1) // 2 :]]

    def hidden_of(part, held, dep):
        return by_group(
            "feed_hidden", hidden_kernel, part, group, [cot_all], [w_down], [units], held, [dep], 1
        )[::-1]

    kept, arrived, (_, grad_hidden) = scatter_sum(
        kept, sent, rank, lambda sent: hidden_of(row_parts[0], [], sent)
    )

    halves_left = [0, 1]

    def by_halves(x):
        return x.reshape(blocks * lanes, 2, half_rows, x.shape[-1])

    def fill_rows(deps):
        half = halves_left.pop(0)
        *found, token = by_group(
            "feed_rows", rows_kernel, others, lanes * half_rows, [feed_halves[half], by_halves(grad_hidden)],
            weights[:2], [units] * 3, [by_halves(x) for x in arrays], deps, 2, half,
        )
        arrays[:] = [x.reshape(blocks * group, units) for x in found]
        return token

    order = [0, 1, 2]
    ffn_grads = [[], [], []]
    done = [0, 0, 0]

    def fill_grads(parts, dep):
        which = order[0]
        lefts = [cot_all] if which == 2 else feed_halves
        hidden, grad_gate, grad_lifted = arrays
        right = (grad_gate, grad_lifted, hidden)[which]
        right = by_halves(right)
        out, token = weight_grad(done[which], parts, lefts, right, ffn_grads[which], [dep], which == 2)
        ffn_grads[which] = [out]
        done[which] += 1
        if done[which] == parts:
            order.pop(0)
        return token

    grad_residual, grad_mlp_gain, *sent = vmem_call(
        "residual",
        functools.partial(residual_kernel, lanes),
        [shape((width, model)), shape((1, model))] + [shape((width, 2 * cols), BF)] * lanes,
        [by_rank, *w_out, kept, arrived, own_residual, cotangent, mlp_gain[None]],
        2 * width * model * model,
        scratch=[pltpu.VMEM((width, model), BF)],
    )
    by_heads = [swap(x, "ta", j) if j else x for j, x in enumerate(sent)]
    token, grad_hidden = hidden_of(row_parts[1], [grad_hidden], sent[0])
    leak, grad_head_gain, mixed_cols = mixer.leak(at_rank, by_heads, [token])
    beside = swap(leak, "dev", 1)
    pair = jnp.stack([leak, beside])
    pairs = [
        lax.ppermute(pair, "dev", [(i, i - 2 * k) for i in range(2 * k, blocks)]) for k in range(1, blocks // 2)
    ]
    token = fill_rows([pair])
    grad_q, grad_k, grad_v, tail, spill, grad_conv, grad_beta = mixer.back([beside, *pairs], [token])
    arrived = lax.ppermute(spill.astype(BF), "dev", [(i, i - 1) for i in range(1, blocks)])
    grad_logit = grad_beta[:, 0] * beta * (1.0 - sig_beta)
    grad_bias = jnp.sum(grad_logit, axis=1)
    grad_logit_low = jnp.pad(grad_logit.astype(BF), ((0, 8 - own_heads), (0, 0)))

    half = (lanes // 2, 2 * width, model)
    grad_projected, kept, sent, grad_attn_gain = vmem_call(
        "normed_back",
        functools.partial(normed_back_kernel, blocks),
        [shape((group, 3 * cols), BF), shape(half, BF), shape(half, BF), shape((1, model))],
        [jnp.concatenate([core, ring.slots]), *w, grad_q, grad_k, grad_v, tail, arrived]
        + [live[group - PAD :, None], grad_logit_low, wbeta, group_tokens, kept_result, sent_result],
        2 * group * model * 3 * cols,
        scratch=[pltpu.VMEM((group, model), BF)],
    )

    *partial_rows, partial_wbeta = vmem_call(
        "weight_rows",
        functools.partial(weight_rows_kernel, lanes),
        [shape((model // blocks, 4 * cols), BF)] * (blocks - 1)
        + [shape((model // blocks // 2, 4 * cols), BF)] * 2
        + [shape((8, model))],
        [jnp.concatenate([at_rank, ring.slots]), *heads_low, normed_group, grad_projected, mixed_cols]
        + [grad_logit_low],
        2 * group * model * 4 * cols,
        scratch=[pltpu.VMEM((group, model), BF)],
    )
    made = []

    def fill(function, *deps):
        made.append(function(*deps))
        return made[-1]

    terms, deps = ring.scatter(
        partial_rows,
        [
            lambda x: fill(fill_rows, [x]),
            lambda x: fill(fill_grads, 1, x),
            lambda x: fill(fill_grads, 1, x),
            lambda x: fill(fill_grads, 1, x),
        ],
    )
    w_parts = vmem_call("sum", sum_kernel, [shape((rows, 4 * cols), BF)] * lanes, [at_rank, *terms], 0, deps)
    w_parts = [swap(x, "ta", j) if j else x for j, x in enumerate(w_parts)]
    (grad_projection,) = vmem_call(
        "assemble",
        assemble_kernel,
        [shape((rows, 4, model))],
        [at_rank, *w_parts],
        0,
    )

    kept, arrived, _ = scatter_sum(kept, sent, rank, lambda sent: (made[0],))
    block_out, grad_tokens = vmem_call(
        "finish",
        finish_kernel,
        [shape((width, model), BF), shape((width, model))],
        [kept, arrived, own_residual, grad_residual, tokens, attn_gain[None]],
        0,
    )

    own = jnp.concatenate([grad_conv.reshape(-1), partial_wbeta[:own_heads].reshape(-1), grad_bias])
    gains = jnp.concatenate([grad_mlp_gain[0], grad_head_gain[0], grad_attn_gain[0]])
    length = own.shape[0]
    apart = length + (-length % 1024)
    flat = jnp.zeros((lanes, apart), F32)
    flat = lax.dynamic_update_slice(flat, jnp.pad(own, (0, apart - length))[None], (rank, 0))
    flat = jnp.concatenate([flat.reshape(-1, 128), jnp.pad(gains, (0, -gains.shape[0] % 1024)).reshape(-1, 128)])
    flat = gate(lax.psum(flat, BOTH), made[-1]).reshape(-1)
    gains = flat[lanes * apart :]
    flat = flat[: lanes * apart].reshape(lanes, apart)
    convs = 3 * ksize * cols
    conv_sum = jnp.transpose(flat[:, :convs].reshape(lanes, 3, ksize, cols), (1, 2, 0, 3))
    conv_sum = conv_sum.reshape(3, ksize, lanes * cols)
    wbeta_sum = flat[:, convs : convs + own_heads * model].reshape(heads, model)
    grad_w_beta = lax.dynamic_slice_in_dim(wbeta_sum, (place * lanes + rank) * rows, rows, 1).T
    bias_sum = flat[:, convs + own_heads * model : length].reshape(heads)

    (grad_w_gate,), (grad_w_up,), (grad_w_down,) = ffn_grads
    return (
        block_out,
        grad_tokens,
        gains[model + depth : 2 * model + depth],
        grad_projection,
        grad_w_beta,
        bias_sum,
        conv_sum,
        gains[model : model + depth],
        gains[:model],
        grad_w_gate,
        grad_w_up,
        grad_w_down,
    )


def solution(mesh):
    rows = P(BOTH, None)
    three = P(BOTH, None, None)
    return jax.shard_map(
        body,
        mesh=mesh,
        in_specs=(
            rows,
            rows,
            P(),
            P(BOTH),
            P(),
            three,
            rows,
            P(),
            P(),
            P(),
            P(),
            P(None, "ta"),
            P(None, "ta"),
            P("ta", None),
        ),
        out_specs=(
            rows,
            rows,
            P(),
            three,
            rows,
            P(),
            P(),
            P(),
            P(),
            P(None, "ta"),
            P(None, "ta"),
            P("ta", None),
        ),
        check_vma=False,
    )
```

```python
import functools

import jax
import jax.numpy as jnp
from jax import lax
from jax.experimental import pallas as pl
from jax.experimental.pallas import tpu as pltpu
from jax.sharding import PartitionSpec as P

NORM_EPS = 1e-06
HEAD_EPS = 1e-05
UNIT_EPS = 1e-06
BOTH = ("dev", "ta")
BF = jnp.bfloat16
F32 = jnp.float32


def swap(x, axis, bit):
    return lax.ppermute(x, axis, [(i, i ^ bit) for i in range(lax.axis_size(axis))])


def gather_parts(x, *waits):
    parts = [x]
    for j in range(1, lax.axis_size("ta")):
        bit = j & -j
        if waits and j == 2 * bit + bit:
            parts[j ^ bit] = gate(parts[j ^ bit], *waits)
        parts.append(swap(parts[j ^ bit], "ta", bit))
    return parts


def gate(x, *deps):
    return pl.pallas_call(
        lambda *refs: None,
        name="gate",
        out_shape=jax.ShapeDtypeStruct(x.shape, x.dtype),
        in_specs=[pl.BlockSpec(memory_space=pl.ANY)] * (1 + len(deps)),
        out_specs=pl.BlockSpec(memory_space=pl.ANY),
        input_output_aliases={0: 0},
    )(x, *deps)


class Ring:
    def __init__(self):
        n = self.size = lax.axis_size("dev")
        self.last = n // 2
        self.order = list(range(0, n, 2)) + list(range(n - 1, 0, -2))
        self.place = lax.axis_index("dev")
        self.spot = self.spot_of(self.place)
        distances = [0] + [d for s in range(1, self.last) for d in (-s, s)] + [self.last]
        spots = lax.rem(self.spot + n + jnp.array(distances, jnp.int32), n)
        self.slots = jnp.where(2 * spots < n, 2 * spots, 2 * (n - 1 - spots) + 1)
        away = lax.rem(self.spot_of(jnp.arange(n, dtype=jnp.int32)) + n - self.spot, n)
        slot = jnp.where(away < self.last, 2 * away, 2 * (n - away) - 1)
        self.slot_of = jnp.where(away == self.last, n - 1, slot)

    def spot_of(self, index):
        return jnp.where(index % 2 == 0, index // 2, self.size - 1 - index // 2)

    def move(self, x, step):
        n = self.size
        return lax.ppermute(x, "dev", [(self.order[p], self.order[(p + step) % n]) for p in range(n)])

    def collect(self, x, waits=()):
        half = x.shape[0] // 2
        found = [x]
        onward, back = x, x
        for s in range(1, self.last):
            onward, back = self.move(onward, 1), self.move(back, -1)
            if len(waits) >= s and waits[s - 1]:
                onward, back = gate(onward, *waits[s - 1]), gate(back, *waits[s - 1])
            found += [onward, back]
        far = [self.move(onward[:half], 1), self.move(back[half:], -1)]
        return found + [jnp.concatenate(far, axis=0)]

    def scatter(self, blocks, beside=()):
        last = self.last
        beside = list(beside) + [None] * last
        block = lambda d: blocks[0 if d == 0 else 2 * d if d > 0 else -2 * d - 1]
        right, left = blocks[-2:]
        for s in range(last - 1, -1, -1):
            ahead, behind = self.move(right, 1), self.move(left, -1)
            deps = [beside[last - 1 - s](right)] if beside[last - 1 - s] else []
            if s:
                like = [shape(block(s).shape, BF)] * 2
                right, left = vmem_call(
                    "ring_add", ring_add_kernel, like, [block(s), block(-s), ahead, behind], 0, deps
                )
        return [block(0), ahead, behind], deps


def ring_add_kernel(first, second, ahead, behind, right, left):
    rows, part = first.shape[0], ahead.shape[0]
    for block, arrived, out, at in (
        (first, ahead, right, slice(0, part)),
        (second, behind, left, slice(rows - part, rows)),
    ):
        if part < rows:
            out[...] = block[...]
        out[at, :] = (block[at, :].astype(F32) + arrived[...].astype(F32)).astype(BF)


def sum_kernel(rank, x, y, z, *outs):
    rows = outs[0].shape[0]
    for j, out in enumerate(outs):
        at = pl.ds(pl.multiple_of((rank[0] ^ j) * rows, rows), rows)
        out[...] = (x[at, :].astype(F32) + (y[at, :].astype(F32) + z[at, :].astype(F32))).astype(BF)


def assemble_kernel(rank, *refs):
    out, parts = refs[-1], refs[:-1]
    count = out.shape[1]
    cols = parts[0].shape[1] // count
    for j, part in enumerate(parts):
        at = pl.ds(pl.multiple_of((rank[0] ^ j) * cols, cols), cols)
        for i in range(count):
            out[:, i, at] = part[:, i * cols : (i + 1) * cols].astype(F32)


def exchange(blocks, rank):
    parts = []
    for j in range(lax.axis_size("ta")):
        block = lax.dynamic_index_in_dim(blocks, rank ^ j, 0, False)
        parts.append(swap(block, "ta", j) if j else block)
    return parts


def scatter_sum(kept, sent, rank, beside=None):
    lanes = lax.axis_size("ta")
    made = None
    bit = 1
    while True:
        arrived = swap(sent, "ta", bit)
        bit *= 2
        if bit == lanes:
            if beside:
                made = beside(sent)
                arrived = gate(arrived, made[0])
            return kept[0], arrived[0], made
        half = (kept.shape[0] // 2,) + kept.shape[1:]
        mine = ((rank // bit) % 2).astype(jnp.int32).reshape(1)
        kept, sent = vmem_call("stage", stage_kernel, [shape(half), shape(half, BF)], [mine, kept, arrived], 0)


def stage_kernel(mine, first, second, kept, sent):
    for n in range(kept.shape[0]):
        for out, which in ((kept, mine[0]), (sent, 1 - mine[0])):
            at = 2 * n + which
            out[n] = (first[at].astype(F32) + second[at].astype(F32)).astype(out.dtype)


def rms_scale(values, gain):
    return values * lax.rsqrt(jnp.mean(values * values, axis=-1, keepdims=True) + NORM_EPS) * gain


def document_of(lengths, positions):
    starts = jnp.cumsum(lengths) - lengths
    above = (starts[None, :] <= positions[:, None]).astype(jnp.int32)
    return jnp.sum(above, axis=1) - 1


def contract_rows(left, right):
    return lax.dot_general(left, right, (((0,), (0,)), ((), ())), preferred_element_type=F32)


def contract_cols(left, right):
    return lax.dot_general(left, right, (((1,), (1,)), ((), ())), preferred_element_type=F32)


def dot(left, right):
    return jnp.dot(left, right, preferred_element_type=F32)


PAD = 8
HEADS_A_STEP = 2
VMEM_LIMIT = 48 * 1024 * 1024
FFN_VMEM = 56 * 1024 * 1024


def dims(a, b, ca, cb):
    return lax.dot_general(a, b, (((ca,), (cb,)), ((), ())), preferred_element_type=F32)


def d1(a, b, ca=1, cb=0):
    return dims(a.astype(BF), b.astype(BF), ca, cb)


def parts_of(a):
    high = a.astype(BF)
    return high, (a - high.astype(F32)).astype(BF)


def d3(a, b, ca=1, cb=0):
    ah, al = parts_of(a)
    bh, bl = parts_of(b)
    return dims(ah, bh, ca, cb) + (dims(ah, bl, ca, cb) + dims(al, bh, ca, cb))


def iotas(size):
    return (
        lax.broadcasted_iota(jnp.int32, (size, size), 0),
        lax.broadcasted_iota(jnp.int32, (size, size), 1),
    )


def inverses_of(lowers):
    size = lowers[0].shape[0]
    row, col = iotas(size)
    eye = (row == col).astype(F32)
    pair = (row // 2 == col // 2).astype(F32)
    found = [eye - low * pair for low in lowers]
    block = 2
    while block < size:
        joint = ((row // (2 * block) == col // (2 * block)) & (row // block != col // block)).astype(F32)
        steps = [d1(low * joint, x) for low, x in zip(lowers, found)]
        found = [x - d1(x, s) for x, s in zip(found, steps)]
        block *= 2
    errors = [d3(low, x) + (x - eye) for low, x in zip(lowers, found)]
    return [x - d1(x, e) for x, e in zip(found, errors)]


def unit_of(active):
    scale = lax.rsqrt(jnp.sum(active * active, axis=-1, keepdims=True) + UNIT_EPS)
    return active * scale, scale


def masks_of(aux, row, at, size):
    doc, doc_row = aux[at, 6:7], row[6:7, at]
    r, c = iotas(size)
    same = doc == doc_row
    weak = (same & (r >= c)).astype(F32)
    strict = (same & (r > c)).astype(F32)
    return weak, strict


def forward_kernel(size, xq, xk, xv, conv, aux_ref, row_ref, yq, yk, yv, inv, plain, reach, read, direct, trans, fresh, whole):
    heads, count = inv.shape[0], inv.shape[1]
    depth = xq.shape[1] // heads
    ksize = conv.shape[1]
    r, c = iotas(depth)
    eye = (r == c).astype(F32)
    spans = [slice(n * size, (n + 1) * size) for n in range(count)]
    saved = []
    lowers = []
    for h in range(heads):
        aux, row = aux_ref.at[h], row_ref.at[h]
        col = slice(h * depth, (h + 1) * depth)
        for n, at in enumerate(spans):
            active = []
            for i, (x, y) in enumerate(((xq, yq), (xk, yk), (xv, yv))):
                first = PAD - (ksize - 1) + n * size
                summed = x[first + ksize - 1 : first + ksize - 1 + size, col] * conv[i, ksize - 1 : ksize, col]
                for j in range(ksize - 1):
                    moved = x[first + j : first + j + size, col]
                    summed = summed + moved * conv[i, j : j + 1, col] * aux[at, j : j + 1]
                y[at, col] = summed
                active.append(summed * jax.nn.sigmoid(summed))
            q = unit_of(active[0])[0] * depth ** (-0.5)
            k = unit_of(active[1])[0]
            weak, strict = masks_of(aux, row, at, size)
            rate = row[7:8, at]
            products = d3(jnp.concatenate([q, k], axis=0), k, 1, 1)
            lowers.append(products[size:] * rate * strict)
            saved.append((h, n, q, k, active[2], products[:size] * rate * weak))
    inverses = inverses_of(lowers)
    total, added = [None] * heads, [None] * heads
    for inverse, (h, n, q, k, v, mix) in zip(inverses, saved):
        at = spans[n]
        aux = aux_ref.at[h]
        cont, clos, beta = aux[at, 3:4], aux[at, 4:5], aux[at, 7:8]
        both = d3(inverse, jnp.concatenate([v, k * cont], axis=1))
        spread = d1(mix, both)
        inv[h, n] = inverse
        plain[h, at, :] = both[:, :depth]
        reach[h, at, :] = both[:, depth:]
        direct[h, at, :] = spread[:, :depth]
        read[h, at, :] = q * cont - spread[:, depth:]
        gained = d3(k * (beta * clos), both, 0, 0)
        map_n = aux[(n + 1) * size - 1 : (n + 1) * size, 3:4] * eye - gained[:, depth:]
        add_n = gained[:, :depth]
        trans[h, n] = map_n
        fresh[h, n] = add_n
        if n == 0:
            total[h], added[h] = map_n, add_n
        else:
            new = d3(map_n, jnp.concatenate([added[h], total[h]], axis=1))
            total[h], added[h] = new[:, depth:], new[:, :depth] + add_n
    for h in range(heads):
        whole[h, 0] = total[h].astype(BF)
        whole[h, 1] = added[h].astype(BF)


def read_kernel(size, count_of, index, *refs):
    parts, refs = refs[:count_of], refs[count_of:]
    trans, fresh, read, direct, gain, both, states, outputs, normed = refs
    heads, count = trans.shape[0], trans.shape[1]
    depth = trans.shape[-1]
    for n, part in enumerate(parts):
        both[index[1 + n]] = part[...]

    def earlier(i, carry):
        return tuple(
            d3(both[i, h, 0].astype(F32), carry[h]) + both[i, h, 1].astype(F32) for h in range(heads)
        )

    carry = lax.fori_loop(0, index[0], earlier, tuple(jnp.zeros((depth, depth), F32) for _ in range(heads)))
    carry = list(carry)
    for n in range(count):
        at = slice(n * size, (n + 1) * size)
        for h in range(heads):
            state = carry[h]
            states[h, n] = state
            out = direct[h, at, :] + d3(read[h, at, :], state)
            cols = slice(h * depth, (h + 1) * depth)
            outputs[at, cols] = out
            scale = lax.rsqrt(jnp.mean(out * out, axis=-1, keepdims=True) + HEAD_EPS)
            normed[at, cols] = (out * scale * gain[...]).astype(BF)
            if n < count - 1:
                carry[h] = d3(trans[h, n], state) + fresh[h, n]


def leak_kernel(size, lanes, rank, *refs):
    parts, refs = refs[:lanes], refs[lanes:]
    outputs, gain, read, trans, grad_out, from_out, leak, grad_gain, mixed, grads = refs
    heads, count = trans.shape[0], trans.shape[1]
    depth = trans.shape[-1]
    for j, part in enumerate(parts):
        at = pl.ds(pl.multiple_of((rank[0] ^ j) * size, size), size)
        grads[at, :] = part[:, : heads * depth]
        mixed[at, :] = part[:, heads * depth :]
    gained = jnp.zeros((1, depth), F32)
    totals = [None] * heads
    for n in range(count - 1, -1, -1):
        at = slice(n * size, (n + 1) * size)
        for h in range(heads):
            cols = slice(h * depth, (h + 1) * depth)
            out, grad = outputs[at, cols], grads[at, cols].astype(F32)
            scale = lax.rsqrt(jnp.mean(out * out, axis=-1, keepdims=True) + HEAD_EPS)
            unit = out * scale
            gained = gained + jnp.sum(grad * unit, axis=0, keepdims=True)
            grad = grad * gain[...]
            grad = scale * (grad - unit * jnp.mean(grad * unit, axis=-1, keepdims=True))
            grad_out[h, at, :] = grad
            term = d3(read[h, at, :], grad, 0, 0)
            from_out[h, n] = term
            totals[h] = term if n == count - 1 else d3(trans[h, n], totals[h], 0, 0) + term
    for h in range(heads):
        leak[h] = totals[h].astype(BF)
    grad_gain[...] = gained


def chain_kernel(index, beside, *refs):
    both, trans, from_out, grads = refs[-4:]
    pairs = refs[:-4]
    heads, count = trans.shape[0], trans.shape[1]
    depth = trans.shape[-1]
    devices = both.shape[0]
    odd = index[0] % 2
    carry = [jnp.zeros((depth, depth), F32) for _ in range(heads)]

    def follow(at, leak):
        at = jnp.minimum(at, devices - 1)
        return [d3(both[at, h, 0].astype(F32), carry[h], 0, 0) + leak(h).astype(F32) for h in range(heads)]

    for k in range(len(pairs), 0, -1):
        pair = pairs[k - 1]
        first = index[0] - odd + 2 * k
        carry = follow(first + 1, lambda h: pair[1 - odd, h])
        carry = follow(first, lambda h: pair[odd, h])
    later = follow(index[0] + 1, lambda h: beside[h])
    carry = [jnp.where(odd == 0, x, y) for x, y in zip(later, carry)]
    for n in range(count - 1, -1, -1):
        for h in range(heads):
            grads[h, n] = carry[h]
            if n:
                carry[h] = d3(trans[h, n], carry[h], 0, 0) + from_out[h, n]


def backward_kernel(size, xq, xk, xv, yq, yk, yv, conv, aux_ref, row_ref, inv, plain, reach, states, grads, grad_out,
                    gq, gk, gv, tail, spill, grad_conv, grad_beta, zs):
    count = inv.shape[1]
    depth = xq.shape[1]
    ksize = conv.shape[1]
    aux, row = aux_ref.at[0], row_ref.at[0]
    length = count * size
    scale_q = depth ** (-0.5)
    for n in range(count):
        at = slice(n * size, (n + 1) * size)
        cont, clos, beta = aux[at, 3:4], aux[at, 4:5], aux[at, 7:8]
        weak, strict = masks_of(aux, row, at, size)
        rate = row[7:8, at]
        ys = [yq[at, :], yk[at, :], yv[at, :]]
        sigs = [jax.nn.sigmoid(y) for y in ys]
        uq, rq = unit_of(ys[0] * sigs[0])
        k, rk = unit_of(ys[1] * sigs[1])
        q = uq * scale_q
        products = d1(jnp.concatenate([q, k], axis=0), k, 1, 1)
        qk, kk = products[:size], products[size:]
        mix = qk * rate * weak
        state, grad_state, dout = states[0, n], grads[0, n], grad_out[0, at, :]
        u = plain[0, at, :] - d1(reach[0, at, :], state)
        kds = d1(k, grad_state)
        written = beta * clos
        du = d1(mix, dout, 0, 0) + written * kds
        dr = d1(inv[0, n], du, 0, 0)
        pair = jnp.concatenate([dout, dr], axis=0)
        outer = d1(pair, u, 1, 1)
        through = d1(pair, state, 1, 1)
        dp = outer[:size] * weak
        dl = -outer[size:] * strict
        per_key = jnp.sum(dp * qk + dl * kk, axis=0, keepdims=True)
        per_state = jnp.sum((kds * u).T, axis=0, keepdims=True)
        grad_beta[0, :, at] = per_key + row[4:5, at] * per_state
        dqk = dp * rate
        da = dl * rate
        dq = cont * through[:size] + d1(dqk, k)
        dk = d1(dqk, q, 0, 0) + written * d1(u, grad_state, 1, 1) - cont * through[size:] + d1(da + da.T, k)
        dq = dq * scale_q
        acts = [
            rq * (dq - uq * jnp.sum(uq * dq, axis=-1, keepdims=True)),
            rk * (dk - k * jnp.sum(k * dk, axis=-1, keepdims=True)),
            dr,
        ]
        for i, x in enumerate((xq, xk, xv)):
            dy = acts[i] * sigs[i] * (1.0 + ys[i] * (1.0 - sigs[i]))
            first = PAD - (ksize - 1) + n * size
            for j in range(ksize):
                dv = dy if j == ksize - 1 else dy * aux[at, j : j + 1]
                term = jnp.sum(dv * x[first + j : first + j + size, :], axis=0, keepdims=True)
                before = jnp.zeros_like(term) if n == 0 else grad_conv[i, j : j + 1, :]
                grad_conv[i, j : j + 1, :] = before + term
                zs[i, j, PAD + n * size : PAD + (n + 1) * size, :] = dv * conv[i, j : j + 1, :]
    for i, g in enumerate((gq, gk, gv)):
        for j in range(ksize):
            zs[i, j, 0:PAD, :] = jnp.zeros((PAD, depth), F32)
            zs[i, j, PAD + length : 2 * PAD + length, :] = jnp.zeros((PAD, depth), F32)

        def shifted_sum(first, rows):
            return sum(zs[i, j, first + ksize - 1 - j : first + ksize - 1 - j + rows, :] for j in range(ksize))

        for n in range(count):
            at = slice(n * size, (n + 1) * size)
            g[at, :] = (shifted_sum(PAD + n * size, size) * aux[at, 5:6]).astype(BF)
        tail[i] = shifted_sum(length, PAD)
        spill[i] = shifted_sum(0, PAD)


def vmem_call(name, kernel, out_shape, inputs, flops, deps=(), scratch=()):
    smem, vmem = (pl.BlockSpec(memory_space=m) for m in (pltpu.SMEM, pltpu.VMEM))

    def run(*refs):
        kernel(*refs[: len(inputs)], *refs[len(inputs) + len(deps) :])

    return pl.pallas_call(
        run,
        name=name,
        out_shape=out_shape,
        in_specs=[smem if x.dtype == jnp.int32 else vmem for x in inputs]
        + [pl.BlockSpec(memory_space=pl.ANY)] * len(deps),
        out_specs=[vmem] * len(out_shape),
        scratch_shapes=list(scratch),
        cost_estimate=cost(flops, inputs, out_shape),
        compiler_params=pltpu.CompilerParams(vmem_limit_bytes=FFN_VMEM),
    )(*inputs, *deps)


def cost(flops, inputs, outputs):
    moved = sum(x.size * x.dtype.itemsize for x in list(inputs) + list(outputs))
    return pl.CostEstimate(flops=int(flops), bytes_accessed=int(moved), transcendentals=0)


def shape(dims, dtype=F32):
    return jax.ShapeDtypeStruct(dims, dtype)


class Mixer:
    def __init__(self, projected, own_conv, aux, row, size):
        self.size = size
        self.heads, self.length = aux.shape[0], aux.shape[1]
        self.depth = own_conv.shape[2] // self.heads
        self.count = self.length // size
        self.projected, self.conv, self.aux, self.row = projected, own_conv, aux, row
        heads, length, depth, count = self.heads, self.length, self.depth, self.count
        ksize = own_conv.shape[1]
        self.token_specs = [
            pl.BlockSpec((length + PAD, depth), lambda h, i=i: (0, i * heads + h)) for i in range(3)
        ]
        self.head_cols = pl.BlockSpec((length, depth), lambda h: (0, h))
        self.conv_spec = pl.BlockSpec((3, ksize, depth), lambda h: (0, 0, h))
        self.aux_specs = [
            pl.BlockSpec((1, length, 8), lambda h: (h, 0, 0)),
            pl.BlockSpec((1, 8, length), lambda h: (h, 0, 0)),
        ]
        self.chunk_spec = pl.BlockSpec((1, count, depth, depth), lambda h: (h, 0, 0, 0))
        self.inv_spec = pl.BlockSpec((1, count, size, size), lambda h: (h, 0, 0, 0))
        self.rows_spec = pl.BlockSpec((1, length, depth), lambda h: (h, 0, 0))
        self.flops = 2 * heads * count * size * depth * depth
        inputs = [projected] * 3 + [own_conv, aux, row]
        square = shape((heads, count, depth, depth))
        tokens = shape((heads, length, depth))
        out_shape = (
            [shape((length, heads * depth))] * 3
            + [shape((heads, count, size, size))]
            + [tokens] * 4
            + [square] * 2
            + [shape((heads, 2, depth, depth), BF)]
        )
        step = HEADS_A_STEP if heads % HEADS_A_STEP == 0 else 1
        each = lambda x: pl.BlockSpec((step,) + x.shape[1:], lambda h: (h,) + (0,) * (len(x.shape) - 1))
        column = pl.BlockSpec((length, step * depth), lambda h: (0, h))
        (
            self.yq, self.yk, self.yv, self.inv, self.plain, self.reach, self.read, self.direct,
            self.trans, self.fresh, self.whole,
        ) = pl.pallas_call(
            functools.partial(forward_kernel, size),
            name="mixer_forward",
            out_shape=out_shape,
            grid=(heads // step,),
            in_specs=[
                pl.BlockSpec((length + PAD, step * depth), lambda h, i=i: (0, i * (heads // step) + h))
                for i in range(3)
            ]
            + [pl.BlockSpec((3, ksize, step * depth), lambda h: (0, 0, h)), each(aux), each(row)],
            out_specs=[column] * 3 + [each(x) for x in out_shape[3:]],
            cost_estimate=cost(60 * self.flops, inputs, out_shape),
            compiler_params=pltpu.CompilerParams(vmem_limit_bytes=VMEM_LIMIT),
        )(*inputs)

    def outputs(self, index, parts, head_gain):
        heads, length, depth, count = self.heads, self.length, self.depth, self.count
        self.index, self.gain = index, head_gain
        self.both, self.states, self.out, normed = vmem_call(
            "mixer_read",
            functools.partial(read_kernel, self.size, len(parts)),
            [
                shape((len(parts),) + parts[0].shape, BF),
                shape((heads, count, depth, depth)),
                shape((length, heads * depth)),
                shape((length, heads * depth), BF),
            ],
            [index, *parts, self.trans, self.fresh, self.read, self.direct, head_gain],
            12 * self.flops,
        )
        return normed

    def leak(self, rank, parts, deps=()):
        heads, length, depth, count = self.heads, self.length, self.depth, self.count
        self.grad_out, self.from_out, leak, grad_gain, mixed = vmem_call(
            "mixer_leak",
            functools.partial(leak_kernel, self.size, len(parts)),
            [
                shape((heads, length, depth)),
                shape((heads, count, depth, depth)),
                shape((heads, depth, depth), BF),
                shape((1, depth)),
                shape((length, heads * depth), BF),
            ],
            [rank, *parts, self.out, self.gain, self.read, self.trans],
            6 * self.flops,
            deps,
            scratch=[pltpu.VMEM((length, heads * depth), BF)],
        )
        return leak, grad_gain, mixed

    def back(self, leaks, deps=()):
        heads, length, depth, count = self.heads, self.length, self.depth, self.count
        ksize = self.conv.shape[1]
        (grads,) = vmem_call(
            "mixer_chain",
            chain_kernel,
            [shape((heads, count, depth, depth))],
            [self.index, *leaks, self.both, self.trans, self.from_out],
            6 * self.flops,
            deps,
        )
        inputs = [self.projected] * 3 + [self.yq, self.yk, self.yv, self.conv, self.aux, self.row]
        inputs += [self.inv, self.plain, self.reach, self.states, grads, self.grad_out]
        edge = shape((3, PAD, heads * depth))
        out_shape = [shape((length, heads * depth), BF)] * 3 + [edge] * 2
        out_shape += [shape((3, ksize, heads * depth)), shape((heads, 1, length))]
        edge_spec = pl.BlockSpec((3, PAD, depth), lambda h: (0, 0, h))
        return pl.pallas_call(
            functools.partial(backward_kernel, self.size),
            name="mixer_backward",
            out_shape=out_shape,
            grid=(heads,),
            in_specs=self.token_specs
            + [self.head_cols] * 3
            + [self.conv_spec]
            + self.aux_specs
            + [self.inv_spec, self.rows_spec, self.rows_spec, self.chunk_spec, self.chunk_spec, self.rows_spec],
            out_specs=[self.head_cols] * 3
            + [edge_spec] * 2
            + [self.conv_spec, pl.BlockSpec((1, 1, length), lambda h: (h, 0, 0))],
            scratch_shapes=[pltpu.VMEM((3, ksize, length + 2 * PAD, depth), F32)],
            cost_estimate=cost(30 * self.flops, inputs, out_shape),
            compiler_params=pltpu.CompilerParams(vmem_limit_bytes=VMEM_LIMIT),
        )(*inputs)


ANY = pl.BlockSpec(memory_space=pl.ANY)
TOKEN = shape((8, 128))


def resident(x):
    return pl.BlockSpec(x.shape, lambda *_: (0,) * x.ndim, pipeline_mode=pl.Buffered(1))


def activations(gate, lifted, grad_hidden):
    sig = jax.nn.sigmoid(gate)
    swish = gate * sig
    return (
        (swish * lifted).astype(BF),
        (grad_hidden * lifted * sig * (1.0 + gate * (1.0 - sig))).astype(BF),
        (grad_hidden * swish).astype(BF),
    )


def chunks_of(size, chunk=256):
    return [slice(at, min(at + chunk, size)) for at in range(0, size, chunk)]


def params(flops, moved):
    return dict(
        cost_estimate=pl.CostEstimate(flops=int(flops), bytes_accessed=int(moved), transcendentals=0),
        compiler_params=pltpu.CompilerParams(vmem_limit_bytes=FFN_VMEM),
    )


TOKEN_SPEC = pl.BlockSpec((8, 128), lambda *_: (0, 0))


def split_by_core(source, core, width, kept, sent):
    for p in range(kept.shape[0]):
        for ref, which in ((kept, core), (sent, 1 - core)):
            ref[p, 0:width, :] = source[pl.ds(pl.multiple_of((2 * p + which) * width, width), width), :]


def first_step(act):
    pl.when(pl.program_id(0) == 0)(act)


def own_kernel(index, feed, cot, wg, wu_source, wd_source, hidden, grad_gate, grad_lifted, *refs):
    (kept, sent, kept_result, sent_result), (total, result, wu, wd, sems) = refs[:4], refs[4:]
    up, down = (
        pltpu.make_async_copy(source, held, sems.at[n])
        for n, (source, held) in enumerate(((wu_source, wu), (wd_source, wd)))
    )
    first_step(up.start)
    first_step(down.start)
    model = wd.shape[1]
    gated = jnp.dot(feed[...], wg[...], preferred_element_type=F32)
    first_step(up.wait)
    lifted = jnp.dot(feed[...], wu[...], preferred_element_type=F32)
    first_step(down.wait)
    grad_hidden = dims(cot[...], wd[...], 1, 1)
    hidden[...], grad_gate[...], grad_lifted[...] = activations(gated, lifted, grad_hidden)
    for cut in chunks_of(model):
        grad_feed = dims(grad_gate[...], wg[cut, :], 1, 1) + dims(grad_lifted[...], wu[cut, :], 1, 1)
        total[:, cut] = grad_feed.astype(BF)
        result[:, cut] = jnp.dot(hidden[...], wd[:, cut], preferred_element_type=F32).astype(BF)
    split_by_core(total, index[1], kept.shape[1], kept, sent)
    split_by_core(result, index[1], kept.shape[1], kept_result, sent_result)


def hidden_kernel(groups, cot, wd, *refs):
    out, token = refs[-2:]
    out[...] = dims(cot[...], wd[...], 1, 1).astype(BF)
    token[...] = jnp.zeros_like(token)


def rows_kernel(groups, feed, grad_hidden, wg, wu, *refs):
    *outs, token = refs[-4:]
    before = grad_hidden[...].reshape(feed.shape[0], -1)
    gated = jnp.dot(feed[...], wg[...], preferred_element_type=F32)
    lifted = jnp.dot(feed[...], wu[...], preferred_element_type=F32)
    for out, value in zip(outs, activations(gated, lifted, before.astype(F32))):
        out[...] = value.reshape(out.shape)
    token[...] = jnp.zeros_like(token)


def by_group(name, kernel, groups, size, inputs, weights, outs, held, deps, products, half=0):
    like = inputs[-1].shape
    count = groups.shape[0]

    def picked(x, width):
        if x.ndim == 2:
            return pl.BlockSpec((size, width), lambda i, g: (g[i], 0))
        return pl.BlockSpec((size // like[2], 1, like[2], width), lambda i, g: (g[i], half, 0, 0))

    first = 1 + len(inputs) + len(weights) + len(deps)
    return pl.pallas_call(
        kernel,
        name=name,
        out_shape=[shape(like[:-1] + (width,), BF) for width in outs] + [TOKEN],
        grid_spec=pltpu.PrefetchScalarGridSpec(
            num_scalar_prefetch=1,
            grid=(count,),
            in_specs=[picked(x, x.shape[-1]) for x in inputs]
            + [resident(w) for w in weights]
            + [ANY] * (len(deps) + len(held)),
            out_specs=[picked(inputs[-1], width) for width in outs] + [TOKEN_SPEC],
        ),
        input_output_aliases={first + n: n for n in range(len(held))},
        **params(
            2 * count * size * weights[0].size * products,
            sum(w.size for w in weights) * 2 + count * size * 2 * (sum(outs) + sum(x.shape[-1] for x in inputs)),
        ),
    )(groups, *inputs, *weights, *deps, *held)


def feed_own(index, feed, cot, weights, tokens, width):
    rows, model = feed.shape
    units = weights[0].shape[1]
    block = 2 * width
    count = rows // block
    wide = pl.BlockSpec((block, units), lambda i, g: (g[0] * count + i, 0))
    here = pl.BlockSpec((block, model), lambda i, g: (i, 0))
    half = pl.BlockSpec((1, width, model), lambda i, g: (i, 0, 0))
    return pl.pallas_call(
        own_kernel,
        name="feed_own",
        out_shape=[shape((tokens, units), BF)] * 3
        + [shape((count, width, model), BF)] * 4,
        grid_spec=pltpu.PrefetchScalarGridSpec(
            num_scalar_prefetch=1,
            grid=(count,),
            in_specs=[here] * 2 + [resident(weights[0])] + [ANY] * 2,
            out_specs=[wide] * 3 + [half] * 4,
            scratch_shapes=[pltpu.VMEM((block, model), BF)] * 2
            + [pltpu.VMEM(w.shape, w.dtype) for w in weights[1:]]
            + [pltpu.SemaphoreType.DMA((2,))],
        ),
        **params(12 * rows * model * units, 6 * model * units + rows * (3 * units + 4 * model) * 2),
    )(index, feed, cot, *weights)


GRAD_COLS = 256


def grad_kernel(transposed, count, *refs):
    lefts, right = refs[:count], refs[count]
    out, token = refs[-2:]
    units = right.shape[-1]
    if count == 1:
        term = dims(lefts[0][...], right[...].reshape(-1, units), 0, 0)
    else:
        term = sum(dims(left[...], right[:, n].reshape(-1, units), 0, 0) for n, left in enumerate(lefts))
    out[...] = term.T if transposed else term
    token[...] = jnp.zeros_like(token)


def weight_grad(part, parts, lefts, right, held, deps, transposed):
    rows, model = lefts[0].shape
    units = right.shape[-1]
    count = model // GRAD_COLS // parts
    if transposed:
        out_spec = pl.BlockSpec((units, GRAD_COLS), lambda m: (0, part * count + m))
    else:
        out_spec = pl.BlockSpec((GRAD_COLS, units), lambda m: (part * count + m, 0))
    first = len(lefts) + 1 + len(deps)
    tokens = rows * len(lefts)
    return pl.pallas_call(
        functools.partial(grad_kernel, transposed, len(lefts)),
        name="weight_grad",
        out_shape=[shape((units, model) if transposed else (model, units)), TOKEN],
        grid=(count,),
        in_specs=[pl.BlockSpec((rows, GRAD_COLS), lambda m: (0, part * count + m))] * len(lefts)
        + [resident(right)]
        + [ANY] * (len(deps) + len(held)),
        out_specs=[out_spec, TOKEN_SPEC],
        input_output_aliases={first + n: n for n in range(len(held))},
        **params(
            2 * tokens * count * GRAD_COLS * units,
            2 * tokens * (units + count * GRAD_COLS) + 4 * count * GRAD_COLS * units,
        ),
    )(*lefts, right, *deps, *held)


def order_kernel(rank, *refs):
    out = refs[-1]
    size = refs[0].shape[0]
    for j, part in enumerate(refs[:-1]):
        out[pl.ds(pl.multiple_of((rank[0] ^ j) * size, size), size), :] = part[...]


def in_order(parts, rank):
    rows, width = parts[0].shape
    return vmem_call(
        "in_order", order_kernel, [shape((rows * len(parts), width), parts[0].dtype)], [rank, *parts], 0
    )[0]


def norm_kernel(width, rank, *refs):
    gain, group, normed, extended, live = refs[-5:]
    parts = refs[:-5]

    def scaled(values):
        values = values.astype(F32)
        scale = lax.rsqrt(jnp.mean(values * values, axis=-1, keepdims=True) + NORM_EPS)
        return (values * scale * gain[...]).astype(BF)

    for j, part in enumerate(parts):
        at = rank[0] ^ j
        rows = part[0:width, :]
        group[pl.ds(pl.multiple_of(at * width, width), width), :] = rows
        rows = scaled(rows)
        normed[pl.ds(pl.multiple_of(at * width, width), width), :] = rows
        extended[pl.ds(pl.multiple_of(PAD + at * width, PAD), width), :] = rows
        live[at] = part[width : width + 8, 0 : 2 * width]

        @pl.when(at == 0)
        def _():
            extended[0:PAD, :] = scaled(part[width + 8 : width + 8 + PAD, :])


def weights_kernel(lanes, rank, *refs):
    out, parts = refs[-1], refs[:-1]
    rows = out.shape[0] - parts[0].shape[0]
    rows = rows // (lanes - 1)
    heads = parts[0].shape[0] - rows
    mine = lax.broadcasted_iota(jnp.int32, (heads, 128), 0) // (heads // lanes)
    tile = jnp.zeros((heads, 128), F32)
    for j, part in enumerate(parts):
        at = rank[0] ^ j
        out[pl.ds(pl.multiple_of(at * rows, rows), rows), :] = part[0:rows, :]
        tile = jnp.where(mine == at, part[rows:, 0:128].astype(F32), tile)
    out[lanes * rows :, :] = jnp.zeros((heads, out.shape[1]), BF)
    out[lanes * rows :, 0:128] = tile.astype(BF)


def project_kernel(lanes, slots, x, live, *refs):
    out, out_w, logit, wbeta = refs[-4:]
    parts, last = refs[: len(refs) // 2 - 2], refs[len(refs) // 2 - 2 : -4]
    size = out_w.shape[0] // len(parts)
    heads = parts[0].shape[0] - size
    own = heads // lanes
    total = None
    for n, part in enumerate(parts):
        at = pl.ds(pl.multiple_of(slots[n] * size, size), size)
        term = jnp.dot(x[:, at], part[0:size, :], preferred_element_type=F32)
        total = term if total is None else total + term
    out[...] = total * live[...]

    @pl.when(pl.program_id(0) == 0)
    def _():
        each = size // lanes
        row = lax.broadcasted_iota(jnp.int32, (heads, size), 0)
        col = lax.broadcasted_iota(jnp.int32, (heads, size), 1)
        own_row = lax.broadcasted_iota(jnp.int32, (8, heads), 0)
        own_col = lax.broadcasted_iota(jnp.int32, (8, heads), 1)
        picked = ((own_col % own == own_row) & (own_row < own)).astype(BF)
        for n, (part, columns) in enumerate(zip(parts, last)):
            out_w[n * size : (n + 1) * size, :] = columns[0:size, :]
            tile = jnp.concatenate([part[size:, 0:each]] * lanes, axis=1)
            tile = jnp.where(col // each == row // own, tile.astype(F32), 0.0).astype(BF)
            at = pl.ds(pl.multiple_of(slots[n] * size, size), size)
            wbeta[:, at] = jnp.dot(picked, tile, preferred_element_type=F32).astype(BF)
        logit[...] = dims(x[...], wbeta[...], 1, 1)


def project(slots, x, live, parts, lanes):
    rows, model = x.shape
    size, width = parts[0].shape
    cols = width // 4
    whole = lambda a: pl.BlockSpec(a.shape, lambda i, s: (0,) * len(a.shape))
    outs = [shape((rows, 3 * cols)), shape((model, cols), BF), shape((rows, 8)), shape((8, model), BF)]
    return pl.pallas_call(
        functools.partial(project_kernel, lanes),
        name="project",
        out_shape=outs,
        grid_spec=pltpu.PrefetchScalarGridSpec(
            num_scalar_prefetch=1,
            grid=(3,),
            in_specs=[whole(x), whole(live)]
            + [pl.BlockSpec((size, cols), lambda i, s: (0, i))] * len(parts)
            + [pl.BlockSpec((size, cols), lambda i, s: (0, 3))] * len(parts),
            out_specs=[pl.BlockSpec((rows, cols), lambda i, s: (0, i))] + [whole(a) for a in outs[1:]],
        ),
        **params(6 * rows * model * cols, 2 * x.size + 8 * model * cols),
    )(slots, x, live, *parts, *parts)


def finish_kernel(kept, arrived, residual, grad_residual, tokens, gain, block_out, grad_tokens):
    width = tokens.shape[0]
    both = kept[...].astype(F32) + arrived[...].astype(F32)
    block_out[...] = (residual[...] + both[width:]).astype(BF)
    values = tokens[...].astype(F32)
    scale = lax.rsqrt(jnp.mean(values * values, axis=-1, keepdims=True) + NORM_EPS)
    unit = values * scale
    grad = both[:width] * gain[...]
    grad_tokens[...] = grad_residual[...] + scale * (
        grad - unit * jnp.mean(grad * unit, axis=-1, keepdims=True)
    )


def out_kernel(lanes, index, *refs):
    heads, w, refs = refs[:lanes], refs[lanes : 2 * lanes], refs[2 * lanes :]
    tokens, gain, feed, *own_feed, own_residual, total = refs
    rank = index[0]
    width = own_residual.shape[0]
    cols = heads[0].shape[1]
    blocks = w[0].shape[0]
    size = w[0].shape[0] // (index.shape[0] - 1)
    per = cols // size
    for j in range(lanes):
        acc = None
        for i in range(lanes):
            for p in range(per):
                slot = index[1 + (rank ^ i) * per + p]
                rows = w[j][pl.ds(pl.multiple_of(slot * size, size), size), :]
                term = jnp.dot(heads[i][:, p * size : (p + 1) * size], rows, preferred_element_type=F32)
                acc = term if acc is None else acc + term
        at = pl.ds(pl.multiple_of((rank ^ j) * cols, cols), cols)
        total[:, at] = tokens[:, at].astype(F32) + acc
    for n in range(lanes):
        at = slice(n * width, (n + 1) * width)
        values = total[at, :]
        scale = lax.rsqrt(jnp.mean(values * values, axis=-1, keepdims=True) + NORM_EPS)
        feed[at, :] = (values * scale * gain[...]).astype(BF)
    own = pl.ds(pl.multiple_of(rank * width, width), width)
    own_residual[...] = total[own, :]
    for n, out in enumerate(own_feed):
        out[...] = feed[pl.ds(pl.multiple_of(rank * width + n * (width // 2), width // 2), width // 2), :]


def residual_kernel(lanes, index, *refs):
    w, refs = refs[:lanes], refs[lanes:]
    kept, arrived, residual, cot, gain, grad_residual, grad_gain = refs[:7]
    sent, mixed = refs[7 : 7 + lanes], refs[7 + lanes]
    rank = index[0]
    cols = w[0].shape[1]
    size = w[0].shape[0] // (index.shape[0] - 1)
    per = cols // size
    grad = kept[...].astype(F32) + arrived[...].astype(F32)
    values = residual[...]
    scale = lax.rsqrt(jnp.mean(values * values, axis=-1, keepdims=True) + NORM_EPS)
    unit = values * scale
    grad_gain[...] = jnp.sum(grad * unit, axis=0, keepdims=True)
    grad = grad * gain[...]
    grad = cot[...].astype(F32) + scale * (grad - unit * jnp.mean(grad * unit, axis=-1, keepdims=True))
    grad_residual[...] = grad
    mixed[...] = grad.astype(BF)
    columns = [pl.ds(pl.multiple_of((rank ^ j) * cols, cols), cols) for j in range(lanes)]
    for j in range(lanes):
        for p in range(per):
            slot = index[1 + (rank ^ j) * per + p]
            acc = None
            for i in range(lanes):
                rows = w[i][pl.ds(pl.multiple_of(slot * size, size), size), :]
                term = dims(mixed[:, columns[i]], rows, 1, 1)
                acc = term if acc is None else acc + term
            sent[j][:, p * size : (p + 1) * size] = acc.astype(BF)
        sent[j][:, cols:] = mixed[:, columns[j]]


def normed_back_kernel(blocks, index, *refs):
    w, refs = refs[:blocks], refs[blocks:]
    gq, gk, gv, tail, arrived, live, logit, wbeta, tokens, kept_result, sent_result = refs[:11]
    grads, kept, sent, gain, total = refs[11:]
    size = total.shape[1] // blocks
    cols = gq.shape[1]
    length = gq.shape[0]
    for i, g in enumerate((gq, gk, gv)):
        at = slice(i * cols, (i + 1) * cols)
        grads[:, at] = g[...]
        last = ((tail[i] + arrived[i].astype(F32)) * live[...]).astype(BF)
        grads[length - 16 :, at] = jnp.concatenate([g[length - 16 : length - PAD, :], last], axis=0)
    values = tokens[...].astype(F32)
    scale = lax.rsqrt(jnp.mean(values * values, axis=-1, keepdims=True) + NORM_EPS)
    for n in range(blocks):
        at = pl.ds(pl.multiple_of(index[1 + n] * size, size), size)
        part = dims(grads[...], w[n][0:size, : 3 * cols], 1, 1) + dims(logit[...], wbeta[:, at], 0, 0)
        gain[:, at] = jnp.sum(part * (tokens[:, at].astype(F32) * scale), axis=0, keepdims=True)
        total[:, at] = part.astype(BF)
    width = kept_result.shape[1]
    split_by_core(total, index[0], width, kept, sent)
    for out, result in ((kept, kept_result), (sent, sent_result)):
        for n in range(out.shape[0]):
            out[n, width:, :] = result[n]


def weight_rows_kernel(lanes, index, *refs):
    heads, refs = refs[:lanes], refs[lanes:]
    normed, grads, mixed, logit = refs[:4]
    *outs, wbeta, joined = refs[4:]
    cols = mixed.shape[1]
    wide = grads.shape[1]
    size = outs[0].shape[0]
    rank = index[0]
    outs[-2:] = [outs[-2:]]
    for j, part in enumerate(heads):
        joined[:, pl.ds(pl.multiple_of((rank ^ j) * cols, cols), cols)] = part[...]
    for n, out in enumerate(outs):
        at = pl.ds(pl.multiple_of(index[1 + n] * size, size), size)
        first = dims(normed[:, at], grads[...], 0, 0).astype(BF)
        second = dims(joined[:, at], mixed[...], 0, 0).astype(BF)
        pieces = out if isinstance(out, list) else [out]
        for n, piece in enumerate(pieces):
            rows = slice(n * piece.shape[0], (n + 1) * piece.shape[0])
            piece[:, :wide] = first[rows]
            piece[:, wide:] = second[rows]
    wbeta[...] = dims(logit[...], normed[...], 1, 0)


def body(
    tokens,
    cotangent,
    lengths,
    pad_mask,
    attn_gain,
    projection_weight,
    w_beta,
    beta_bias,
    conv_weight,
    head_gain,
    mlp_gain,
    w_gate,
    w_up,
    w_down,
):
    width, model = tokens.shape
    heads = w_beta.shape[1]
    depth = head_gain.shape[0]
    ksize = conv_weight.shape[1]
    margin = ksize - 1
    lanes, blocks = lax.axis_size("ta"), lax.axis_size("dev")
    rank, place = lax.axis_index("ta"), lax.axis_index("dev")
    own_heads = heads // lanes
    cols = own_heads * depth
    rows = projection_weight.shape[0]
    group = lanes * width
    ring = Ring()

    positions = place * group + jnp.arange(group, dtype=jnp.int32)
    documents = document_of(lengths, positions)
    valid = jnp.stack(
        [
            (document_of(lengths, positions - margin + offset) == documents).astype(F32)
            for offset in range(ksize)
        ],
        axis=1,
    )
    previous = document_of(lengths, positions[::width] - 1)

    at_rank = rank.astype(jnp.int32).reshape(1)
    at_place = place.astype(jnp.int32).reshape(1)
    by_rank = jnp.concatenate([at_rank, ring.slot_of])

    flags = jnp.zeros((8, model), BF).at[0, 0:width].set(pad_mask.astype(BF))
    edge = jnp.concatenate([tokens[width - PAD :], flags], axis=0)
    route = [(i, i + 1) for i in range(lanes - 1, blocks * lanes - 1, lanes)]
    before = lax.ppermute(edge, BOTH, route)
    flags = flags.at[0, width : width + PAD].set(before[PAD, width - PAD : width])
    packed = gather_parts(jnp.concatenate([tokens, flags, before[0:PAD]], axis=0))
    cot_parts = gather_parts(cotangent)
    group_tokens, normed_group, normed, flags = vmem_call(
        "norm",
        functools.partial(norm_kernel, width),
        [
            shape((group, model), BF),
            shape((group, model), BF),
            shape((group + PAD, model), BF),
            shape((lanes, 8, 2 * width), BF),
        ],
        [at_rank, *packed, attn_gain[None]],
        0,
    )
    cot_group = in_order(cot_parts, at_rank)
    live = flags[:, 0, 0:width].reshape(group).astype(F32)
    live_ext = jnp.concatenate([flags[0, 0, width : width + PAD].astype(F32), live])[:, None]

    own_conv = lax.dynamic_slice_in_dim(conv_weight, rank * cols, cols, 2)
    own_bias = lax.dynamic_slice_in_dim(beta_bias, rank * own_heads, own_heads, 0)
    chunk_docs = documents.reshape(lanes, width)
    continuing = (chunk_docs == previous[:, None]).reshape(group).astype(F32)
    closing = (chunk_docs == chunk_docs[:, width - 1 :]).reshape(group).astype(F32)
    shared = jnp.stack(
        [valid[:, j] for j in range(margin)] + [continuing, closing, live, documents.astype(F32)], axis=0
    )
    shared = jnp.broadcast_to(shared, (own_heads,) + shared.shape)
    columns = jnp.transpose(shared, (0, 2, 1))

    split = jnp.transpose(projection_weight.reshape(rows, 4, lanes, cols), (2, 0, 1, 3)).reshape(lanes, rows, 4 * cols)
    turned = jnp.tile(w_beta.T.reshape(lanes, own_heads, rows), (1, lanes, 1))
    turned = jnp.pad(turned, ((0, 0), (0, 0), (0, 4 * cols - rows)))
    parts = exchange(jnp.concatenate([split, turned], axis=1), rank)
    (own_rows,) = vmem_call(
        "weights",
        functools.partial(weights_kernel, lanes),
        [shape((lanes * rows + heads, 4 * cols), BF)],
        [at_rank, *parts],
        0,
    )
    w = ring.collect(own_rows, [[packed[-1]], [normed, cot_group, live_ext], [columns, own_conv]])
    cot_all = lax.all_gather(gate(cotangent, w[-1]), BOTH, axis=0, tiled=True)
    projected, w_out, beta_logit, wbeta = project(ring.slots, normed, live_ext, w, lanes)
    sig_beta = jax.nn.sigmoid(beta_logit[PAD:, :own_heads].T + own_bias[:, None])
    beta = sig_beta * live[None]
    row = jnp.concatenate([shared, beta[:, None]], axis=1)
    columns = jnp.concatenate([columns, beta[:, :, None]], axis=2)
    mixer = Mixer(projected, own_conv, columns, row, width)
    head_normed = mixer.outputs(
        jnp.concatenate([at_place, ring.slots]), ring.collect(mixer.whole), head_gain[None]
    )
    w_out = gather_parts(w_out, head_normed)
    heads_low = gather_parts(head_normed)
    feed_rows, *own_feed, own_residual = vmem_call(
        "out",
        functools.partial(out_kernel, lanes),
        [shape((group, model), BF)] + [shape((width // 2, model), BF)] * 2 + [shape((width, model))],
        [by_rank, *heads_low, *w_out, group_tokens, mlp_gain[None]],
        2 * group * model * model,
        scratch=[pltpu.VMEM((group, model), F32)],
    )
    half_rows = width // 2
    feed_halves = [lax.all_gather(x, BOTH, axis=0, tiled=True) for x in own_feed]

    weights = [w_gate, w_up, w_down]
    units = w_gate.shape[1]
    core = (rank % 2).astype(jnp.int32).reshape(1)
    *arrays, kept, sent, kept_result, sent_result = feed_own(
        jnp.concatenate([at_place, core]), feed_rows, cot_group, weights, blocks * group, width
    )
    others = lax.rem(place + 1 + jnp.arange(blocks - 1, dtype=jnp.int32), blocks)
    row_parts = [others[: (blocks + 1) // 2], others[(blocks + 1) // 2 :]]

    def hidden_of(part, held, dep):
        return by_group(
            "feed_hidden", hidden_kernel, part, group, [cot_all], [w_down], [units], held, [dep], 1
        )[::-1]

    kept, arrived, (_, grad_hidden) = scatter_sum(
        kept, sent, rank, lambda sent: hidden_of(row_parts[0], [], sent)
    )

    halves_left = [0, 1]

    def by_halves(x):
        return x.reshape(blocks * lanes, 2, half_rows, x.shape[-1])

    def fill_rows(deps):
        half = halves_left.pop(0)
        *found, token = by_group(
            "feed_rows", rows_kernel, others, lanes * half_rows, [feed_halves[half], by_halves(grad_hidden)],
            weights[:2], [units] * 3, [by_halves(x) for x in arrays], deps, 2, half,
        )
        arrays[:] = [x.reshape(blocks * group, units) for x in found]
        return token

    order = [0, 1, 2]
    ffn_grads = [[], [], []]
    done = [0, 0, 0]

    def fill_grads(parts, dep):
        which = order[0]
        lefts = [cot_all] if which == 2 else feed_halves
        hidden, grad_gate, grad_lifted = arrays
        right = (grad_gate, grad_lifted, hidden)[which]
        right = by_halves(right)
        out, token = weight_grad(done[which], parts, lefts, right, ffn_grads[which], [dep], which == 2)
        ffn_grads[which] = [out]
        done[which] += 1
        if done[which] == parts:
            order.pop(0)
        return token

    grad_residual, grad_mlp_gain, *sent = vmem_call(
        "residual",
        functools.partial(residual_kernel, lanes),
        [shape((width, model)), shape((1, model))] + [shape((width, 2 * cols), BF)] * lanes,
        [by_rank, *w_out, kept, arrived, own_residual, cotangent, mlp_gain[None]],
        2 * width * model * model,
        scratch=[pltpu.VMEM((width, model), BF)],
    )
    by_heads = [swap(x, "ta", j) if j else x for j, x in enumerate(sent)]
    token, grad_hidden = hidden_of(row_parts[1], [grad_hidden], sent[0])
    leak, grad_head_gain, mixed_cols = mixer.leak(at_rank, by_heads, [token])
    beside = swap(leak, "dev", 1)
    pair = jnp.stack([leak, beside])
    pairs = [
        lax.ppermute(pair, "dev", [(i, i - 2 * k) for i in range(2 * k, blocks)]) for k in range(1, blocks // 2)
    ]
    token = fill_rows([pair])
    grad_q, grad_k, grad_v, tail, spill, grad_conv, grad_beta = mixer.back([beside, *pairs], [token])
    arrived = lax.ppermute(spill.astype(BF), "dev", [(i, i - 1) for i in range(1, blocks)])
    grad_logit = grad_beta[:, 0] * beta * (1.0 - sig_beta)
    grad_bias = jnp.sum(grad_logit, axis=1)
    grad_logit_low = jnp.pad(grad_logit.astype(BF), ((0, 8 - own_heads), (0, 0)))

    half = (lanes // 2, 2 * width, model)
    grad_projected, kept, sent, grad_attn_gain = vmem_call(
        "normed_back",
        functools.partial(normed_back_kernel, blocks),
        [shape((group, 3 * cols), BF), shape(half, BF), shape(half, BF), shape((1, model))],
        [jnp.concatenate([core, ring.slots]), *w, grad_q, grad_k, grad_v, tail, arrived]
        + [live[group - PAD :, None], grad_logit_low, wbeta, group_tokens, kept_result, sent_result],
        2 * group * model * 3 * cols,
        scratch=[pltpu.VMEM((group, model), BF)],
    )

    *partial_rows, partial_wbeta = vmem_call(
        "weight_rows",
        functools.partial(weight_rows_kernel, lanes),
        [shape((model // blocks, 4 * cols), BF)] * (blocks - 1)
        + [shape((model // blocks // 2, 4 * cols), BF)] * 2
        + [shape((8, model))],
        [jnp.concatenate([at_rank, ring.slots]), *heads_low, normed_group, grad_projected, mixed_cols]
        + [grad_logit_low],
        2 * group * model * 4 * cols,
        scratch=[pltpu.VMEM((group, model), BF)],
    )
    made = []

    def fill(function, *deps):
        made.append(function(*deps))
        return made[-1]

    terms, deps = ring.scatter(
        partial_rows,
        [
            lambda x: fill(fill_rows, [x]),
            lambda x: fill(fill_grads, 1, x),
            lambda x: fill(fill_grads, 1, x),
            lambda x: fill(fill_grads, 1, x),
        ],
    )
    w_parts = vmem_call("sum", sum_kernel, [shape((rows, 4 * cols), BF)] * lanes, [at_rank, *terms], 0, deps)
    moved_parts = [swap(x, "ta", j) if j else x for j, x in enumerate(w_parts)]
    (grad_projection,) = vmem_call(
        "assemble",
        assemble_kernel,
        [shape((rows, 4, model))],
        [at_rank, *moved_parts],
        0,
    )

    kept, arrived, _ = scatter_sum(kept, sent, rank, lambda sent: (made[0],))
    block_out, grad_tokens = vmem_call(
        "finish",
        finish_kernel,
        [shape((width, model), BF), shape((width, model))],
        [kept, arrived, own_residual, grad_residual, tokens, attn_gain[None]],
        0,
        w_parts[:1],
    )

    own = jnp.concatenate([grad_conv.reshape(-1), partial_wbeta[:own_heads].reshape(-1), grad_bias])
    gains = jnp.concatenate([grad_mlp_gain[0], grad_head_gain[0], grad_attn_gain[0]])
    length = own.shape[0]
    apart = length + (-length % 1024)
    flat = jnp.zeros((lanes, apart), F32)
    flat = lax.dynamic_update_slice(flat, jnp.pad(own, (0, apart - length))[None], (rank, 0))
    flat = jnp.concatenate([flat.reshape(-1, 128), jnp.pad(gains, (0, -gains.shape[0] % 1024)).reshape(-1, 128)])
    flat = gate(lax.psum(flat, BOTH), w_parts[0]).reshape(-1)
    gains = flat[lanes * apart :]
    flat = flat[: lanes * apart].reshape(lanes, apart)
    convs = 3 * ksize * cols
    conv_sum = jnp.transpose(flat[:, :convs].reshape(lanes, 3, ksize, cols), (1, 2, 0, 3))
    conv_sum = conv_sum.reshape(3, ksize, lanes * cols)
    wbeta_sum = flat[:, convs : convs + own_heads * model].reshape(heads, model)
    grad_w_beta = lax.dynamic_slice_in_dim(wbeta_sum, (place * lanes + rank) * rows, rows, 1).T
    bias_sum = flat[:, convs + own_heads * model : length].reshape(heads)

    (grad_w_gate,), (grad_w_up,), (grad_w_down,) = ffn_grads
    return (
        block_out,
        grad_tokens,
        gains[model + depth : 2 * model + depth],
        grad_projection,
        grad_w_beta,
        bias_sum,
        conv_sum,
        gains[model : model + depth],
        gains[:model],
        grad_w_gate,
        grad_w_up,
        grad_w_down,
    )


def solution(mesh):
    rows = P(BOTH, None)
    three = P(BOTH, None, None)
    return jax.shard_map(
        body,
        mesh=mesh,
        in_specs=(
            rows,
            rows,
            P(),
            P(BOTH),
            P(),
            three,
            rows,
            P(),
            P(),
            P(),
            P(),
            P(None, "ta"),
            P(None, "ta"),
            P("ta", None),
        ),
        out_specs=(
            rows,
            rows,
            P(),
            three,
            rows,
            P(),
            P(),
            P(),
            P(),
            P(None, "ta"),
            P(None, "ta"),
            P("ta", None),
        ),
        check_vma=False,
    )
```

```python
import functools

import jax
import jax.numpy as jnp
from jax import lax
from jax.experimental import pallas as pl
from jax.experimental.pallas import tpu as pltpu
from jax.sharding import PartitionSpec as P

NORM_EPS = 1e-06
HEAD_EPS = 1e-05
UNIT_EPS = 1e-06
BOTH = ("dev", "ta")
BF = jnp.bfloat16
F32 = jnp.float32


def swap(x, axis, bit):
    return lax.ppermute(x, axis, [(i, i ^ bit) for i in range(lax.axis_size(axis))])


def gather_parts(x, *waits):
    parts = [x]
    for j in range(1, lax.axis_size("ta")):
        bit = j & -j
        if waits and j == 2 * bit + bit:
            parts[j ^ bit] = gate(parts[j ^ bit], *waits)
        parts.append(swap(parts[j ^ bit], "ta", bit))
    return parts


def gate(x, *deps):
    return pl.pallas_call(
        lambda *refs: None,
        name="gate",
        out_shape=jax.ShapeDtypeStruct(x.shape, x.dtype),
        in_specs=[pl.BlockSpec(memory_space=pl.ANY)] * (1 + len(deps)),
        out_specs=pl.BlockSpec(memory_space=pl.ANY),
        input_output_aliases={0: 0},
    )(x, *deps)


class Ring:
    def __init__(self):
        n = self.size = lax.axis_size("dev")
        self.last = n // 2
        self.order = list(range(0, n, 2)) + list(range(n - 1, 0, -2))
        self.place = lax.axis_index("dev")
        self.spot = self.spot_of(self.place)
        distances = [0] + [d for s in range(1, self.last) for d in (-s, s)] + [self.last]
        spots = lax.rem(self.spot + n + jnp.array(distances, jnp.int32), n)
        self.slots = jnp.where(2 * spots < n, 2 * spots, 2 * (n - 1 - spots) + 1)
        away = lax.rem(self.spot_of(jnp.arange(n, dtype=jnp.int32)) + n - self.spot, n)
        slot = jnp.where(away < self.last, 2 * away, 2 * (n - away) - 1)
        self.slot_of = jnp.where(away == self.last, n - 1, slot)

    def spot_of(self, index):
        return jnp.where(index % 2 == 0, index // 2, self.size - 1 - index // 2)

    def move(self, x, step):
        n = self.size
        return lax.ppermute(x, "dev", [(self.order[p], self.order[(p + step) % n]) for p in range(n)])

    def collect(self, x, waits=()):
        half = x.shape[0] // 2
        found = [x]
        onward, back = x, x
        for s in range(1, self.last):
            onward, back = self.move(onward, 1), self.move(back, -1)
            if len(waits) >= s and waits[s - 1]:
                onward, back = gate(onward, *waits[s - 1]), gate(back, *waits[s - 1])
            found += [onward, back]
        far = [self.move(onward[:half], 1), self.move(back[half:], -1)]
        return found + [jnp.concatenate(far, axis=0)]

    def scatter(self, blocks, beside=()):
        last = self.last
        beside = list(beside) + [None] * last
        block = lambda d: blocks[0 if d == 0 else 2 * d if d > 0 else -2 * d - 1]
        right, left = blocks[-2:]
        for s in range(last - 1, -1, -1):
            ahead, behind = self.move(right, 1), self.move(left, -1)
            deps = [beside[last - 1 - s](right)] if beside[last - 1 - s] else []
            if s:
                like = [shape(block(s).shape, BF)] * 2
                right, left = vmem_call(
                    "ring_add", ring_add_kernel, like, [block(s), block(-s), ahead, behind], 0, deps
                )
        return [block(0), ahead, behind], deps


def ring_add_kernel(first, second, ahead, behind, right, left):
    rows, part = first.shape[0], ahead.shape[0]
    for block, arrived, out, at in (
        (first, ahead, right, slice(0, part)),
        (second, behind, left, slice(rows - part, rows)),
    ):
        if part < rows:
            out[...] = block[...]
        out[at, :] = (block[at, :].astype(F32) + arrived[...].astype(F32)).astype(BF)


def sum_kernel(rank, x, y, z, *outs):
    rows = outs[0].shape[0]
    for j, out in enumerate(outs):
        at = pl.ds(pl.multiple_of((rank[0] ^ j) * rows, rows), rows)
        out[...] = (x[at, :].astype(F32) + (y[at, :].astype(F32) + z[at, :].astype(F32))).astype(BF)


def assemble_kernel(rank, *refs):
    out, parts = refs[-1], refs[:-1]
    count = out.shape[1]
    cols = parts[0].shape[1] // count
    for j, part in enumerate(parts):
        at = pl.ds(pl.multiple_of((rank[0] ^ j) * cols, cols), cols)
        for i in range(count):
            out[:, i, at] = part[:, i * cols : (i + 1) * cols].astype(F32)


def exchange(blocks, rank):
    parts = []
    for j in range(lax.axis_size("ta")):
        block = lax.dynamic_index_in_dim(blocks, rank ^ j, 0, False)
        parts.append(swap(block, "ta", j) if j else block)
    return parts


def scatter_sum(kept, sent, rank, beside=None):
    lanes = lax.axis_size("ta")
    made = None
    bit = 1
    while True:
        arrived = swap(sent, "ta", bit)
        bit *= 2
        if bit == lanes:
            if beside:
                made = beside(sent)
                arrived = gate(arrived, made[0])
            return kept[0], arrived[0], made
        half = (kept.shape[0] // 2,) + kept.shape[1:]
        mine = ((rank // bit) % 2).astype(jnp.int32).reshape(1)
        kept, sent = vmem_call("stage", stage_kernel, [shape(half), shape(half, BF)], [mine, kept, arrived], 0)


def stage_kernel(mine, first, second, kept, sent):
    for n in range(kept.shape[0]):
        for out, which in ((kept, mine[0]), (sent, 1 - mine[0])):
            at = 2 * n + which
            out[n] = (first[at].astype(F32) + second[at].astype(F32)).astype(out.dtype)


def rms_scale(values, gain):
    return values * lax.rsqrt(jnp.mean(values * values, axis=-1, keepdims=True) + NORM_EPS) * gain


def document_of(lengths, positions):
    starts = jnp.cumsum(lengths) - lengths
    above = (starts[None, :] <= positions[:, None]).astype(jnp.int32)
    return jnp.sum(above, axis=1) - 1


def contract_rows(left, right):
    return lax.dot_general(left, right, (((0,), (0,)), ((), ())), preferred_element_type=F32)


def contract_cols(left, right):
    return lax.dot_general(left, right, (((1,), (1,)), ((), ())), preferred_element_type=F32)


def dot(left, right):
    return jnp.dot(left, right, preferred_element_type=F32)


PAD = 8
HEADS_A_STEP = 2
VMEM_LIMIT = 48 * 1024 * 1024
FFN_VMEM = 56 * 1024 * 1024


def dims(a, b, ca, cb):
    return lax.dot_general(a, b, (((ca,), (cb,)), ((), ())), preferred_element_type=F32)


def d1(a, b, ca=1, cb=0):
    return dims(a.astype(BF), b.astype(BF), ca, cb)


def parts_of(a):
    high = a.astype(BF)
    return high, (a - high.astype(F32)).astype(BF)


def d3(a, b, ca=1, cb=0):
    ah, al = parts_of(a)
    bh, bl = parts_of(b)
    return dims(ah, bh, ca, cb) + (dims(ah, bl, ca, cb) + dims(al, bh, ca, cb))


def iotas(size):
    return (
        lax.broadcasted_iota(jnp.int32, (size, size), 0),
        lax.broadcasted_iota(jnp.int32, (size, size), 1),
    )


def inverses_of(lowers):
    size = lowers[0].shape[0]
    row, col = iotas(size)
    eye = (row == col).astype(F32)
    pair = (row // 2 == col // 2).astype(F32)
    found = [eye - low * pair for low in lowers]
    block = 2
    while block < size:
        joint = ((row // (2 * block) == col // (2 * block)) & (row // block != col // block)).astype(F32)
        steps = [d1(low * joint, x) for low, x in zip(lowers, found)]
        found = [x - d1(x, s) for x, s in zip(found, steps)]
        block *= 2
    errors = [d3(low, x) + (x - eye) for low, x in zip(lowers, found)]
    return [x - d1(x, e) for x, e in zip(found, errors)]


def unit_of(active):
    scale = lax.rsqrt(jnp.sum(active * active, axis=-1, keepdims=True) + UNIT_EPS)
    return active * scale, scale


def masks_of(aux, row, at, size):
    doc, doc_row = aux[at, 6:7], row[6:7, at]
    r, c = iotas(size)
    same = doc == doc_row
    weak = (same & (r >= c)).astype(F32)
    strict = (same & (r > c)).astype(F32)
    return weak, strict


def forward_kernel(size, xq, xk, xv, conv, aux_ref, row_ref, yq, yk, yv, inv, plain, reach, read, direct, trans, fresh, whole):
    heads, count = inv.shape[0], inv.shape[1]
    depth = xq.shape[1] // heads
    ksize = conv.shape[1]
    r, c = iotas(depth)
    eye = (r == c).astype(F32)
    spans = [slice(n * size, (n + 1) * size) for n in range(count)]
    saved = []
    lowers = []
    for h in range(heads):
        aux, row = aux_ref.at[h], row_ref.at[h]
        col = slice(h * depth, (h + 1) * depth)
        for n, at in enumerate(spans):
            active = []
            for i, (x, y) in enumerate(((xq, yq), (xk, yk), (xv, yv))):
                first = PAD - (ksize - 1) + n * size
                summed = x[first + ksize - 1 : first + ksize - 1 + size, col] * conv[i, ksize - 1 : ksize, col]
                for j in range(ksize - 1):
                    moved = x[first + j : first + j + size, col]
                    summed = summed + moved * conv[i, j : j + 1, col] * aux[at, j : j + 1]
                y[at, col] = summed
                active.append(summed * jax.nn.sigmoid(summed))
            q = unit_of(active[0])[0] * depth ** (-0.5)
            k = unit_of(active[1])[0]
            weak, strict = masks_of(aux, row, at, size)
            rate = row[7:8, at]
            products = d3(jnp.concatenate([q, k], axis=0), k, 1, 1)
            lowers.append(products[size:] * rate * strict)
            saved.append((h, n, q, k, active[2], products[:size] * rate * weak))
    inverses = inverses_of(lowers)
    total, added = [None] * heads, [None] * heads
    for inverse, (h, n, q, k, v, mix) in zip(inverses, saved):
        at = spans[n]
        aux = aux_ref.at[h]
        cont, clos, beta = aux[at, 3:4], aux[at, 4:5], aux[at, 7:8]
        both = d3(inverse, jnp.concatenate([v, k * cont], axis=1))
        spread = d1(mix, both)
        inv[h, n] = inverse
        plain[h, at, :] = both[:, :depth]
        reach[h, at, :] = both[:, depth:]
        direct[h, at, :] = spread[:, :depth]
        read[h, at, :] = q * cont - spread[:, depth:]
        gained = d3(k * (beta * clos), both, 0, 0)
        map_n = aux[(n + 1) * size - 1 : (n + 1) * size, 3:4] * eye - gained[:, depth:]
        add_n = gained[:, :depth]
        trans[h, n] = map_n
        fresh[h, n] = add_n
        if n == 0:
            total[h], added[h] = map_n, add_n
        else:
            new = d3(map_n, jnp.concatenate([added[h], total[h]], axis=1))
            total[h], added[h] = new[:, depth:], new[:, :depth] + add_n
    for h in range(heads):
        whole[h, 0] = total[h].astype(BF)
        whole[h, 1] = added[h].astype(BF)


def read_kernel(size, count_of, index, *refs):
    parts, refs = refs[:count_of], refs[count_of:]
    trans, fresh, read, direct, gain, both, states, outputs, normed = refs
    heads, count = trans.shape[0], trans.shape[1]
    depth = trans.shape[-1]
    for n, part in enumerate(parts):
        both[index[1 + n]] = part[...]

    def earlier(i, carry):
        return tuple(
            d3(both[i, h, 0].astype(F32), carry[h]) + both[i, h, 1].astype(F32) for h in range(heads)
        )

    carry = lax.fori_loop(0, index[0], earlier, tuple(jnp.zeros((depth, depth), F32) for _ in range(heads)))
    carry = list(carry)
    for n in range(count):
        at = slice(n * size, (n + 1) * size)
        for h in range(heads):
            state = carry[h]
            states[h, n] = state
            out = direct[h, at, :] + d3(read[h, at, :], state)
            cols = slice(h * depth, (h + 1) * depth)
            outputs[at, cols] = out
            scale = lax.rsqrt(jnp.mean(out * out, axis=-1, keepdims=True) + HEAD_EPS)
            normed[at, cols] = (out * scale * gain[...]).astype(BF)
            if n < count - 1:
                carry[h] = d3(trans[h, n], state) + fresh[h, n]


def leak_kernel(size, lanes, rank, *refs):
    parts, refs = refs[:lanes], refs[lanes:]
    outputs, gain, read, trans, grad_out, from_out, leak, grad_gain, mixed, grads = refs
    heads, count = trans.shape[0], trans.shape[1]
    depth = trans.shape[-1]
    for j, part in enumerate(parts):
        at = pl.ds(pl.multiple_of((rank[0] ^ j) * size, size), size)
        grads[at, :] = part[:, : heads * depth]
        mixed[at, :] = part[:, heads * depth :]
    gained = jnp.zeros((1, depth), F32)
    totals = [None] * heads
    for n in range(count - 1, -1, -1):
        at = slice(n * size, (n + 1) * size)
        for h in range(heads):
            cols = slice(h * depth, (h + 1) * depth)
            out, grad = outputs[at, cols], grads[at, cols].astype(F32)
            scale = lax.rsqrt(jnp.mean(out * out, axis=-1, keepdims=True) + HEAD_EPS)
            unit = out * scale
            gained = gained + jnp.sum(grad * unit, axis=0, keepdims=True)
            grad = grad * gain[...]
            grad = scale * (grad - unit * jnp.mean(grad * unit, axis=-1, keepdims=True))
            grad_out[h, at, :] = grad
            term = d3(read[h, at, :], grad, 0, 0)
            from_out[h, n] = term
            totals[h] = term if n == count - 1 else d3(trans[h, n], totals[h], 0, 0) + term
    for h in range(heads):
        leak[h] = totals[h].astype(BF)
    grad_gain[...] = gained


def chain_kernel(index, beside, *refs):
    both, trans, from_out, grads = refs[-4:]
    pairs = refs[:-4]
    heads, count = trans.shape[0], trans.shape[1]
    depth = trans.shape[-1]
    devices = both.shape[0]
    odd = index[0] % 2
    carry = [jnp.zeros((depth, depth), F32) for _ in range(heads)]

    def follow(at, leak):
        at = jnp.minimum(at, devices - 1)
        return [d3(both[at, h, 0].astype(F32), carry[h], 0, 0) + leak(h).astype(F32) for h in range(heads)]

    for k in range(len(pairs), 0, -1):
        pair = pairs[k - 1]
        first = index[0] - odd + 2 * k
        carry = follow(first + 1, lambda h: pair[1 - odd, h])
        carry = follow(first, lambda h: pair[odd, h])
    later = follow(index[0] + 1, lambda h: beside[h])
    carry = [jnp.where(odd == 0, x, y) for x, y in zip(later, carry)]
    for n in range(count - 1, -1, -1):
        for h in range(heads):
            grads[h, n] = carry[h]
            if n:
                carry[h] = d3(trans[h, n], carry[h], 0, 0) + from_out[h, n]


def backward_kernel(size, xq, xk, xv, yq, yk, yv, conv, aux_ref, row_ref, inv, plain, reach, states, grads, grad_out,
                    gq, gk, gv, tail, spill, grad_conv, grad_beta, zs):
    count = inv.shape[1]
    depth = xq.shape[1]
    ksize = conv.shape[1]
    aux, row = aux_ref.at[0], row_ref.at[0]
    length = count * size
    scale_q = depth ** (-0.5)
    for n in range(count):
        at = slice(n * size, (n + 1) * size)
        cont, clos, beta = aux[at, 3:4], aux[at, 4:5], aux[at, 7:8]
        weak, strict = masks_of(aux, row, at, size)
        rate = row[7:8, at]
        ys = [yq[at, :], yk[at, :], yv[at, :]]
        sigs = [jax.nn.sigmoid(y) for y in ys]
        uq, rq = unit_of(ys[0] * sigs[0])
        k, rk = unit_of(ys[1] * sigs[1])
        q = uq * scale_q
        products = d1(jnp.concatenate([q, k], axis=0), k, 1, 1)
        qk, kk = products[:size], products[size:]
        mix = qk * rate * weak
        state, grad_state, dout = states[0, n], grads[0, n], grad_out[0, at, :]
        u = plain[0, at, :] - d1(reach[0, at, :], state)
        kds = d1(k, grad_state)
        written = beta * clos
        du = d1(mix, dout, 0, 0) + written * kds
        dr = d1(inv[0, n], du, 0, 0)
        pair = jnp.concatenate([dout, dr], axis=0)
        outer = d1(pair, u, 1, 1)
        through = d1(pair, state, 1, 1)
        dp = outer[:size] * weak
        dl = -outer[size:] * strict
        per_key = jnp.sum(dp * qk + dl * kk, axis=0, keepdims=True)
        per_state = jnp.sum((kds * u).T, axis=0, keepdims=True)
        grad_beta[0, :, at] = per_key + row[4:5, at] * per_state
        dqk = dp * rate
        da = dl * rate
        dq = cont * through[:size] + d1(dqk, k)
        dk = d1(dqk, q, 0, 0) + written * d1(u, grad_state, 1, 1) - cont * through[size:] + d1(da + da.T, k)
        dq = dq * scale_q
        acts = [
            rq * (dq - uq * jnp.sum(uq * dq, axis=-1, keepdims=True)),
            rk * (dk - k * jnp.sum(k * dk, axis=-1, keepdims=True)),
            dr,
        ]
        for i, x in enumerate((xq, xk, xv)):
            dy = acts[i] * sigs[i] * (1.0 + ys[i] * (1.0 - sigs[i]))
            first = PAD - (ksize - 1) + n * size
            for j in range(ksize):
                dv = dy if j == ksize - 1 else dy * aux[at, j : j + 1]
                term = jnp.sum(dv * x[first + j : first + j + size, :], axis=0, keepdims=True)
                before = jnp.zeros_like(term) if n == 0 else grad_conv[i, j : j + 1, :]
                grad_conv[i, j : j + 1, :] = before + term
                zs[i, j, PAD + n * size : PAD + (n + 1) * size, :] = dv * conv[i, j : j + 1, :]
    for i, g in enumerate((gq, gk, gv)):
        for j in range(ksize):
            zs[i, j, 0:PAD, :] = jnp.zeros((PAD, depth), F32)
            zs[i, j, PAD + length : 2 * PAD + length, :] = jnp.zeros((PAD, depth), F32)

        def shifted_sum(first, rows):
            return sum(zs[i, j, first + ksize - 1 - j : first + ksize - 1 - j + rows, :] for j in range(ksize))

        for n in range(count):
            at = slice(n * size, (n + 1) * size)
            g[at, :] = (shifted_sum(PAD + n * size, size) * aux[at, 5:6]).astype(BF)
        tail[i] = shifted_sum(length, PAD)
        spill[i] = shifted_sum(0, PAD)


def vmem_call(name, kernel, out_shape, inputs, flops, deps=(), scratch=(), grant=FFN_VMEM):
    smem, vmem = (pl.BlockSpec(memory_space=m) for m in (pltpu.SMEM, pltpu.VMEM))

    def run(*refs):
        kernel(*refs[: len(inputs)], *refs[len(inputs) + len(deps) :])

    return pl.pallas_call(
        run,
        name=name,
        out_shape=out_shape,
        in_specs=[smem if x.dtype == jnp.int32 else vmem for x in inputs]
        + [pl.BlockSpec(memory_space=pl.ANY)] * len(deps),
        out_specs=[vmem] * len(out_shape),
        scratch_shapes=list(scratch),
        cost_estimate=cost(flops, inputs, out_shape),
        compiler_params=pltpu.CompilerParams(vmem_limit_bytes=grant),
    )(*inputs, *deps)


def cost(flops, inputs, outputs):
    moved = sum(x.size * x.dtype.itemsize for x in list(inputs) + list(outputs))
    return pl.CostEstimate(flops=int(flops), bytes_accessed=int(moved), transcendentals=0)


def shape(dims, dtype=F32):
    return jax.ShapeDtypeStruct(dims, dtype)


class Mixer:
    def __init__(self, projected, own_conv, aux, row, size):
        self.size = size
        self.heads, self.length = aux.shape[0], aux.shape[1]
        self.depth = own_conv.shape[2] // self.heads
        self.count = self.length // size
        self.projected, self.conv, self.aux, self.row = projected, own_conv, aux, row
        heads, length, depth, count = self.heads, self.length, self.depth, self.count
        ksize = own_conv.shape[1]
        self.token_specs = [
            pl.BlockSpec((length + PAD, depth), lambda h, i=i: (0, i * heads + h)) for i in range(3)
        ]
        self.head_cols = pl.BlockSpec((length, depth), lambda h: (0, h))
        self.conv_spec = pl.BlockSpec((3, ksize, depth), lambda h: (0, 0, h))
        self.aux_specs = [
            pl.BlockSpec((1, length, 8), lambda h: (h, 0, 0)),
            pl.BlockSpec((1, 8, length), lambda h: (h, 0, 0)),
        ]
        self.chunk_spec = pl.BlockSpec((1, count, depth, depth), lambda h: (h, 0, 0, 0))
        self.inv_spec = pl.BlockSpec((1, count, size, size), lambda h: (h, 0, 0, 0))
        self.rows_spec = pl.BlockSpec((1, length, depth), lambda h: (h, 0, 0))
        self.flops = 2 * heads * count * size * depth * depth
        inputs = [projected] * 3 + [own_conv, aux, row]
        square = shape((heads, count, depth, depth))
        tokens = shape((heads, length, depth))
        out_shape = (
            [shape((length, heads * depth))] * 3
            + [shape((heads, count, size, size))]
            + [tokens] * 4
            + [square] * 2
            + [shape((heads, 2, depth, depth), BF)]
        )
        step = HEADS_A_STEP if heads % HEADS_A_STEP == 0 else 1
        each = lambda x: pl.BlockSpec((step,) + x.shape[1:], lambda h: (h,) + (0,) * (len(x.shape) - 1))
        column = pl.BlockSpec((length, step * depth), lambda h: (0, h))
        (
            self.yq, self.yk, self.yv, self.inv, self.plain, self.reach, self.read, self.direct,
            self.trans, self.fresh, self.whole,
        ) = pl.pallas_call(
            functools.partial(forward_kernel, size),
            name="mixer_forward",
            out_shape=out_shape,
            grid=(heads // step,),
            in_specs=[
                pl.BlockSpec((length + PAD, step * depth), lambda h, i=i: (0, i * (heads // step) + h))
                for i in range(3)
            ]
            + [pl.BlockSpec((3, ksize, step * depth), lambda h: (0, 0, h)), each(aux), each(row)],
            out_specs=[column] * 3 + [each(x) for x in out_shape[3:]],
            cost_estimate=cost(60 * self.flops, inputs, out_shape),
            compiler_params=pltpu.CompilerParams(vmem_limit_bytes=VMEM_LIMIT),
        )(*inputs)

    def outputs(self, index, parts, head_gain):
        heads, length, depth, count = self.heads, self.length, self.depth, self.count
        self.index, self.gain = index, head_gain
        self.both, self.states, self.out, normed = vmem_call(
            "mixer_read",
            functools.partial(read_kernel, self.size, len(parts)),
            [
                shape((len(parts),) + parts[0].shape, BF),
                shape((heads, count, depth, depth)),
                shape((length, heads * depth)),
                shape((length, heads * depth), BF),
            ],
            [index, *parts, self.trans, self.fresh, self.read, self.direct, head_gain],
            12 * self.flops,
            grant=32 * 1024 * 1024,
        )
        return normed

    def leak(self, rank, parts, deps=()):
        heads, length, depth, count = self.heads, self.length, self.depth, self.count
        self.grad_out, self.from_out, leak, grad_gain, mixed = vmem_call(
            "mixer_leak",
            functools.partial(leak_kernel, self.size, len(parts)),
            [
                shape((heads, length, depth)),
                shape((heads, count, depth, depth)),
                shape((heads, depth, depth), BF),
                shape((1, depth)),
                shape((length, heads * depth), BF),
            ],
            [rank, *parts, self.out, self.gain, self.read, self.trans],
            6 * self.flops,
            deps,
            scratch=[pltpu.VMEM((length, heads * depth), BF)],
        )
        return leak, grad_gain, mixed

    def back(self, leaks, deps=()):
        heads, length, depth, count = self.heads, self.length, self.depth, self.count
        ksize = self.conv.shape[1]
        (grads,) = vmem_call(
            "mixer_chain",
            chain_kernel,
            [shape((heads, count, depth, depth))],
            [self.index, *leaks, self.both, self.trans, self.from_out],
            6 * self.flops,
            deps,
        )
        inputs = [self.projected] * 3 + [self.yq, self.yk, self.yv, self.conv, self.aux, self.row]
        inputs += [self.inv, self.plain, self.reach, self.states, grads, self.grad_out]
        edge = shape((3, PAD, heads * depth))
        out_shape = [shape((length, heads * depth), BF)] * 3 + [edge] * 2
        out_shape += [shape((3, ksize, heads * depth)), shape((heads, 1, length))]
        edge_spec = pl.BlockSpec((3, PAD, depth), lambda h: (0, 0, h))
        return pl.pallas_call(
            functools.partial(backward_kernel, self.size),
            name="mixer_backward",
            out_shape=out_shape,
            grid=(heads,),
            in_specs=self.token_specs
            + [self.head_cols] * 3
            + [self.conv_spec]
            + self.aux_specs
            + [self.inv_spec, self.rows_spec, self.rows_spec, self.chunk_spec, self.chunk_spec, self.rows_spec],
            out_specs=[self.head_cols] * 3
            + [edge_spec] * 2
            + [self.conv_spec, pl.BlockSpec((1, 1, length), lambda h: (h, 0, 0))],
            scratch_shapes=[pltpu.VMEM((3, ksize, length + 2 * PAD, depth), F32)],
            cost_estimate=cost(30 * self.flops, inputs, out_shape),
            compiler_params=pltpu.CompilerParams(vmem_limit_bytes=VMEM_LIMIT),
        )(*inputs)


ANY = pl.BlockSpec(memory_space=pl.ANY)
TOKEN = shape((8, 128))


def resident(x):
    return pl.BlockSpec(x.shape, lambda *_: (0,) * x.ndim, pipeline_mode=pl.Buffered(1))


def activations(gate, lifted, grad_hidden):
    sig = jax.nn.sigmoid(gate)
    swish = gate * sig
    return (
        (swish * lifted).astype(BF),
        (grad_hidden * lifted * sig * (1.0 + gate * (1.0 - sig))).astype(BF),
        (grad_hidden * swish).astype(BF),
    )


def chunks_of(size, chunk=256):
    return [slice(at, min(at + chunk, size)) for at in range(0, size, chunk)]


def params(flops, moved):
    return dict(
        cost_estimate=pl.CostEstimate(flops=int(flops), bytes_accessed=int(moved), transcendentals=0),
        compiler_params=pltpu.CompilerParams(vmem_limit_bytes=FFN_VMEM),
    )


TOKEN_SPEC = pl.BlockSpec((8, 128), lambda *_: (0, 0))


def split_by_core(source, core, width, kept, sent):
    for p in range(kept.shape[0]):
        for ref, which in ((kept, core), (sent, 1 - core)):
            ref[p, 0:width, :] = source[pl.ds(pl.multiple_of((2 * p + which) * width, width), width), :]


def first_step(act):
    pl.when(pl.program_id(0) == 0)(act)


def own_kernel(index, feed, cot, wg, wu_source, wd_source, hidden, grad_gate, grad_lifted, *refs):
    (kept, sent, kept_result, sent_result), (total, result, wu, wd, sems) = refs[:4], refs[4:]
    up, down = (
        pltpu.make_async_copy(source, held, sems.at[n])
        for n, (source, held) in enumerate(((wu_source, wu), (wd_source, wd)))
    )
    first_step(up.start)
    first_step(down.start)
    model = wd.shape[1]
    gated = jnp.dot(feed[...], wg[...], preferred_element_type=F32)
    first_step(up.wait)
    lifted = jnp.dot(feed[...], wu[...], preferred_element_type=F32)
    first_step(down.wait)
    grad_hidden = dims(cot[...], wd[...], 1, 1)
    hidden[...], grad_gate[...], grad_lifted[...] = activations(gated, lifted, grad_hidden)
    for cut in chunks_of(model):
        grad_feed = dims(grad_gate[...], wg[cut, :], 1, 1) + dims(grad_lifted[...], wu[cut, :], 1, 1)
        total[:, cut] = grad_feed.astype(BF)
        result[:, cut] = jnp.dot(hidden[...], wd[:, cut], preferred_element_type=F32).astype(BF)
    split_by_core(total, index[1], kept.shape[1], kept, sent)
    split_by_core(result, index[1], kept.shape[1], kept_result, sent_result)


def hidden_kernel(groups, cot, wd, *refs):
    out, token = refs[-2:]
    out[...] = dims(cot[...], wd[...], 1, 1).astype(BF)
    token[...] = jnp.zeros_like(token)


def rows_kernel(groups, feed, grad_hidden, wg, wu, *refs):
    *outs, token = refs[-4:]
    before = grad_hidden[...].reshape(feed.shape[0], -1)
    gated = jnp.dot(feed[...], wg[...], preferred_element_type=F32)
    lifted = jnp.dot(feed[...], wu[...], preferred_element_type=F32)
    for out, value in zip(outs, activations(gated, lifted, before.astype(F32))):
        out[...] = value.reshape(out.shape)
    token[...] = jnp.zeros_like(token)


def by_group(name, kernel, groups, size, inputs, weights, outs, held, deps, products, half=0):
    like = inputs[-1].shape
    count = groups.shape[0]

    def picked(x, width):
        if x.ndim == 2:
            return pl.BlockSpec((size, width), lambda i, g: (g[i], 0))
        return pl.BlockSpec((size // like[2], 1, like[2], width), lambda i, g: (g[i], half, 0, 0))

    first = 1 + len(inputs) + len(weights) + len(deps)
    return pl.pallas_call(
        kernel,
        name=name,
        out_shape=[shape(like[:-1] + (width,), BF) for width in outs] + [TOKEN],
        grid_spec=pltpu.PrefetchScalarGridSpec(
            num_scalar_prefetch=1,
            grid=(count,),
            in_specs=[picked(x, x.shape[-1]) for x in inputs]
            + [resident(w) for w in weights]
            + [ANY] * (len(deps) + len(held)),
            out_specs=[picked(inputs[-1], width) for width in outs] + [TOKEN_SPEC],
        ),
        input_output_aliases={first + n: n for n in range(len(held))},
        **params(
            2 * count * size * weights[0].size * products,
            sum(w.size for w in weights) * 2 + count * size * 2 * (sum(outs) + sum(x.shape[-1] for x in inputs)),
        ),
    )(groups, *inputs, *weights, *deps, *held)


def feed_own(index, feed, cot, weights, tokens, width):
    rows, model = feed.shape
    units = weights[0].shape[1]
    block = 2 * width
    count = rows // block
    wide = pl.BlockSpec((block, units), lambda i, g: (g[0] * count + i, 0))
    here = pl.BlockSpec((block, model), lambda i, g: (i, 0))
    half = pl.BlockSpec((1, width, model), lambda i, g: (i, 0, 0))
    return pl.pallas_call(
        own_kernel,
        name="feed_own",
        out_shape=[shape((tokens, units), BF)] * 3
        + [shape((count, width, model), BF)] * 4,
        grid_spec=pltpu.PrefetchScalarGridSpec(
            num_scalar_prefetch=1,
            grid=(count,),
            in_specs=[here] * 2 + [resident(weights[0])] + [ANY] * 2,
            out_specs=[wide] * 3 + [half] * 4,
            scratch_shapes=[pltpu.VMEM((block, model), BF)] * 2
            + [pltpu.VMEM(w.shape, w.dtype) for w in weights[1:]]
            + [pltpu.SemaphoreType.DMA((2,))],
        ),
        **params(12 * rows * model * units, 6 * model * units + rows * (3 * units + 4 * model) * 2),
    )(index, feed, cot, *weights)


GRAD_COLS = 256


def grad_kernel(transposed, count, *refs):
    lefts, right = refs[:count], refs[count]
    out, token = refs[-2:]
    units = right.shape[-1]
    if count == 1:
        term = dims(lefts[0][...], right[...].reshape(-1, units), 0, 0)
    else:
        term = sum(dims(left[...], right[:, n].reshape(-1, units), 0, 0) for n, left in enumerate(lefts))
    out[...] = term.T if transposed else term
    token[...] = jnp.zeros_like(token)


def weight_grad(part, parts, lefts, right, held, deps, transposed):
    rows, model = lefts[0].shape
    units = right.shape[-1]
    count = model // GRAD_COLS // parts
    if transposed:
        out_spec = pl.BlockSpec((units, GRAD_COLS), lambda m: (0, part * count + m))
    else:
        out_spec = pl.BlockSpec((GRAD_COLS, units), lambda m: (part * count + m, 0))
    first = len(lefts) + 1 + len(deps)
    tokens = rows * len(lefts)
    return pl.pallas_call(
        functools.partial(grad_kernel, transposed, len(lefts)),
        name="weight_grad",
        out_shape=[shape((units, model) if transposed else (model, units)), TOKEN],
        grid=(count,),
        in_specs=[pl.BlockSpec((rows, GRAD_COLS), lambda m: (0, part * count + m))] * len(lefts)
        + [resident(right)]
        + [ANY] * (len(deps) + len(held)),
        out_specs=[out_spec, TOKEN_SPEC],
        input_output_aliases={first + n: n for n in range(len(held))},
        **params(
            2 * tokens * count * GRAD_COLS * units,
            2 * tokens * (units + count * GRAD_COLS) + 4 * count * GRAD_COLS * units,
        ),
    )(*lefts, right, *deps, *held)


def order_kernel(rank, *refs):
    out = refs[-1]
    size = refs[0].shape[0]
    for j, part in enumerate(refs[:-1]):
        out[pl.ds(pl.multiple_of((rank[0] ^ j) * size, size), size), :] = part[...]


def in_order(parts, rank):
    rows, width = parts[0].shape
    return vmem_call(
        "in_order", order_kernel, [shape((rows * len(parts), width), parts[0].dtype)], [rank, *parts], 0
    )[0]


def norm_kernel(width, rank, *refs):
    gain, group, normed, extended, live = refs[-5:]
    parts = refs[:-5]

    def scaled(values):
        values = values.astype(F32)
        scale = lax.rsqrt(jnp.mean(values * values, axis=-1, keepdims=True) + NORM_EPS)
        return (values * scale * gain[...]).astype(BF)

    for j, part in enumerate(parts):
        at = rank[0] ^ j
        rows = part[0:width, :]
        group[pl.ds(pl.multiple_of(at * width, width), width), :] = rows
        rows = scaled(rows)
        normed[pl.ds(pl.multiple_of(at * width, width), width), :] = rows
        extended[pl.ds(pl.multiple_of(PAD + at * width, PAD), width), :] = rows
        live[at] = part[width : width + 8, 0 : 2 * width]

        @pl.when(at == 0)
        def _():
            extended[0:PAD, :] = scaled(part[width + 8 : width + 8 + PAD, :])


def weights_kernel(lanes, rank, *refs):
    out, parts = refs[-1], refs[:-1]
    rows = out.shape[0] - parts[0].shape[0]
    rows = rows // (lanes - 1)
    heads = parts[0].shape[0] - rows
    mine = lax.broadcasted_iota(jnp.int32, (heads, 128), 0) // (heads // lanes)
    tile = jnp.zeros((heads, 128), F32)
    for j, part in enumerate(parts):
        at = rank[0] ^ j
        out[pl.ds(pl.multiple_of(at * rows, rows), rows), :] = part[0:rows, :]
        tile = jnp.where(mine == at, part[rows:, 0:128].astype(F32), tile)
    out[lanes * rows :, :] = jnp.zeros((heads, out.shape[1]), BF)
    out[lanes * rows :, 0:128] = tile.astype(BF)


def project_kernel(lanes, slots, x, live, *refs):
    out, out_w, logit, wbeta = refs[-4:]
    parts, last = refs[: len(refs) // 2 - 2], refs[len(refs) // 2 - 2 : -4]
    size = out_w.shape[0] // len(parts)
    heads = parts[0].shape[0] - size
    own = heads // lanes
    total = None
    for n, part in enumerate(parts):
        at = pl.ds(pl.multiple_of(slots[n] * size, size), size)
        term = jnp.dot(x[:, at], part[0:size, :], preferred_element_type=F32)
        total = term if total is None else total + term
    out[...] = total * live[...]

    @pl.when(pl.program_id(0) == 0)
    def _():
        each = size // lanes
        row = lax.broadcasted_iota(jnp.int32, (heads, size), 0)
        col = lax.broadcasted_iota(jnp.int32, (heads, size), 1)
        own_row = lax.broadcasted_iota(jnp.int32, (8, heads), 0)
        own_col = lax.broadcasted_iota(jnp.int32, (8, heads), 1)
        picked = ((own_col % own == own_row) & (own_row < own)).astype(BF)
        for n, (part, columns) in enumerate(zip(parts, last)):
            out_w[n * size : (n + 1) * size, :] = columns[0:size, :]
            tile = jnp.concatenate([part[size:, 0:each]] * lanes, axis=1)
            tile = jnp.where(col // each == row // own, tile.astype(F32), 0.0).astype(BF)
            at = pl.ds(pl.multiple_of(slots[n] * size, size), size)
            wbeta[:, at] = jnp.dot(picked, tile, preferred_element_type=F32).astype(BF)
        logit[...] = dims(x[...], wbeta[...], 1, 1)


def project(slots, x, live, parts, lanes):
    rows, model = x.shape
    size, width = parts[0].shape
    cols = width // 4
    whole = lambda a: pl.BlockSpec(a.shape, lambda i, s: (0,) * len(a.shape))
    outs = [shape((rows, 3 * cols)), shape((model, cols), BF), shape((rows, 8)), shape((8, model), BF)]
    return pl.pallas_call(
        functools.partial(project_kernel, lanes),
        name="project",
        out_shape=outs,
        grid_spec=pltpu.PrefetchScalarGridSpec(
            num_scalar_prefetch=1,
            grid=(3,),
            in_specs=[whole(x), whole(live)]
            + [pl.BlockSpec((size, cols), lambda i, s: (0, i))] * len(parts)
            + [pl.BlockSpec((size, cols), lambda i, s: (0, 3))] * len(parts),
            out_specs=[pl.BlockSpec((rows, cols), lambda i, s: (0, i))] + [whole(a) for a in outs[1:]],
        ),
        **params(6 * rows * model * cols, 2 * x.size + 8 * model * cols),
    )(slots, x, live, *parts, *parts)


def finish_kernel(kept, arrived, residual, grad_residual, tokens, gain, block_out, grad_tokens):
    width = tokens.shape[0]
    both = kept[...].astype(F32) + arrived[...].astype(F32)
    block_out[...] = (residual[...] + both[width:]).astype(BF)
    values = tokens[...].astype(F32)
    scale = lax.rsqrt(jnp.mean(values * values, axis=-1, keepdims=True) + NORM_EPS)
    unit = values * scale
    grad = both[:width] * gain[...]
    grad_tokens[...] = grad_residual[...] + scale * (
        grad - unit * jnp.mean(grad * unit, axis=-1, keepdims=True)
    )


def out_kernel(lanes, index, *refs):
    heads, w, refs = refs[:lanes], refs[lanes : 2 * lanes], refs[2 * lanes :]
    tokens, gain, feed, *own_feed, own_residual, total = refs
    rank = index[0]
    width = own_residual.shape[0]
    cols = heads[0].shape[1]
    blocks = w[0].shape[0]
    size = w[0].shape[0] // (index.shape[0] - 1)
    per = cols // size
    for j in range(lanes):
        acc = None
        for i in range(lanes):
            for p in range(per):
                slot = index[1 + (rank ^ i) * per + p]
                rows = w[j][pl.ds(pl.multiple_of(slot * size, size), size), :]
                term = jnp.dot(heads[i][:, p * size : (p + 1) * size], rows, preferred_element_type=F32)
                acc = term if acc is None else acc + term
        at = pl.ds(pl.multiple_of((rank ^ j) * cols, cols), cols)
        total[:, at] = tokens[:, at].astype(F32) + acc
    for n in range(lanes):
        at = slice(n * width, (n + 1) * width)
        values = total[at, :]
        scale = lax.rsqrt(jnp.mean(values * values, axis=-1, keepdims=True) + NORM_EPS)
        feed[at, :] = (values * scale * gain[...]).astype(BF)
    own = pl.ds(pl.multiple_of(rank * width, width), width)
    own_residual[...] = total[own, :]
    for n, out in enumerate(own_feed):
        out[...] = feed[pl.ds(pl.multiple_of(rank * width + n * (width // 2), width // 2), width // 2), :]


def residual_kernel(lanes, index, *refs):
    w, refs = refs[:lanes], refs[lanes:]
    kept, arrived, residual, cot, gain, grad_residual, grad_gain = refs[:7]
    sent, mixed = refs[7 : 7 + lanes], refs[7 + lanes]
    rank = index[0]
    cols = w[0].shape[1]
    size = w[0].shape[0] // (index.shape[0] - 1)
    per = cols // size
    grad = kept[...].astype(F32) + arrived[...].astype(F32)
    values = residual[...]
    scale = lax.rsqrt(jnp.mean(values * values, axis=-1, keepdims=True) + NORM_EPS)
    unit = values * scale
    grad_gain[...] = jnp.sum(grad * unit, axis=0, keepdims=True)
    grad = grad * gain[...]
    grad = cot[...].astype(F32) + scale * (grad - unit * jnp.mean(grad * unit, axis=-1, keepdims=True))
    grad_residual[...] = grad
    mixed[...] = grad.astype(BF)
    columns = [pl.ds(pl.multiple_of((rank ^ j) * cols, cols), cols) for j in range(lanes)]
    for j in range(lanes):
        for p in range(per):
            slot = index[1 + (rank ^ j) * per + p]
            acc = None
            for i in range(lanes):
                rows = w[i][pl.ds(pl.multiple_of(slot * size, size), size), :]
                term = dims(mixed[:, columns[i]], rows, 1, 1)
                acc = term if acc is None else acc + term
            sent[j][:, p * size : (p + 1) * size] = acc.astype(BF)
        sent[j][:, cols:] = mixed[:, columns[j]]


def normed_back_kernel(blocks, index, *refs):
    w, refs = refs[:blocks], refs[blocks:]
    gq, gk, gv, tail, arrived, live, logit, wbeta, tokens, kept_result, sent_result = refs[:11]
    grads, kept, sent, gain, total = refs[11:]
    size = total.shape[1] // blocks
    cols = gq.shape[1]
    length = gq.shape[0]
    for i, g in enumerate((gq, gk, gv)):
        at = slice(i * cols, (i + 1) * cols)
        grads[:, at] = g[...]
        last = ((tail[i] + arrived[i].astype(F32)) * live[...]).astype(BF)
        grads[length - 16 :, at] = jnp.concatenate([g[length - 16 : length - PAD, :], last], axis=0)
    values = tokens[...].astype(F32)
    scale = lax.rsqrt(jnp.mean(values * values, axis=-1, keepdims=True) + NORM_EPS)
    for n in range(blocks):
        at = pl.ds(pl.multiple_of(index[1 + n] * size, size), size)
        part = dims(grads[...], w[n][0:size, : 3 * cols], 1, 1) + dims(logit[...], wbeta[:, at], 0, 0)
        gain[:, at] = jnp.sum(part * (tokens[:, at].astype(F32) * scale), axis=0, keepdims=True)
        total[:, at] = part.astype(BF)
    width = kept_result.shape[1]
    split_by_core(total, index[0], width, kept, sent)
    for out, result in ((kept, kept_result), (sent, sent_result)):
        for n in range(out.shape[0]):
            out[n, width:, :] = result[n]


def weight_rows_kernel(lanes, index, *refs):
    heads, refs = refs[:lanes], refs[lanes:]
    normed, grads, mixed, logit = refs[:4]
    *outs, wbeta, joined = refs[4:]
    cols = mixed.shape[1]
    wide = grads.shape[1]
    size = outs[0].shape[0]
    rank = index[0]
    outs[-2:] = [outs[-2:]]
    for j, part in enumerate(heads):
        joined[:, pl.ds(pl.multiple_of((rank ^ j) * cols, cols), cols)] = part[...]
    for n, out in enumerate(outs):
        at = pl.ds(pl.multiple_of(index[1 + n] * size, size), size)
        first = dims(normed[:, at], grads[...], 0, 0).astype(BF)
        second = dims(joined[:, at], mixed[...], 0, 0).astype(BF)
        pieces = out if isinstance(out, list) else [out]
        for n, piece in enumerate(pieces):
            rows = slice(n * piece.shape[0], (n + 1) * piece.shape[0])
            piece[:, :wide] = first[rows]
            piece[:, wide:] = second[rows]
    wbeta[...] = dims(logit[...], normed[...], 1, 0)


def body(
    tokens,
    cotangent,
    lengths,
    pad_mask,
    attn_gain,
    projection_weight,
    w_beta,
    beta_bias,
    conv_weight,
    head_gain,
    mlp_gain,
    w_gate,
    w_up,
    w_down,
):
    width, model = tokens.shape
    heads = w_beta.shape[1]
    depth = head_gain.shape[0]
    ksize = conv_weight.shape[1]
    margin = ksize - 1
    lanes, blocks = lax.axis_size("ta"), lax.axis_size("dev")
    rank, place = lax.axis_index("ta"), lax.axis_index("dev")
    own_heads = heads // lanes
    cols = own_heads * depth
    rows = projection_weight.shape[0]
    group = lanes * width
    ring = Ring()

    positions = place * group + jnp.arange(group, dtype=jnp.int32)
    documents = document_of(lengths, positions)
    valid = jnp.stack(
        [
            (document_of(lengths, positions - margin + offset) == documents).astype(F32)
            for offset in range(ksize)
        ],
        axis=1,
    )
    previous = document_of(lengths, positions[::width] - 1)

    at_rank = rank.astype(jnp.int32).reshape(1)
    at_place = place.astype(jnp.int32).reshape(1)
    by_rank = jnp.concatenate([at_rank, ring.slot_of])

    flags = jnp.zeros((8, model), BF).at[0, 0:width].set(pad_mask.astype(BF))
    edge = jnp.concatenate([tokens[width - PAD :], flags], axis=0)
    route = [(i, i + 1) for i in range(lanes - 1, blocks * lanes - 1, lanes)]
    before = lax.ppermute(edge, BOTH, route)
    flags = flags.at[0, width : width + PAD].set(before[PAD, width - PAD : width])
    packed = gather_parts(jnp.concatenate([tokens, flags, before[0:PAD]], axis=0))
    cot_parts = gather_parts(cotangent)
    group_tokens, normed_group, normed, flags = vmem_call(
        "norm",
        functools.partial(norm_kernel, width),
        [
            shape((group, model), BF),
            shape((group, model), BF),
            shape((group + PAD, model), BF),
            shape((lanes, 8, 2 * width), BF),
        ],
        [at_rank, *packed, attn_gain[None]],
        0,
    )
    cot_group = in_order(cot_parts, at_rank)
    live = flags[:, 0, 0:width].reshape(group).astype(F32)
    live_ext = jnp.concatenate([flags[0, 0, width : width + PAD].astype(F32), live])[:, None]

    own_conv = lax.dynamic_slice_in_dim(conv_weight, rank * cols, cols, 2)
    own_bias = lax.dynamic_slice_in_dim(beta_bias, rank * own_heads, own_heads, 0)
    chunk_docs = documents.reshape(lanes, width)
    continuing = (chunk_docs == previous[:, None]).reshape(group).astype(F32)
    closing = (chunk_docs == chunk_docs[:, width - 1 :]).reshape(group).astype(F32)
    shared = jnp.stack(
        [valid[:, j] for j in range(margin)] + [continuing, closing, live, documents.astype(F32)], axis=0
    )
    shared = jnp.broadcast_to(shared, (own_heads,) + shared.shape)
    columns = jnp.transpose(shared, (0, 2, 1))

    split = jnp.transpose(projection_weight.reshape(rows, 4, lanes, cols), (2, 0, 1, 3)).reshape(lanes, rows, 4 * cols)
    turned = jnp.tile(w_beta.T.reshape(lanes, own_heads, rows), (1, lanes, 1))
    turned = jnp.pad(turned, ((0, 0), (0, 0), (0, 4 * cols - rows)))
    parts = exchange(jnp.concatenate([split, turned], axis=1), rank)
    (own_rows,) = vmem_call(
        "weights",
        functools.partial(weights_kernel, lanes),
        [shape((lanes * rows + heads, 4 * cols), BF)],
        [at_rank, *parts],
        0,
    )
    w = ring.collect(own_rows, [[packed[-1]], [normed, cot_group, live_ext], [columns, own_conv]])
    cot_all = lax.all_gather(gate(cotangent, w[-1]), BOTH, axis=0, tiled=True)
    projected, w_out, beta_logit, wbeta = project(ring.slots, normed, live_ext, w, lanes)
    sig_beta = jax.nn.sigmoid(beta_logit[PAD:, :own_heads].T + own_bias[:, None])
    beta = sig_beta * live[None]
    row = jnp.concatenate([shared, beta[:, None]], axis=1)
    columns = jnp.concatenate([columns, beta[:, :, None]], axis=2)
    mixer = Mixer(projected, own_conv, columns, row, width)
    head_normed = mixer.outputs(
        jnp.concatenate([at_place, ring.slots]), ring.collect(mixer.whole), head_gain[None]
    )
    w_out = gather_parts(w_out, head_normed)
    heads_low = gather_parts(head_normed)
    feed_rows, *own_feed, own_residual = vmem_call(
        "out",
        functools.partial(out_kernel, lanes),
        [shape((group, model), BF)] + [shape((width // 2, model), BF)] * 2 + [shape((width, model))],
        [by_rank, *heads_low, *w_out, group_tokens, mlp_gain[None]],
        2 * group * model * model,
        scratch=[pltpu.VMEM((group, model), F32)],
    )
    half_rows = width // 2
    feed_halves = [lax.all_gather(x, BOTH, axis=0, tiled=True) for x in own_feed]

    weights = [w_gate, w_up, w_down]
    units = w_gate.shape[1]
    core = (rank % 2).astype(jnp.int32).reshape(1)
    *arrays, kept, sent, kept_result, sent_result = feed_own(
        jnp.concatenate([at_place, core]), feed_rows, cot_group, weights, blocks * group, width
    )
    others = lax.rem(place + 1 + jnp.arange(blocks - 1, dtype=jnp.int32), blocks)
    row_parts = [others[: (blocks + 1) // 2], others[(blocks + 1) // 2 :]]

    def hidden_of(part, held, dep):
        return by_group(
            "feed_hidden", hidden_kernel, part, group, [cot_all], [w_down], [units], held, [dep], 1
        )[::-1]

    kept, arrived, (_, grad_hidden) = scatter_sum(
        kept, sent, rank, lambda sent: hidden_of(row_parts[0], [], sent)
    )

    halves_left = [0, 1]

    def by_halves(x):
        return x.reshape(blocks * lanes, 2, half_rows, x.shape[-1])

    def fill_rows(deps):
        half = halves_left.pop(0)
        *found, token = by_group(
            "feed_rows", rows_kernel, others, lanes * half_rows, [feed_halves[half], by_halves(grad_hidden)],
            weights[:2], [units] * 3, [by_halves(x) for x in arrays], deps, 2, half,
        )
        arrays[:] = [x.reshape(blocks * group, units) for x in found]
        return token

    order = [0, 1, 2]
    ffn_grads = [[], [], []]
    done = [0, 0, 0]

    def fill_grads(parts, dep):
        which = order[0]
        lefts = [cot_all] if which == 2 else feed_halves
        hidden, grad_gate, grad_lifted = arrays
        right = (grad_gate, grad_lifted, hidden)[which]
        right = by_halves(right)
        out, token = weight_grad(done[which], parts, lefts, right, ffn_grads[which], [dep], which == 2)
        ffn_grads[which] = [out]
        done[which] += 1
        if done[which] == parts:
            order.pop(0)
        return token

    grad_residual, grad_mlp_gain, *sent = vmem_call(
        "residual",
        functools.partial(residual_kernel, lanes),
        [shape((width, model)), shape((1, model))] + [shape((width, 2 * cols), BF)] * lanes,
        [by_rank, *w_out, kept, arrived, own_residual, cotangent, mlp_gain[None]],
        2 * width * model * model,
        scratch=[pltpu.VMEM((width, model), BF)],
    )
    by_heads = [swap(x, "ta", j) if j else x for j, x in enumerate(sent)]
    token, grad_hidden = hidden_of(row_parts[1], [grad_hidden], sent[0])
    leak, grad_head_gain, mixed_cols = mixer.leak(at_rank, by_heads, [token])
    beside = swap(leak, "dev", 1)
    pair = jnp.stack([leak, beside])
    pairs = [
        lax.ppermute(pair, "dev", [(i, i - 2 * k) for i in range(2 * k, blocks)]) for k in range(1, blocks // 2)
    ]
    token = fill_rows([pair])
    grad_q, grad_k, grad_v, tail, spill, grad_conv, grad_beta = mixer.back([beside, *pairs], [token])
    arrived = lax.ppermute(spill.astype(BF), "dev", [(i, i - 1) for i in range(1, blocks)])
    grad_logit = grad_beta[:, 0] * beta * (1.0 - sig_beta)
    grad_bias = jnp.sum(grad_logit, axis=1)
    grad_logit_low = jnp.pad(grad_logit.astype(BF), ((0, 8 - own_heads), (0, 0)))

    half = (lanes // 2, 2 * width, model)
    grad_projected, kept, sent, grad_attn_gain = vmem_call(
        "normed_back",
        functools.partial(normed_back_kernel, blocks),
        [shape((group, 3 * cols), BF), shape(half, BF), shape(half, BF), shape((1, model))],
        [jnp.concatenate([core, ring.slots]), *w, grad_q, grad_k, grad_v, tail, arrived]
        + [live[group - PAD :, None], grad_logit_low, wbeta, group_tokens, kept_result, sent_result],
        2 * group * model * 3 * cols,
        scratch=[pltpu.VMEM((group, model), BF)],
    )

    *partial_rows, partial_wbeta = vmem_call(
        "weight_rows",
        functools.partial(weight_rows_kernel, lanes),
        [shape((model // blocks, 4 * cols), BF)] * (blocks - 1)
        + [shape((model // blocks // 2, 4 * cols), BF)] * 2
        + [shape((8, model))],
        [jnp.concatenate([at_rank, ring.slots]), *heads_low, normed_group, grad_projected, mixed_cols]
        + [grad_logit_low],
        2 * group * model * 4 * cols,
        scratch=[pltpu.VMEM((group, model), BF)],
    )
    made = []

    def fill(function, *deps):
        made.append(function(*deps))
        return made[-1]

    terms, deps = ring.scatter(
        partial_rows,
        [
            lambda x: fill(fill_rows, [x]),
            lambda x: fill(fill_grads, 1, x),
            lambda x: fill(fill_grads, 1, x),
            lambda x: fill(fill_grads, 1, x),
        ],
    )
    w_parts = vmem_call("sum", sum_kernel, [shape((rows, 4 * cols), BF)] * lanes, [at_rank, *terms], 0, deps)
    moved_parts = [swap(x, "ta", j) if j else x for j, x in enumerate(w_parts)]
    (grad_projection,) = vmem_call(
        "assemble",
        assemble_kernel,
        [shape((rows, 4, model))],
        [at_rank, *moved_parts],
        0,
    )

    kept, arrived, _ = scatter_sum(kept, sent, rank, lambda sent: (made[0],))
    block_out, grad_tokens = vmem_call(
        "finish",
        finish_kernel,
        [shape((width, model), BF), shape((width, model))],
        [kept, arrived, own_residual, grad_residual, tokens, attn_gain[None]],
        0,
        w_parts[:1],
    )

    own = jnp.concatenate([grad_conv.reshape(-1), partial_wbeta[:own_heads].reshape(-1), grad_bias])
    gains = jnp.concatenate([grad_mlp_gain[0], grad_head_gain[0], grad_attn_gain[0]])
    length = own.shape[0]
    apart = length + (-length % 1024)
    flat = jnp.zeros((lanes, apart), F32)
    flat = lax.dynamic_update_slice(flat, jnp.pad(own, (0, apart - length))[None], (rank, 0))
    flat = jnp.concatenate([flat.reshape(-1, 128), jnp.pad(gains, (0, -gains.shape[0] % 1024)).reshape(-1, 128)])
    flat = gate(lax.psum(flat, BOTH), w_parts[0]).reshape(-1)
    gains = flat[lanes * apart :]
    flat = flat[: lanes * apart].reshape(lanes, apart)
    convs = 3 * ksize * cols
    conv_sum = jnp.transpose(flat[:, :convs].reshape(lanes, 3, ksize, cols), (1, 2, 0, 3))
    conv_sum = conv_sum.reshape(3, ksize, lanes * cols)
    wbeta_sum = flat[:, convs : convs + own_heads * model].reshape(heads, model)
    grad_w_beta = lax.dynamic_slice_in_dim(wbeta_sum, (place * lanes + rank) * rows, rows, 1).T
    bias_sum = flat[:, convs + own_heads * model : length].reshape(heads)

    (grad_w_gate,), (grad_w_up,), (grad_w_down,) = ffn_grads
    return (
        block_out,
        grad_tokens,
        gains[model + depth : 2 * model + depth],
        grad_projection,
        grad_w_beta,
        bias_sum,
        conv_sum,
        gains[model : model + depth],
        gains[:model],
        grad_w_gate,
        grad_w_up,
        grad_w_down,
    )


def solution(mesh):
    rows = P(BOTH, None)
    three = P(BOTH, None, None)
    return jax.shard_map(
        body,
        mesh=mesh,
        in_specs=(
            rows,
            rows,
            P(),
            P(BOTH),
            P(),
            three,
            rows,
            P(),
            P(),
            P(),
            P(),
            P(None, "ta"),
            P(None, "ta"),
            P("ta", None),
        ),
        out_specs=(
            rows,
            rows,
            P(),
            three,
            rows,
            P(),
            P(),
            P(),
            P(),
            P(None, "ta"),
            P(None, "ta"),
            P("ta", None),
        ),
        check_vma=False,
    )
```
